32 devices in a mesh: section: 2 (over core), batch: 16 (over z, y, x).
Axes of the slice: x: 2, y: 2, z: 4, core: 2. Of those that a mesh axis runs over, the one named last changes fastest.
Arguments:
- params: float32 [2, 3673088], P('section', 'batch'), may hold values from -1.5 to 1.5, as said below
- first_moment: float32 [2, 3673088], P('section', 'batch'), may hold values from -5.340576e-05 to 5.340576e-05
- second_moment: float32 [2, 3673088], P('section', 'batch'), may hold values from 1.9057533e-11 to 1.9057535e-10
- inputs: bfloat16 [2, 24576, 512], P('section', 'batch'), may hold values from -6 to 6
- segments: int32 [24576], P('batch'), may hold values from 0 to 191, never falling along the last dimension, each value on 1 to 250 neighbouring positions
- live_mask: int32 [2, 24576], P(None, 'batch'), may hold values 0 or 1
- out_grad: bfloat16 [24576, 512], P('batch'), may hold values from -6 to 6
Outputs:
- param_step: float32 [2, 3673088], P('section', 'batch')
- new_first: float32 [2, 3673088], P('section', 'batch')
- new_second: float32 [2, 3673088], P('section', 'batch')
- param_grad: float32 [2, 3673088], P('section', 'batch')
- layer_out: bfloat16 [2, 24576, 512], P('section', 'batch')
- input_grad: bfloat16 [2, 24576, 512], P('section', 'batch')
- grad_norm: float32 [], replicated
The draws below stay inside these ranges and needn't reach their ends.
Inputs may be any that keep to these rules, and one draw needn't show every extreme that they name: `params`: weights are scaled by their fan-in, gains lie near 1 and shifts near 0.
All inputs are finite; a program needn't handle non-finite values. No bound on the sum of `live_mask` on one device may be relied on, other than what follows from the above.
Results may differ from the reference program's by a relative error of at most 0.02.
Values may be sent and summed in bfloat16 or wider, within the bound.
No kernel may reach another device: no remote copies, remote signals or barrier semaphores. Data moves between devices by JAX's collectives and lax.ppermute only.
A program may use at most 256 MiB of HBM per device.

```python
import math
import jax
import jax.numpy as jnp
import numpy as np
from jax import lax

D = 512
FF = 2048
HEADS = 8
HD = 64
ROW = 512
TOKENS = 24576
SEG_MEAN = 128
SEG_MOST = 250
STEP = 1000
WARMUP = 4000
P_SIZE = 3673088


def draw_params(key, part):
    key = jax.random.fold_in(key, 7)
    key_list = jax.random.split(key, 7)

    def normal_block(sub_key, shape, factor):
        return jax.random.truncated_normal(sub_key, -4.0, 4.0, shape, jnp.float32) * factor
    w_qkv = normal_block(key_list[0], (2, D, 3 * D), D ** (-0.5))
    w_out = normal_block(key_list[1], (2, D, D), 3.0 * D ** (-0.5))
    cross_scale = jnp.where((jnp.arange(2)[:, None, None] == 1) & (jnp.arange(2 * D)[None, None, :] >= D), 3.0, 1.0)
    w_cross = normal_block(key_list[2], (2, D, 2 * D), D ** (-0.5)) * cross_scale
    w_up = normal_block(key_list[3], (2, D, FF), D ** (-0.5))
    w_down = normal_block(key_list[4], (2, FF, D), FF ** (-0.5))
    gains = 1.0 + normal_block(key_list[5], (2, 3, 1, D), 0.1)
    shifts = normal_block(key_list[6], (2, 3, 1, D), 0.1)
    vectors = jnp.concatenate([gains, shifts], axis=2).reshape(2, 6 * D)
    return jnp.concatenate([w_qkv.reshape(2, -1), w_out.reshape(2, -1), w_cross.reshape(2, -1), w_up.reshape(2, -1), w_down.reshape(2, -1), vectors], axis=1)


def set_ends(entries, own_key, smallest, high):
    extent = entries.shape
    place = [jax.random.randint(jax.random.fold_in(own_key, axis), (), 0, extent[axis]) for axis in range(len(extent))]
    entries = entries.at[tuple(place)].set(smallest)
    longest = extent.index(max(extent))
    place[longest] = (place[longest] + 1) % extent[longest]
    return entries.at[tuple(place)].set(high)


def level_of(own_key, extent, cuts, smallest, top_value):
    gain, own = 1.0, jax.random.fold_in(own_key, 6)
    for position, blocks in cuts:
        draws = jnp.exp(jax.random.uniform(jax.random.fold_in(own, position), (blocks,), jnp.float32, smallest / len(cuts), top_value / len(cuts)))
        gain = gain * jnp.repeat(draws, extent[position] // blocks).reshape([-1 if axis == position else 1 for axis in range(len(extent))])
    return gain


def profile(amount, total, reach, skew):
    portions = [(1 << 20) // math.isqrt(standing ** skew) + 1 for standing in range(2, amount + 1)]
    surplus, counts = total - reach - (amount - 1), [1] * (amount - 1)
    while surplus > 0:
        candidates = [i for i in range(amount - 1) if counts[i] < reach]
        whole, left = sum([portions[i] for i in candidates]), surplus
        for i in candidates:
            addition = min(reach - counts[i], max(1, left * portions[i] // whole), surplus)
            counts[i] = counts[i] + addition
            surplus = surplus - addition
    return np.array([reach] + counts)


def ragged_sizes(key, number_of, total, most, slope):
    if number_of == 2:
        one = jax.random.randint(key, (), max(1, total - most), min(most, total - 1) + 1)
        return jnp.stack([one, total - one])
    tallies = jnp.asarray(profile(number_of, total, most, slope), jnp.int32)
    couples = (number_of - 1) // 2
    donor, taker = tallies[1:1 + 2 * couples:2], tallies[2:2 + 2 * couples:2]
    slack = jnp.minimum(donor - 1, most - taker)
    passed = jax.random.randint(jax.random.fold_in(key, 1), (couples,), 0, 1 << 20) % (slack + 1)
    tallies = tallies.at[1:1 + 2 * couples:2].set(donor - passed).at[2:2 + 2 * couples:2].set(taker + passed)
    return tallies[jax.random.permutation(jax.random.fold_in(key, 2), number_of)]


def centred(stream_key, extent, deviation, reach, cuts=(), kind=jnp.bfloat16):
    factor_of = level_of(stream_key, extent, cuts, -0.22, 0.18) if cuts else 1.0
    entries = jax.random.normal(stream_key, extent, jnp.float32) * deviation * factor_of
    return jnp.minimum(jnp.maximum(entries, -reach), reach).astype(kind)


def setup_inputs(seed: int = 0) -> dict:
    key_of = jax.random.split(jax.random.key(seed), 8)
    params = draw_params(jax.random.fold_in(key_of[7], 71), 0)
    first_moment = centred(key_of[1], (2, P_SIZE), (0.01 * (2 * P_SIZE) ** -0.5), 5.340576171875e-05, ((0, 2), (1, 16)), jnp.float32)
    second_moment = jnp.clip(jnp.exp(math.log(1.9057534716981905e-10) - 2.3025852 * jax.random.uniform(key_of[2], (2, P_SIZE), jnp.float32) ** level_of(key_of[2], (2, P_SIZE), ((0, 2), (1, 16)), -0.2, 0.2)), 1.9057533329203125e-11, 1.9057534716981905e-10)
    inputs = centred(key_of[3], (2, TOKENS, D), 1.0, 6.0, ((0, 2), (1, 16)))
    segments = jnp.searchsorted(jnp.cumsum(ragged_sizes(key_of[4], TOKENS // SEG_MEAN, TOKENS, SEG_MOST, 2)), jnp.arange(TOKENS), side="right").astype(jnp.int32)
    live_mask = set_ends((jax.random.randint(key_of[5], (2, TOKENS), 0, 8) < 7).astype(jnp.int32), jax.random.fold_in(key_of[5], 1), 0, 1)
    out_grad = centred(key_of[6], (TOKENS, D), 1.0, 6.0, ((0, 16),))
    return dict(params=params, first_moment=first_moment, second_moment=second_moment, inputs=inputs, segments=segments, live_mask=live_mask, out_grad=out_grad)


NEG = -1e+30
LN_EPS = 1e-05
BETA_ONE = 0.9
BETA_TWO = 0.98
ADAM_EPS = 1e-09
MAXNORM = 0.1

@jax.custom_vjp
def low(v):
    return lax.optimization_barrier(v.astype(jnp.bfloat16)).astype(jnp.float32)

@jax.custom_vjp
def low_back(v):
    return v

def low_keep(v):
    return (low(v), None)

def low_pass(kept, grad):
    return (grad,)

def back_keep(v):
    return (v, None)

def back_low(kept, grad):
    return (low(grad),)
low.defvjp(low_keep, low_pass)
low_back.defvjp(back_keep, back_low)

def both_ways(tensor):
    return low(low_back(tensor))

def matmul(lhs_mat, rhs_mat):
    return jnp.dot(lhs_mat, rhs_mat, precision=lax.Precision.HIGHEST)

def layer_norm(residual, gain_vec, shift_vec):
    center = residual - lax.optimization_barrier(jnp.mean(residual, axis=-1, keepdims=True))
    spread = lax.optimization_barrier(jnp.mean(center * center, axis=-1, keepdims=True))
    return center * lax.rsqrt(spread + LN_EPS) * gain_vec + shift_vec

def unpack(flat_vec):
    pieces = []
    offset = 0
    for rows_n, cols_n in ((D, 3 * D), (D, D), (D, 2 * D), (D, FF), (FF, D), (6, D)):
        pieces.append(flat_vec[offset:offset + rows_n * cols_n].reshape(rows_n, cols_n))
        offset = offset + rows_n * cols_n
    return pieces

def build_masks(seg_rows, live_src, live_tgt):
    places = jnp.arange(seg_rows.shape[0])
    same_seg = seg_rows[:, None] == seg_rows[None, :]
    diagonal = places[:, None] == places[None, :]
    causal = places[None, :] <= places[:, None]
    enc_mask = same_seg & ((live_src[None, :] == 1) | diagonal)
    dec_mask = same_seg & causal & ((live_tgt[None, :] == 1) | diagonal)
    return (enc_mask, dec_mask)

def attend(queries, key_rows, values, allowed):
    rows_n = queries.shape[0]
    head_q = queries.reshape(rows_n, HEADS, HD)
    head_k = key_rows.reshape(rows_n, HEADS, HD)
    head_v = values.reshape(rows_n, HEADS, HD)
    scores = jnp.einsum('qhd,khd->hqk', head_q, head_k, precision=lax.Precision.HIGHEST) * HD ** (-0.5)
    scores = jnp.where(allowed[None], low_back(scores), NEG)
    attn_probs = jax.nn.softmax(scores, axis=-1)
    context = jnp.einsum('hqk,khd->qhd', low(attn_probs), head_v, precision=lax.Precision.HIGHEST)
    return both_ways(context.reshape(rows_n, D))

def feed_forward(w_up, w_down, hidden):
    pre_act = low_back(matmul(low(hidden), w_up))
    return hidden + low_back(matmul(low(jax.nn.gelu(pre_act, approximate=False)), w_down))

def self_block(w_qkv, w_out, block_in, allowed):
    projected = both_ways(matmul(block_in, w_qkv))
    context = attend(projected[:, :D], projected[:, D:2 * D], projected[:, 2 * D:], allowed)
    return block_in + low_back(matmul(context, w_out))

def encode(pieces, source, enc_mask):
    w_qkv, w_out, w_cross, w_up, w_down, vectors = pieces
    hidden_one = layer_norm(self_block(w_qkv, w_out, source, enc_mask), vectors[0], vectors[1])
    memory = layer_norm(feed_forward(w_up, w_down, hidden_one), vectors[2], vectors[3])
    key_value = both_ways(matmul(low(memory), w_cross))
    return (memory, key_value)

def decode(pieces, target, key_value, enc_mask, dec_mask):
    w_qkv, w_out, w_cross, w_up, w_down, vectors = pieces
    hidden_one = layer_norm(self_block(w_qkv, w_out, target, dec_mask), vectors[0], vectors[1])
    cross_query = both_ways(matmul(low(hidden_one), w_cross[:, :D]))
    cross_context = attend(cross_query, key_value[:, :D], key_value[:, D:], enc_mask)
    residual = hidden_one + low_back(matmul(cross_context, w_cross[:, D:]))
    hidden_two = layer_norm(residual, vectors[2], vectors[3])
    return layer_norm(feed_forward(w_up, w_down, hidden_two), vectors[4], vectors[5])

def reference(params, first_moment, second_moment, inputs, segments, live_mask, out_grad):
    rows_n = TOKENS // ROW
    sources = inputs[0].astype(jnp.float32).reshape(rows_n, ROW, D)
    targets = inputs[1].astype(jnp.float32).reshape(rows_n, ROW, D)
    seg_rows = segments.reshape(rows_n, ROW)
    live_src = live_mask[0].reshape(rows_n, ROW)
    live_tgt = live_mask[1].reshape(rows_n, ROW)

    def forward(flat_enc, flat_dec, source_rows, target_rows):

        def one_row(row_args):
            source, target, seg_one, src_one, tgt_one = row_args
            enc_mask, dec_mask = build_masks(seg_one, src_one, tgt_one)
            memory, key_value = encode(unpack(low(flat_enc)), source, enc_mask)
            result = decode(unpack(low(flat_dec)), target, key_value, enc_mask, dec_mask)
            return (memory, result)
        return lax.map(jax.checkpoint(one_row), (source_rows, target_rows, seg_rows, live_src, live_tgt))
    (memory, result), pull_back = jax.vjp(forward, params[0], params[1], sources, targets)
    grad_enc, grad_dec, grad_src, grad_tgt = pull_back((jnp.zeros_like(memory), out_grad.astype(jnp.float32).reshape(rows_n, ROW, D)))
    gradients = jnp.stack([grad_enc, grad_dec])
    grad_norm = jnp.sqrt(jnp.sum(gradients * gradients))
    clip_factor = MAXNORM / jnp.maximum(grad_norm, MAXNORM)
    scaled = gradients * clip_factor
    new_first = BETA_ONE * first_moment + (1.0 - BETA_ONE) * scaled
    new_second = BETA_TWO * second_moment + (1.0 - BETA_TWO) * scaled * scaled
    learn_rate = D ** (-0.5) * min(STEP ** (-0.5), STEP * WARMUP ** (-1.5))
    first_hat = new_first / (1.0 - BETA_ONE ** STEP)
    second_hat = new_second / (1.0 - BETA_TWO ** STEP)
    param_step = learn_rate * first_hat / (jnp.sqrt(second_hat) + ADAM_EPS)
    layer_out = jnp.stack([memory, result]).reshape(2, TOKENS, D).astype(jnp.bfloat16)
    input_grad = jnp.stack([grad_src, grad_tgt]).reshape(2, TOKENS, D).astype(jnp.bfloat16)
    return (param_step, new_first, new_second, gradients, layer_out, input_grad, grad_norm)
```

```python
import functools

import jax
import jax.numpy as jnp
from jax import lax
from jax.experimental import pallas as pl
from jax.experimental.pallas import tpu as pltpu
from jax.sharding import PartitionSpec as P

D = 512
FF = 2048
HEADS = 8
HD = 64
ROW = 512
STEP = 1000
WARMUP = 4000

BIG = 1e30
LN_EPS = 1e-05
BETA_ONE = 0.9
BETA_TWO = 0.98
ADAM_EPS = 1e-09
MAXNORM = 0.1

F32 = jnp.float32
BF = jnp.bfloat16
TILE = 16 * 128
CHUNK = 512
SEG_BITS = 12
POS_BITS = 9

MATS = {}
_at = 0
for _name, _rows, _cols in (("qkv", D, 3 * D), ("out", D, D), ("cross", D, 2 * D), ("up", D, FF), ("down", FF, D)):
    _width = _cols // 128
    MATS[_name] = (_rows, _cols, _at, {12: 16, 4: 64, 8: 32, 16: 16}[_width])
    _at += _rows * _width
VEC_AT = _at
FLAT_ROWS = _at + 24


def dot_nn(lhs, rhs):
    return jnp.dot(lhs, rhs, preferred_element_type=F32)


def dot_nt(lhs, rhs):
    return lax.dot_general(lhs, rhs, (((1,), (1,)), ((), ())), preferred_element_type=F32)


def dot_tn(lhs, rhs):
    return lax.dot_general(lhs, rhs, (((0,), (0,)), ((), ())), preferred_element_type=F32)


def params_of(mib):
    return pltpu.CompilerParams(vmem_limit_bytes=mib * 2**20)


def row_spec(rows, cols):
    return pl.BlockSpec((rows, cols), lambda i: (i, 0))


def whole_spec(shape):
    return pl.BlockSpec(shape, lambda i: (0,) * len(shape), pipeline_mode=pl.Buffered(1))


def shape_of(shape, dtype):
    return jax.ShapeDtypeStruct(shape, dtype)


def ln_parts(resid):
    center = resid - jnp.mean(resid, axis=-1, keepdims=True)
    rstd = lax.rsqrt(jnp.mean(center * center, axis=-1, keepdims=True) + LN_EPS)
    return center * rstd, rstd


def ln_back(grad, hat, rstd, gain):
    scaled = grad * gain
    first = jnp.mean(scaled, axis=-1, keepdims=True)
    second = jnp.mean(scaled * hat, axis=-1, keepdims=True)
    grad_resid = rstd * (scaled - first - hat * second)
    return grad_resid, jnp.sum(grad * hat, axis=0, keepdims=True), jnp.sum(grad, axis=0, keepdims=True)


def gelu_both(pre):
    size = jnp.abs(pre)
    near = 1.0 / (1.0 + (0.3275911 * 0.7071067811865476) * size)
    bell = jnp.exp(-0.5 * pre * pre)
    poly = near * (0.127414796 + near * (-0.142248368 + near * (0.7107068705 + near * (-0.7265760135 + near * 0.5307027145))))
    tail = poly * bell
    phi = jnp.where(pre >= 0.0, 1.0 - tail, tail)
    return pre * phi, phi + pre * bell * 0.3989422804014327


def low_lanes(rows):
    return lax.broadcasted_iota(jnp.int32, (rows, 128), 1) < HD


def triangle(keys_first):
    row = lax.broadcasted_iota(jnp.int32, (256, 256), 0)
    col = lax.broadcasted_iota(jnp.int32, (256, 256), 1)
    keep = (row <= col) if keys_first else (col <= row)
    return jnp.where(keep, 0.0, -BIG).astype(F32)


def attend_fwd(causal, q_ref, q_at, k_ref, k_at, v_ref, v_at, fq, fk, ctx_ref, lse_ref):
    low = low_lanes(ROW)
    lane = lax.broadcasted_iota(jnp.int32, (ROW, 128), 1)
    one = jnp.asarray(1.0, BF)
    tri = triangle(False) if causal else None
    lse_all = jnp.zeros((ROW, 128), F32)
    for pair in range(HEADS // 2):
        q_pair = q_ref[:, q_at + 128 * pair : q_at + 128 * pair + 128] * jnp.asarray(HD**-0.5, BF)
        k_pair = k_ref[:, k_at + 128 * pair : k_at + 128 * pair + 128]
        v_pair = v_ref[:, v_at + 128 * pair : v_at + 128 * pair + 128]
        halves = []
        for e in range(2):
            sel = low if e == 0 else ~low
            qa = jnp.where(sel, q_pair, fq)
            ka = jnp.where(sel, k_pair, fk)
            va = jnp.where(sel, v_pair, one)
            outs, tops = [], []
            for half in range(2):
                keys = 256 * (half + 1) if causal else ROW
                s = dot_nt(qa[256 * half : 256 * half + 256], ka[:keys])
                if causal:
                    s = s + tri if half == 0 else jnp.concatenate([s[:, :256], s[:, 256:] + tri], axis=1)
                top = jnp.max(s, axis=1, keepdims=True)
                p = jnp.exp(s - top)
                outs.append(dot_nn(p.astype(BF), va[:keys]))
                tops.append(top)
            o = jnp.concatenate(outs, axis=0)
            total = pltpu.roll(o, 64, 1)
            halves.append(o / total)
            lse = jnp.concatenate(tops, axis=0) + jnp.log(jnp.where(sel, total, o))
            lse_all = jnp.where(lane == 2 * pair + e, lse, lse_all)
        ctx_ref[:, 128 * pair : 128 * pair + 128] = jnp.where(low, halves[0], halves[1]).astype(BF)
    lse_ref[...] = lse_all.T[0:HEADS, :]


def attend_bwd(causal, q_ref, q_at, k_ref, k_at, v_ref, v_at, fq, fk, lse_ref, do_ref, outs, dqt_ref):
    low = low_lanes(ROW)
    zero = jnp.zeros((ROW, 128), BF)
    scale = jnp.asarray(HD**-0.5, BF)
    tri = triangle(True) if causal else None
    k_t = k_ref[:, k_at : k_at + D].T
    for pair in range(HEADS // 2):
        q_pair = q_ref[:, q_at + 128 * pair : q_at + 128 * pair + 128] * scale
        k_pair = k_ref[:, k_at + 128 * pair : k_at + 128 * pair + 128]
        v_pair = v_ref[:, v_at + 128 * pair : v_at + 128 * pair + 128]
        do_pair = do_ref[:, 128 * pair : 128 * pair + 128]
        dks, dvs = [], []
        for e in range(2):
            head = 2 * pair + e
            sel = low if e == 0 else ~low
            qa = jnp.where(sel, q_pair, fq)
            ka = jnp.where(sel, k_pair, fk)
            va = jnp.where(sel, v_pair, zero)
            probs, prods = [], []
            for half in range(2):
                first = 256 * half if causal else 0
                keys = slice(256 * half, 256 * half + 256)
                s = dot_nt(ka[keys], qa[first:])
                if causal:
                    s = s + tri if half == 1 else jnp.concatenate([s[:, :256] + tri, s[:, 256:]], axis=1)
                p = jnp.exp(s - lse_ref[head : head + 1, first:])
                probs.append(p)
                prods.append(p * dot_nt(va[keys], do_pair[first:]))
            if causal:
                top = jnp.sum(prods[0], axis=0, keepdims=True)
                rest = top[:, 256:] + jnp.sum(prods[1], axis=0, keepdims=True)
                deltas = [jnp.concatenate([top[:, :256], rest], axis=1), rest]
            else:
                delta = jnp.sum(prods[0], axis=0, keepdims=True) + jnp.sum(prods[1], axis=0, keepdims=True)
                deltas = [delta, delta]
            ds = [(prods[i] - probs[i] * deltas[i]).astype(BF) for i in range(2)]
            firsts = (0, 256) if causal else (0, 0)
            dvs.append(jnp.concatenate([dot_nn(probs[i].astype(BF), do_pair[firsts[i] :]) for i in range(2)], axis=0))
            dks.append(jnp.concatenate([dot_nn(ds[i], q_pair[firsts[i] :]) for i in range(2)], axis=0))
            k_head = k_t[HD * head : HD * head + HD]
            if causal:
                dqt_ref[HD * head : HD * head + HD, :256] = dot_nn(k_head[:, :256], ds[0][:, :256])
                dqt_ref[HD * head : HD * head + HD, 256:] = dot_nn(k_head, jnp.concatenate([ds[0][:, 256:], ds[1]], axis=0))
            else:
                dqt_ref[HD * head : HD * head + HD, :] = dot_nn(k_head, jnp.concatenate(ds, axis=0))
        for (ref, at), parts in ((outs[1], dks), (outs[2], dvs)):
            ref[:, at + 128 * pair : at + 128 * pair + 128] = jnp.where(low, parts[0], parts[1]).astype(BF)
    ref, at = outs[0]
    ref[:, at : at + D] = (dqt_ref[...] * HD**-0.5).T.astype(BF)


def group_perm(name, to_flat):
    _, cols, _, group = MATS[name]
    width = cols // 128
    size = group * width
    row = lax.broadcasted_iota(jnp.int32, (size, size), 0)
    col = lax.broadcasted_iota(jnp.int32, (size, size), 1)
    blocked, flat = (col, row) if to_flat else (row, col)
    source = width * (blocked & (group - 1)) + lax.shift_right_logical(blocked, group.bit_length() - 1)
    return jnp.where(source == flat, 1.0, 0.0).astype(BF)


def to_matrix(name, flat_ref, at, mat_ref):
    rows, cols, _, group = MATS[name]
    width = cols // 128
    size = group * width
    perm = group_perm(name, False)
    for g in range(rows // group):
        got = dot_nn(perm, flat_ref[at + g * size : at + (g + 1) * size, :]).astype(BF)
        for c in range(width):
            mat_ref[g * group : (g + 1) * group, 128 * c : 128 * c + 128] = got[c * group : (c + 1) * group]


def to_flat(name, mat_ref, flat_ref, at):
    rows, cols, _, group = MATS[name]
    width = cols // 128
    size = group * width
    perm = group_perm(name, True)
    for g in range(rows // group):
        blocked = jnp.concatenate(
            [mat_ref[g * group : (g + 1) * group, 128 * c : 128 * c + 128].astype(BF) for c in range(width)], axis=0
        )
        flat_ref[at + g * size : at + (g + 1) * size, :] = dot_nn(perm, blocked).astype(BF)


def ffn_fwd(hidden_b, w_up, w_down, act_ref, slope_ref):
    total = None
    for c in range(FF // CHUNK):
        cols = slice(c * CHUNK, (c + 1) * CHUNK)
        act, slope = gelu_both(dot_nn(hidden_b, w_up[:, cols]))
        act_b = act.astype(BF)
        act_ref[:, cols] = act_b
        slope_ref[:, cols] = slope.astype(slope_ref.dtype)
        part = dot_nn(act_b, w_down[cols, :])
        total = part if total is None else total + part
    return total


def ffn_bwd(hidden_b, branch_b, w_up, w_down, act_ref, slope_ref, g_up, g_down):
    total = None
    hidden_t = hidden_b.T
    for c in range(FF // CHUNK):
        cols = slice(c * CHUNK, (c + 1) * CHUNK)
        grad_act = dot_nt(branch_b, w_down[cols, :])
        grad_pre = (grad_act * slope_ref[:, cols].astype(F32)).astype(BF)
        g_down[cols, :] += dot_tn(act_ref[:, cols], branch_b)
        g_up[:, cols] += dot_nn(hidden_t, grad_pre)
        part = dot_nt(grad_pre, w_up[:, cols])
        total = part if total is None else total + part
    return total


def weights_kernel(n, share, flat_in, *refs):
    outs, flat = refs[:6], refs[6]
    for b in range(n):
        tile = share * b // TILE
        last = -(-share * (b + 1) // TILE)
        start, count = 16 * tile, 16 * (last - tile)
        if (share * b) % TILE:
            flat[start : start + 16, :] += flat_in[b, 0:16, :]
        else:
            flat[start : start + 16, :] = flat_in[b, 0:16, :]
        flat[start + 16 : start + count, :] = flat_in[b, 16:count, :]
    for name, ref in zip(MATS, outs):
        to_matrix(name, flat, MATS[name][2], ref)
    outs[5][...] = flat[VEC_AT : VEC_AT + 32, :]


def self_fwd_kernel(causal, x_ref, wqkv, wout, fq, fk, qkv_ref, ctx_ref, lse_ref, r1_ref):
    x = x_ref[...]
    qkv_ref[...] = dot_nn(x, wqkv[...]).astype(BF)
    attend_fwd(causal, qkv_ref, 0, qkv_ref, D, qkv_ref, 2 * D, fq[...], fk[...], ctx_ref, lse_ref)
    r1_ref[...] = x.astype(F32) + dot_nn(ctx_ref[...], wout[...])


def enc_ffn_kernel(r1_ref, vec, w_up, w_down, w_cross, mem_ref, kv_ref, act_ref, slope_ref, r2_ref):
    hat, _ = ln_parts(r1_ref[...])
    y1 = hat * vec[0:1, :] + vec[1:2, :]
    r2 = y1 + ffn_fwd(y1.astype(BF), w_up, w_down, act_ref, slope_ref)
    r2_ref[...] = r2
    hat, _ = ln_parts(r2)
    mem = (hat * vec[2:3, :] + vec[3:4, :]).astype(BF)
    mem_ref[...] = mem
    kv_ref[...] = dot_nn(mem, w_cross[...]).astype(BF)


def dec_kernel(
    r1_ref, kv_ref, go_ref, vec, w_cross, w_up, w_down, fq, fk,
    out_ref, gkv_ref, dy1_ref, fl_cross, fl_up, fl_down, gvec,
    cq_s, ctx_s, lse_s, dctx_s, dcq_s, dqt_s, act_s, slope_s, g_cross, g_up, g_down,
):
    step = pl.program_id(0)

    @pl.when(step == 0)
    def _():
        g_cross[...] = jnp.zeros_like(g_cross)
        g_up[...] = jnp.zeros_like(g_up)
        g_down[...] = jnp.zeros_like(g_down)
        gvec[...] = jnp.zeros_like(gvec)

    hat1, _ = ln_parts(r1_ref[...])
    y1 = hat1 * vec[0:1, :] + vec[1:2, :]
    y1_b = y1.astype(BF)
    cq_s[...] = dot_nn(y1_b, w_cross[:, :D]).astype(BF)
    attend_fwd(False, cq_s, 0, kv_ref, 0, kv_ref, D, fq[...], fk[...], ctx_s, lse_s)
    r2 = y1 + dot_nn(ctx_s[...], w_cross[:, D:])
    hat2, rstd2 = ln_parts(r2)
    y2 = hat2 * vec[2:3, :] + vec[3:4, :]
    y2_b = y2.astype(BF)
    r3 = y2 + ffn_fwd(y2_b, w_up, w_down, act_s, slope_s)
    hat3, rstd3 = ln_parts(r3)
    out_ref[...] = (hat3 * vec[4:5, :] + vec[5:6, :]).astype(BF)

    dr3, gain3, shift3 = ln_back(go_ref[...].astype(F32), hat3, rstd3, vec[4:5, :])
    dy2 = dr3 + ffn_bwd(y2_b, dr3.astype(BF), w_up, w_down, act_s, slope_s, g_up, g_down)
    dr2, gain2, shift2 = ln_back(dy2, hat2, rstd2, vec[2:3, :])
    dr2_b = dr2.astype(BF)
    g_cross[:, D:] += dot_tn(ctx_s[...], dr2_b)
    dctx_s[...] = dot_nt(dr2_b, w_cross[:, D:]).astype(BF)
    attend_bwd(
        False, cq_s, 0, kv_ref, 0, kv_ref, D, fq[...], fk[...], lse_s, dctx_s,
        ((dcq_s, 0), (gkv_ref, 0), (gkv_ref, D)), dqt_s,
    )
    dcq = dcq_s[...]
    g_cross[:, :D] += dot_tn(y1_b, dcq)
    dy1_ref[...] = dr2 + dot_nt(dcq, w_cross[:, :D])
    gvec[2:3, :] += gain2
    gvec[3:4, :] += shift2
    gvec[4:5, :] += gain3
    gvec[5:6, :] += shift3

    @pl.when(step == pl.num_programs(0) - 1)
    def _():
        to_flat("cross", g_cross, fl_cross, 0)
        to_flat("up", g_up, fl_up, 0)
        to_flat("down", g_down, fl_down, 0)


def enc_back_kernel(
    gkv_ref, mem_ref, r1_ref, r2_ref, act_ref, slope_ref, vec, w_cross, w_up, w_down,
    dy1_ref, fl_cross, fl_up, fl_down, gvec, g_cross, g_up, g_down,
):
    step = pl.program_id(0)

    @pl.when(step == 0)
    def _():
        g_cross[...] = jnp.zeros_like(g_cross)
        g_up[...] = jnp.zeros_like(g_up)
        g_down[...] = jnp.zeros_like(g_down)
        gvec[...] = jnp.zeros_like(gvec)

    gkv = gkv_ref[...]
    g_cross[...] += dot_tn(mem_ref[...], gkv)
    dmem = dot_nt(gkv, w_cross[...])
    hat2, rstd2 = ln_parts(r2_ref[...])
    dr2, gain2, shift2 = ln_back(dmem, hat2, rstd2, vec[2:3, :])
    hat1, _ = ln_parts(r1_ref[...])
    y1_b = (hat1 * vec[0:1, :] + vec[1:2, :]).astype(BF)
    dy1_ref[...] = dr2 + ffn_bwd(y1_b, dr2.astype(BF), w_up, w_down, act_ref, slope_ref, g_up, g_down)
    gvec[2:3, :] += gain2
    gvec[3:4, :] += shift2

    @pl.when(step == pl.num_programs(0) - 1)
    def _():
        to_flat("cross", g_cross, fl_cross, 0)
        to_flat("up", g_up, fl_up, 0)
        to_flat("down", g_down, fl_down, 0)


def self_back_kernel(
    causal, x_ref, r1_ref, dy1_ref, qkv_ref, ctx_ref, lse_ref, vec, wqkv, wout, fq, fk,
    dx_ref, fl_qkv, fl_out, gvec, dctx_s, dqkv_s, dqt_s, g_qkv, g_out,
):
    step = pl.program_id(0)

    @pl.when(step == 0)
    def _():
        g_qkv[...] = jnp.zeros_like(g_qkv)
        g_out[...] = jnp.zeros_like(g_out)
        gvec[...] = jnp.zeros_like(gvec)

    hat1, rstd1 = ln_parts(r1_ref[...])
    dr1, gain1, shift1 = ln_back(dy1_ref[...], hat1, rstd1, vec[0:1, :])
    dr1_b = dr1.astype(BF)
    g_out[...] += dot_tn(ctx_ref[...], dr1_b)
    dctx_s[...] = dot_nt(dr1_b, wout[...]).astype(BF)
    attend_bwd(
        causal, qkv_ref, 0, qkv_ref, D, qkv_ref, 2 * D, fq[...], fk[...], lse_ref, dctx_s,
        ((dqkv_s, 0), (dqkv_s, D), (dqkv_s, 2 * D)), dqt_s,
    )
    dqkv = dqkv_s[...]
    g_qkv[...] += dot_tn(x_ref[...], dqkv)
    dx_ref[...] = (dr1 + dot_nt(dqkv, wqkv[...])).astype(BF)
    gvec[0:1, :] += gain1
    gvec[1:2, :] += shift1

    @pl.when(step == pl.num_programs(0) - 1)
    def _():
        to_flat("qkv", g_qkv, fl_qkv, 0)
        to_flat("out", g_out, fl_out, 0)


def kernel_call(body, **options):
    call = pl.pallas_call(body, **options)
    return lambda *operands: tuple(call(*operands))


def split_weights(pieces, n, share):
    shapes = [(rows, cols) for rows, cols, _, _ in MATS.values()] + [(32, 128)]
    rows = 16 * (-(-share * n // TILE) + 2)
    return kernel_call(
        functools.partial(weights_kernel, n, share),
        in_specs=[pl.BlockSpec(memory_space=pltpu.VMEM)],
        out_specs=[pl.BlockSpec(memory_space=pltpu.VMEM)] * 6,
        out_shape=[shape_of(s, BF) for s in shapes],
        scratch_shapes=[pltpu.VMEM((rows, 128), BF)],
        compiler_params=params_of(48),
    )(pieces)


def self_fwd(causal, x, w, fq, fk):
    t = x.shape[0]
    return kernel_call(
        functools.partial(self_fwd_kernel, causal),
        grid=(t // ROW,),
        in_specs=[
            row_spec(ROW, D), whole_spec((D, 3 * D)), whole_spec((D, D)), row_spec(ROW, 128), row_spec(ROW, 128),
        ],
        out_specs=[row_spec(ROW, 3 * D), row_spec(ROW, D), row_spec(HEADS, ROW), row_spec(ROW, D)],
        out_shape=[
            shape_of((t, 3 * D), BF), shape_of((t, D), BF), shape_of((t // ROW * HEADS, ROW), F32), shape_of((t, D), F32),
        ],
        compiler_params=params_of(48),
    )(x, w["qkv"], w["out"], fq, fk)


def enc_ffn(r1, w, vec):
    t = r1.shape[0]
    return kernel_call(
        enc_ffn_kernel,
        grid=(t // ROW,),
        in_specs=[
            row_spec(ROW, D), whole_spec((6, D)), whole_spec((D, FF)), whole_spec((FF, D)), whole_spec((D, 2 * D)),
        ],
        out_specs=[row_spec(ROW, D), row_spec(ROW, 2 * D), row_spec(ROW, FF), row_spec(ROW, FF), row_spec(ROW, D)],
        out_shape=[
            shape_of((t, D), BF), shape_of((t, 2 * D), BF), shape_of((t, FF), BF), shape_of((t, FF), BF),
            shape_of((t, D), F32),
        ],
        compiler_params=params_of(48),
    )(r1, vec, w["up"], w["down"], w["cross"])


FLAT_FFN = [shape_of((4096, 128), BF), shape_of((8192, 128), BF), shape_of((8192, 128), BF)]


def dec_call(r1, kv, go, w, vec, fq, fk):
    t = r1.shape[0]
    vm = pltpu.VMEM
    return kernel_call(
        dec_kernel,
        grid=(t // ROW,),
        in_specs=[
            row_spec(ROW, D), row_spec(ROW, 2 * D), row_spec(ROW, D), whole_spec((6, D)), whole_spec((D, 2 * D)),
            whole_spec((D, FF)), whole_spec((FF, D)), row_spec(ROW, 128), row_spec(ROW, 128),
        ],
        out_specs=[
            row_spec(ROW, D), row_spec(ROW, 2 * D), row_spec(ROW, D),
            whole_spec((4096, 128)), whole_spec((8192, 128)), whole_spec((8192, 128)), whole_spec((8, D)),
        ],
        out_shape=[shape_of((t, D), BF), shape_of((t, 2 * D), BF), shape_of((t, D), F32)] + FLAT_FFN + [shape_of((8, D), F32)],
        scratch_shapes=[
            vm((ROW, D), BF), vm((ROW, D), BF), vm((HEADS, ROW), F32), vm((ROW, D), BF), vm((ROW, D), BF),
            vm((D, ROW), F32), vm((ROW, FF), BF), vm((ROW, FF), BF), vm((D, 2 * D), F32), vm((D, FF), F32), vm((FF, D), F32),
        ],
        compiler_params=params_of(60),
    )(r1, kv, go, vec, w["cross"], w["up"], w["down"], fq, fk)


def enc_back(gkv, mem, r1, r2, act, slope, w, vec):
    t = r1.shape[0]
    vm = pltpu.VMEM
    return kernel_call(
        enc_back_kernel,
        grid=(t // ROW,),
        in_specs=[
            row_spec(ROW, 2 * D), row_spec(ROW, D), row_spec(ROW, D), row_spec(ROW, D), row_spec(ROW, FF), row_spec(ROW, FF),
            whole_spec((6, D)), whole_spec((D, 2 * D)), whole_spec((D, FF)), whole_spec((FF, D)),
        ],
        out_specs=[
            row_spec(ROW, D), whole_spec((4096, 128)), whole_spec((8192, 128)), whole_spec((8192, 128)), whole_spec((8, D)),
        ],
        out_shape=[shape_of((t, D), F32)] + FLAT_FFN + [shape_of((8, D), F32)],
        scratch_shapes=[vm((D, 2 * D), F32), vm((D, FF), F32), vm((FF, D), F32)],
        compiler_params=params_of(60),
    )(gkv, mem, r1, r2, act, slope, vec, w["cross"], w["up"], w["down"])


def self_back(causal, x, r1, dy1, qkv, ctx, lse, w, vec, fq, fk):
    t = r1.shape[0]
    vm = pltpu.VMEM
    return kernel_call(
        functools.partial(self_back_kernel, causal),
        grid=(t // ROW,),
        in_specs=[
            row_spec(ROW, D), row_spec(ROW, D), row_spec(ROW, D), row_spec(ROW, 3 * D), row_spec(ROW, D), row_spec(HEADS, ROW),
            whole_spec((6, D)), whole_spec((D, 3 * D)), whole_spec((D, D)), row_spec(ROW, 128), row_spec(ROW, 128),
        ],
        out_specs=[row_spec(ROW, D), whole_spec((6144, 128)), whole_spec((2048, 128)), whole_spec((8, D))],
        out_shape=[
            shape_of((t, D), BF), shape_of((6144, 128), BF), shape_of((2048, 128), BF), shape_of((8, D), F32),
        ],
        scratch_shapes=[vm((ROW, D), BF), vm((ROW, 3 * D), BF), vm((D, ROW), F32), vm((D, 3 * D), F32), vm((D, D), F32)],
        compiler_params=params_of(60),
    )(x, r1, dy1, qkv, ctx, lse, vec, w["qkv"], w["out"], fq, fk)


def blanks(*shapes):
    return tuple(jnp.zeros(shape, dtype) for shape, dtype in shapes)


def mask_features(segments, live):
    t = segments.shape[0]
    lane = (jnp.arange(128, dtype=jnp.int32) % HD)[None, :]
    pair = lane // 2
    odd = lane % 2 == 1
    is_seg = pair < SEG_BITS
    is_pos = (pair >= SEG_BITS) & (pair < SEG_BITS + POS_BITS)
    place = (jnp.arange(t, dtype=jnp.int32) % ROW)[:, None]
    bit = jnp.where(
        is_seg,
        (segments[:, None] >> jnp.minimum(pair, SEG_BITS)) & 1,
        (place >> jnp.clip(pair - SEG_BITS, 0, POS_BITS)) & 1,
    )
    query = jnp.where(odd, 1 - bit, bit) * (is_seg | is_pos)
    key = jnp.where(odd, bit, 1 - bit)
    keys = [jnp.where(is_seg | (is_pos & (live[i][:, None] != 1)), key.astype(F32) * -BIG, 0.0).astype(BF) for i in range(2)]
    return query.astype(BF), keys[0], keys[1]


def passed_along(value, axis, steps):
    count = lax.axis_size(axis)
    first, last = (max(0, -steps), min(count, count - steps))
    return lax.ppermute(value, axis, [(source, source + steps) for source in range(first, last)])


def shards(params, first_moment, second_moment, inputs, segments, live_mask, out_grad):
    is_decoder = lax.axis_index("section") == 1
    me = lax.axis_index("batch")
    n = lax.axis_size("batch")
    share = params.shape[1]
    rows = 16 * (share // TILE + 2)
    shift = lax.rem(me * (share % TILE), TILE)
    x = inputs[0]
    t = x.shape[0]

    own = lax.dynamic_update_slice(jnp.zeros((rows * 128,), F32), params[0], (shift,)).reshape(rows, 128).astype(BF)
    pieces = lax.all_gather(own, "batch", axis=0, tiled=False)
    fq, fk_src, fk_tgt = mask_features(segments, live_mask)
    fk_self = jnp.where(is_decoder, fk_tgt, fk_src)
    *mats, vec_rows = split_weights(pieces, n, share)
    w = dict(zip(MATS, mats))
    vec = vec_rows[:24].astype(F32).reshape(6, D)

    qkv, ctx, lse, r1 = lax.cond(
        is_decoder,
        lambda: self_fwd(True, x, w, fq, fk_self),
        lambda: self_fwd(False, x, w, fq, fk_self),
    )
    mem, kv, act, slope, r2 = lax.cond(
        is_decoder,
        lambda: blanks(((t, D), BF), ((t, 2 * D), BF), ((t, FF), BF), ((t, FF), BF), ((t, D), F32)),
        lambda: enc_ffn(r1, w, vec),
    )
    kv_in = passed_along(kv, "section", 1)
    out, gkv, dy1_d, *rest_d = lax.cond(
        is_decoder,
        lambda: dec_call(r1, kv_in, out_grad, w, vec, fq, fk_src),
        lambda: blanks(
            ((t, D), BF), ((t, 2 * D), BF), ((t, D), F32), *((s.shape, s.dtype) for s in FLAT_FFN), ((8, D), F32)
        ),
    )
    gkv_in = passed_along(gkv, "section", -1)
    dy1, fl_cross, fl_up, fl_down, gvec_a = lax.cond(
        is_decoder,
        lambda: (dy1_d, *rest_d),
        lambda: enc_back(gkv_in, mem, r1, r2, act, slope, w, vec),
    )
    dx, fl_qkv, fl_out, gvec_b = lax.cond(
        is_decoder,
        lambda: self_back(True, x, r1, dy1, qkv, ctx, lse, w, vec, fq, fk_self),
        lambda: self_back(False, x, r1, dy1, qkv, ctx, lse, w, vec, fq, fk_self),
    )
    fl_vec = (gvec_a + gvec_b)[:6].reshape(24, 128).astype(BF)
    spare = 16 * (share * (n - 1) // TILE) + rows - FLAT_ROWS
    flat = jnp.concatenate([fl_qkv, fl_out, fl_cross, fl_up, fl_down, fl_vec, jnp.zeros((spare, 128), BF)], axis=0)
    stacked = jnp.concatenate([flat[16 * (share * b // TILE) :][:rows] for b in range(n)], axis=0)
    mine = lax.psum_scatter(stacked, "batch", scatter_dimension=0, tiled=True)
    grad_share = lax.dynamic_slice(mine.astype(F32).reshape(-1), (shift,), (share,))

    square_sum = lax.psum(jnp.sum(grad_share * grad_share), ("section", "batch"))
    grad_norm = jnp.sqrt(square_sum)
    clip_factor = MAXNORM / jnp.maximum(grad_norm, MAXNORM)
    scaled = grad_share * clip_factor
    new_first = BETA_ONE * first_moment[0] + (1.0 - BETA_ONE) * scaled
    new_second = BETA_TWO * second_moment[0] + (1.0 - BETA_TWO) * scaled * scaled
    learn_rate = D ** (-0.5) * min(STEP ** (-0.5), STEP * WARMUP ** (-1.5))
    first_hat = new_first / (1.0 - BETA_ONE**STEP)
    second_hat = new_second / (1.0 - BETA_TWO**STEP)
    param_step = learn_rate * first_hat / (jnp.sqrt(second_hat) + ADAM_EPS)
    layer_out = jnp.where(is_decoder, out, mem)
    return (param_step[None], new_first[None], new_second[None], grad_share[None], layer_out[None], dx[None], grad_norm)


def solution(mesh):
    in_specs = (
        P("section", "batch"),
        P("section", "batch"),
        P("section", "batch"),
        P("section", "batch", None),
        P("batch"),
        P(None, "batch"),
        P("batch", None),
    )
    out_specs = (
        P("section", "batch"),
        P("section", "batch"),
        P("section", "batch"),
        P("section", "batch"),
        P("section", "batch", None),
        P("section", "batch", None),
        P(),
    )
    return jax.shard_map(shards, mesh=mesh, in_specs=in_specs, out_specs=out_specs, check_vma=False)
```

```python
import functools

import jax
import jax.numpy as jnp
from jax import lax
from jax.experimental import pallas as pl
from jax.experimental.pallas import tpu as pltpu
from jax.sharding import PartitionSpec as P

D = 512
FF = 2048
HEADS = 8
HD = 64
ROW = 512
STEP = 1000
WARMUP = 4000

BIG = 1e30
LN_EPS = 1e-05
BETA_ONE = 0.9
BETA_TWO = 0.98
ADAM_EPS = 1e-09
MAXNORM = 0.1

F32 = jnp.float32
BF = jnp.bfloat16
TILE = 16 * 128
CHUNK = 512
SEG_BITS = 12
POS_BITS = 9
LOOP = False

MATS = {}
_at = 0
for _name, _rows, _cols in (("qkv", D, 3 * D), ("out", D, D), ("cross", D, 2 * D), ("up", D, FF), ("down", FF, D)):
    _width = _cols // 128
    MATS[_name] = (_rows, _cols, _at, {12: 16, 4: 64, 8: 32, 16: 16}[_width])
    _at += _rows * _width
VEC_AT = _at
FLAT_ROWS = _at + 24
REST_AT = MATS["out"][2]


def dot_nn(lhs, rhs):
    return jnp.dot(lhs, rhs, preferred_element_type=F32)


def dot_nt(lhs, rhs):
    return lax.dot_general(lhs, rhs, (((1,), (1,)), ((), ())), preferred_element_type=F32)


def dot_tn(lhs, rhs):
    return lax.dot_general(lhs, rhs, (((0,), (0,)), ((), ())), preferred_element_type=F32)


def params_of(mib):
    return pltpu.CompilerParams(vmem_limit_bytes=mib * 2**20)


def row_spec(rows, cols):
    return pl.BlockSpec((rows, cols), lambda i: (i, 0))


def whole_spec(shape):
    return pl.BlockSpec(shape, lambda i: (0,) * len(shape), pipeline_mode=pl.Buffered(1))


def shape_of(shape, dtype):
    return jax.ShapeDtypeStruct(shape, dtype)


def ln_parts(resid):
    center = resid - jnp.mean(resid, axis=-1, keepdims=True)
    rstd = lax.rsqrt(jnp.mean(center * center, axis=-1, keepdims=True) + LN_EPS)
    return center * rstd, rstd


def ln_back(grad, hat, rstd, gain):
    scaled = grad * gain
    first = jnp.mean(scaled, axis=-1, keepdims=True)
    second = jnp.mean(scaled * hat, axis=-1, keepdims=True)
    grad_resid = rstd * (scaled - first - hat * second)
    return grad_resid, jnp.sum(grad * hat, axis=0, keepdims=True), jnp.sum(grad, axis=0, keepdims=True)


def gelu_both(pre):
    size = jnp.abs(pre)
    near = 1.0 / (1.0 + (0.3275911 * 0.7071067811865476) * size)
    bell = jnp.exp(-0.5 * pre * pre)
    poly = near * (0.127414796 + near * (-0.142248368 + near * (0.7107068705 + near * (-0.7265760135 + near * 0.5307027145))))
    tail = poly * bell
    phi = jnp.where(pre >= 0.0, 1.0 - tail, tail)
    return pre * phi, phi + pre * bell * 0.3989422804014327


def low_lanes(rows):
    return lax.broadcasted_iota(jnp.int32, (rows, 128), 1) < HD


def triangle(size, keys_first, causal):
    row = lax.broadcasted_iota(jnp.int32, (size, size), 0)
    col = lax.broadcasted_iota(jnp.int32, (size, size), 1)
    keep = (row <= col) if keys_first else (col <= row)
    return jnp.where(keep | (causal == 0), 0.0, -BIG).astype(F32)


def over_pairs(body):
    if LOOP:

        def step(pair, _):
            body(pair)
            return 0

        lax.fori_loop(0, HEADS // 2, step, 0)
    else:
        for pair in range(HEADS // 2):
            body(pair)


def lanes(at, pair):
    first = at + 128 * pair
    return pl.ds(first if isinstance(pair, int) else pl.multiple_of(first, 128), 128)


def attend_fwd(causal, q_ref, q_at, k_ref, k_at, v_ref, v_at, fq, fk, ctx_ref, lse_ref, lse_s, tri_s):
    low = low_lanes(ROW)
    lane = lax.broadcasted_iota(jnp.int32, (ROW, 128), 1)
    one = jnp.asarray(1.0, BF)
    if causal is not None:
        tri_s[...] = triangle(ROW, False, causal)

    def body(pair):
        q_pair = q_ref[:, lanes(q_at, pair)] * jnp.asarray(HD**-0.5, BF)
        k_pair = k_ref[:, lanes(k_at, pair)]
        v_pair = v_ref[:, lanes(v_at, pair)]
        halves = []
        for e in range(2):
            sel = low if e == 0 else ~low
            s = dot_nt(jnp.where(sel, q_pair, fq), jnp.where(sel, k_pair, fk))
            if causal is not None:
                s = s + tri_s[...]
            top = jnp.max(s, axis=1, keepdims=True)
            p = jnp.exp(s - top)
            o = dot_nn(p.astype(BF), jnp.where(sel, v_pair, one))
            total = pltpu.roll(o, 64, 1)
            halves.append(o / total)
            lse = top + jnp.log(jnp.where(sel, total, o))
            lse_s[...] = jnp.where(lane == 2 * pair + e, lse, lse_s[...])
        ctx_ref[:, lanes(0, pair)] = jnp.where(low, halves[0], halves[1]).astype(BF)

    over_pairs(body)
    lse_ref[...] = lse_s[...].T[0:HEADS, :]


def attend_bwd(causal, q_ref, q_at, k_ref, k_at, v_ref, v_at, fq, fk, lse_ref, do_ref, outs, dqt_ref, kt_ref, tri_s):
    low = low_lanes(ROW)
    zero = jnp.zeros((ROW, 128), BF)
    scale = jnp.asarray(HD**-0.5, BF)
    kt_ref[...] = k_ref[:, k_at : k_at + D].T
    if causal is not None:
        tri_s[...] = triangle(ROW, True, causal)

    def body(pair):
        q_pair = q_ref[:, lanes(q_at, pair)] * scale
        k_pair = k_ref[:, lanes(k_at, pair)]
        v_pair = v_ref[:, lanes(v_at, pair)]
        do_pair = do_ref[:, lanes(0, pair)]
        dks, dvs = [], []
        for e in range(2):
            head = 2 * pair + e
            sel = low if e == 0 else ~low
            s = dot_nt(jnp.where(sel, k_pair, fk), jnp.where(sel, q_pair, fq))
            if causal is not None:
                s = s + tri_s[...]
            p = jnp.exp(s - lse_ref[pl.ds(head, 1), :])
            prod = p * dot_nt(jnp.where(sel, v_pair, zero), do_pair)
            ds = (prod - p * jnp.sum(prod, axis=0, keepdims=True)).astype(BF)
            dvs.append(dot_nn(p.astype(BF), do_pair))
            dks.append(dot_nn(ds, q_pair))
            rows = pl.ds(HD * head if isinstance(pair, int) else pl.multiple_of(HD * head, HD), HD)
            dqt_ref[rows, :] = dot_nn(kt_ref[rows, :], ds)
        for (ref, at), parts in ((outs[1], dks), (outs[2], dvs)):
            ref[:, lanes(at, pair)] = jnp.where(low, parts[0], parts[1]).astype(BF)

    over_pairs(body)
    ref, at = outs[0]
    ref[:, at : at + D] = (dqt_ref[...] * HD**-0.5).T.astype(BF)


def group_perm(name, to_flat):
    _, cols, _, group = MATS[name]
    width = cols // 128
    size = group * width
    row = lax.broadcasted_iota(jnp.int32, (size, size), 0)
    col = lax.broadcasted_iota(jnp.int32, (size, size), 1)
    blocked, flat = (col, row) if to_flat else (row, col)
    source = width * (blocked & (group - 1)) + lax.shift_right_logical(blocked, group.bit_length() - 1)
    return jnp.where(source == flat, 1.0, 0.0).astype(BF)


def to_matrix(name, flat_ref, at, mat_ref):
    rows, cols, _, group = MATS[name]
    width = cols // 128
    size = group * width
    perm = group_perm(name, False)

    def move(g, _):
        got = dot_nn(perm, flat_ref[at + g * size : at + (g + 1) * size, :]).astype(BF)
        for c in range(width):
            mat_ref[g * group : (g + 1) * group, 128 * c : 128 * c + 128] = got[c * group : (c + 1) * group]
        return 0

    for g in range(rows // group):
        move(g, 0)


def to_flat(name, mat_ref, flat_ref, at):
    rows, cols, _, group = MATS[name]
    width = cols // 128
    size = group * width
    perm = group_perm(name, True)

    def move(g, _):
        block = mat_ref[g * group : (g + 1) * group, :].astype(BF)
        blocked = jnp.concatenate([block[:, 128 * c : 128 * c + 128] for c in range(width)], axis=0)
        flat_ref[at + g * size : at + (g + 1) * size, :] = dot_nn(perm, blocked).astype(BF)
        return 0

    for g in range(rows // group):
        move(g, 0)


def chunks(body, total_s, loop):
    if not loop:
        parts = [body(slice(c * CHUNK, (c + 1) * CHUNK)) for c in range(FF // CHUNK)]
        return sum(parts[1:], parts[0])

    def step(c, _):
        part = body(pl.ds(pl.multiple_of(c * CHUNK, CHUNK), CHUNK))
        total_s[...] = jnp.where(c == 0, 0.0, total_s[...]) + part
        return 0

    lax.fori_loop(0, FF // CHUNK, step, 0)
    return total_s[...]


def ffn_fwd(hidden_ref, w_up, w_down, act_ref, slope_ref, total_s, loop):
    def body(cols):
        act, slope = gelu_both(dot_nn(hidden_ref[...], w_up[:, cols]))
        act_b = act.astype(BF)
        act_ref[:, cols] = act_b
        slope_ref[:, cols] = slope.astype(slope_ref.dtype)
        return dot_nn(act_b, w_down[cols, :])

    return chunks(body, total_s, loop)


def ffn_bwd(branch_ref, w_up, w_down, slope_ref, dz_ref, total_s, loop):
    def body(cols):
        grad_act = dot_nt(branch_ref[...], w_down[cols, :])
        grad_pre = (grad_act * slope_ref[:, cols].astype(F32)).astype(BF)
        dz_ref[:, cols] = grad_pre
        return dot_nt(grad_pre, w_up[:, cols])

    return chunks(body, total_s, loop)


def self_head(dy1, r1_ref, vec, w_out, dr1_ref, dctx_ref, gvec):
    hat1, rstd1 = ln_parts(r1_ref[...])
    dr1, gain1, shift1 = ln_back(dy1, hat1, rstd1, vec[0:1, :])
    dr1_ref[...] = dr1
    dctx_ref[...] = dot_nt(dr1.astype(BF), w_out[...]).astype(BF)
    gvec[0:1, :] = gain1
    gvec[1:2, :] = shift1


def copies(sources, targets, sems):
    made = [pltpu.make_async_copy(s, t, sems.at[i]) for i, (s, t) in enumerate(zip(sources, targets))]
    for one in made:
        one.start()
    return made


def piece_row(share, b):
    return 16 * (share * b // TILE)


def shift_kernel(share, shift_ref, params_ref, out_ref, rows_s):
    rows = out_ref.shape[0]
    full = share // 1024
    rows_s[0:16, :] = jnp.zeros((16, 128), F32)
    rows_s[16 + 8 * full :, :] = jnp.zeros((rows_s.shape[0] - 16 - 8 * full, 128), F32)

    def fill(k, _):
        at = pl.multiple_of(1024 * k, 1024)
        rows_s[pl.ds(pl.multiple_of(8 * k + 16, 8), 8), :] = params_ref[:, pl.ds(at, 1024)].reshape(8, 128)
        return 0

    lax.fori_loop(0, full, fill, 0, unroll=8)
    for r in range(-(-(share - 1024 * full) // 128)):
        at = 1024 * full + 128 * r
        width = min(128, share - at)
        rows_s[16 + 8 * full + r : 17 + 8 * full + r, 0:width] = params_ref[:, at : at + width]
    shift = shift_ref[0]
    down, right = shift // 128, lax.rem(shift, 128)
    lane = lax.broadcasted_iota(jnp.int32, (16, 128), 1)

    def move(k, _):
        same = rows_s[pl.ds(16 * k + 16 - down, 16), :]
        above = rows_s[pl.ds(16 * k + 15 - down, 16), :]
        got = jnp.where(lane >= right, pltpu.roll(same, right, 1), pltpu.roll(above, right, 1))
        out_ref[pl.ds(pl.multiple_of(16 * k, 16), 16), :] = got.astype(BF)
        return 0

    lax.fori_loop(0, rows // 16, move, 0, unroll=6)


def unshift_kernel(share, shift_ref, sums_ref, grad_ref, square_ref):
    shift = shift_ref[0]
    down, left = shift // 128, lax.rem(shift, 128)
    lane = lax.broadcasted_iota(jnp.int32, (8, 128), 1)
    full = share // 1024

    def block(at):
        same = sums_ref[pl.ds(at + down, 8), :]
        below = sums_ref[pl.ds(at + down + 1, 8), :]
        back = lax.rem(128 - left, 128)
        return jnp.where(lane < 128 - left, pltpu.roll(same, back, 1), pltpu.roll(below, back, 1))

    def move(k, total):
        got = block(8 * k)
        grad_ref[:, pl.ds(pl.multiple_of(1024 * k, 1024), 1024)] = got.reshape(1, 1024)
        return total + got * got

    total = lax.fori_loop(0, full, move, jnp.zeros((8, 128), F32), unroll=8)
    rest = share - 1024 * full
    if rest:
        got = block(8 * full)
        place = lax.broadcasted_iota(jnp.int32, (8, 128), 0) * 128 + lane
        got = jnp.where(place < rest, got, 0.0)
        total = total + got * got
        for r in range(-(-rest // 128)):
            width = min(128, rest - 128 * r)
            at = 1024 * full + 128 * r
            grad_ref[:, at : at + width] = got[r : r + 1, 0:width]
    square_ref[...] = total


def adam_kernel(share, clip_ref, grad_ref, first_ref, second_ref, step_ref, new_first_ref, new_second_ref):
    clip = clip_ref[0]
    rate = D ** (-0.5) * min(STEP ** (-0.5), STEP * WARMUP ** (-1.5))

    def update(at, width, fold):
        shape = (8, 128) if fold else (1, width)
        scaled = grad_ref[:, pl.ds(at, width)].reshape(shape) * clip
        first = BETA_ONE * first_ref[:, pl.ds(at, width)].reshape(shape) + (1.0 - BETA_ONE) * scaled
        second = BETA_TWO * second_ref[:, pl.ds(at, width)].reshape(shape) + (1.0 - BETA_TWO) * scaled * scaled
        first_hat = first / (1.0 - BETA_ONE**STEP)
        second_hat = second / (1.0 - BETA_TWO**STEP)
        step = rate * first_hat / (jnp.sqrt(second_hat) + ADAM_EPS)
        step_ref[:, pl.ds(at, width)] = step.reshape(1, width)
        new_first_ref[:, pl.ds(at, width)] = first.reshape(1, width)
        new_second_ref[:, pl.ds(at, width)] = second.reshape(1, width)

    def move(k, _):
        update(pl.multiple_of(1024 * k, 1024), 1024, True)
        return 0

    full = share // 1024
    lax.fori_loop(0, full, move, 0, unroll=4)
    for at in range(1024 * full, share, 128):
        update(at, min(128, share - at), False)


def weights_kernel(n, share, flat_in, *refs):
    outs, flat = refs[:6], refs[6]
    for b in range(n):
        tile = share * b // TILE
        last = -(-share * (b + 1) // TILE)
        start, count = 16 * tile, 16 * (last - tile)
        if (share * b) % TILE:
            flat[start : start + 16, :] += flat_in[b, 0:16, :]
        else:
            flat[start : start + 16, :] = flat_in[b, 0:16, :]
        flat[start + 16 : start + count, :] = flat_in[b, 16:count, :]
    for name, ref in zip(MATS, outs):
        to_matrix(name, flat, MATS[name][2], ref)
    outs[5][...] = flat[VEC_AT : VEC_AT + 32, :]


def self_fwd_kernel(causal_ref, x_ref, wqkv, wout, fq, fk, qkv_ref, ctx_ref, lse_ref, r1_ref, lse_s, tri_s):
    x = x_ref[...]
    qkv_ref[...] = dot_nn(x, wqkv[...]).astype(BF)
    attend_fwd(
        causal_ref[0], qkv_ref, 0, qkv_ref, D, qkv_ref, 2 * D, fq[...], fk[...], ctx_ref, lse_ref, lse_s, tri_s
    )
    r1_ref[...] = x.astype(F32) + dot_nn(ctx_ref[...], wout[...])


def enc_ffn_kernel(r1_ref, vec, w_up, w_down, w_cross, mem_ref, kv_ref, act_ref, slope_ref, r2_ref, hid_s, total_s):
    hat, _ = ln_parts(r1_ref[...])
    y1 = hat * vec[0:1, :] + vec[1:2, :]
    hid_s[...] = y1.astype(BF)
    r2_ref[...] = y1
    r2 = r2_ref[...] + ffn_fwd(hid_s, w_up, w_down, act_ref, slope_ref, total_s, True)
    r2_ref[...] = r2
    hat, _ = ln_parts(r2)
    mem = (hat * vec[2:3, :] + vec[3:4, :]).astype(BF)
    mem_ref[:, :D] = mem
    mem_ref[:, D:] = mem
    kv_ref[...] = dot_nn(mem, w_cross[...]).astype(BF)


def dec_kernel(
    row, r1_ref, kv_ref, go_any, vec, w_cross, w_out_any, w_up_any, w_down_any, fq, fk,
    out_any, gkv_ref, dr1_ref, dctx1_ref, act_any, dz_any, hid_any, br_any, left_any, right_ref, gvec,
    cq_s, lse_s, wide_s, dctx_s, dcq_s, dqt_s, kt_s, slope_s, act_s, dz_s, hid_s, br_s, left_s, out_s,
    go_ref, w_out, w_up, w_down, keep_s, total_s, in_sems, out_sems,
):
    up_copy, down_copy, go_copy, out_copy = copies(
        (w_up_any, w_down_any, go_any.at[pl.ds(row * ROW, ROW)], w_out_any), (w_up, w_down, go_ref, w_out), in_sems
    )
    sent = []

    def emit(source, target):
        sent.append(pltpu.make_async_copy(source, target, out_sems.at[len(sent)]))
        sent[-1].start()

    hat1, _ = ln_parts(r1_ref[...])
    y1 = hat1 * vec[0:1, :] + vec[1:2, :]
    y1_b = y1.astype(BF)
    left_s[:, :D] = y1_b
    cq_s[...] = dot_nn(y1_b, w_cross[:, :D]).astype(BF)
    ctx_s = left_s.at[:, D:]
    attend_fwd(None, cq_s, 0, kv_ref, 0, kv_ref, D, fq[...], fk[...], ctx_s, lse_s, wide_s, None)
    emit(left_s, left_any)
    r2 = y1 + dot_nn(ctx_s[...], w_cross[:, D:])
    hat2, rstd2 = ln_parts(r2)
    y2 = hat2 * vec[2:3, :] + vec[3:4, :]
    hid_s[...] = y2.astype(BF)
    keep_s[...] = y2
    emit(hid_s, hid_any)
    up_copy.wait()
    down_copy.wait()
    r3 = keep_s[...] + ffn_fwd(hid_s, w_up, w_down, act_s, slope_s, total_s, False)
    emit(act_s, act_any)
    hat3, rstd3 = ln_parts(r3)
    out_s[...] = (hat3 * vec[4:5, :] + vec[5:6, :]).astype(BF)
    emit(out_s, out_any)

    go_copy.wait()
    dr3, gain3, shift3 = ln_back(go_ref[...].astype(F32), hat3, rstd3, vec[4:5, :])
    br_s[...] = dr3.astype(BF)
    emit(br_s, br_any)
    keep_s[...] = dr3
    dy2 = keep_s[...] + ffn_bwd(br_s, w_up, w_down, slope_s, dz_s, total_s, False)
    emit(dz_s, dz_any)
    dr2, gain2, shift2 = ln_back(dy2, hat2, rstd2, vec[2:3, :])
    dr2_b = dr2.astype(BF)
    right_ref[:, D:] = dr2_b
    dctx_s[...] = dot_nt(dr2_b, w_cross[:, D:]).astype(BF)
    attend_bwd(
        None, cq_s, 0, kv_ref, 0, kv_ref, D, fq[...], fk[...], lse_s, dctx_s,
        ((dcq_s, 0), (gkv_ref, 0), (gkv_ref, D)), dqt_s, kt_s, None,
    )
    dcq = dcq_s[...]
    right_ref[:, :D] = dcq
    out_copy.wait()
    self_head(dr2 + dot_nt(dcq, w_cross[:, :D]), r1_ref, vec, w_out, dr1_ref, dctx1_ref, gvec)
    gvec[2:3, :] = gain2
    gvec[3:4, :] = shift2
    gvec[4:5, :] = gain3
    gvec[5:6, :] = shift3
    for one in sent:
        one.wait()


def enc_back_kernel(
    gkv_ref, r1_ref, r2_ref, slope_ref, vec, w_cross, w_out, w_up, w_down,
    dr1_ref, dctx1_ref, dz_ref, hid_ref, br_ref, gvec, keep_s, total_s,
):
    dmem = dot_nt(gkv_ref[...], w_cross[...])
    hat2, rstd2 = ln_parts(r2_ref[...])
    dr2, gain2, shift2 = ln_back(dmem, hat2, rstd2, vec[2:3, :])
    hat1, _ = ln_parts(r1_ref[...])
    hid_ref[...] = (hat1 * vec[0:1, :] + vec[1:2, :]).astype(BF)
    br_ref[...] = dr2.astype(BF)
    keep_s[...] = dr2
    dy1 = keep_s[...] + ffn_bwd(br_ref, w_up, w_down, slope_ref, dz_ref, total_s, True)
    self_head(dy1, r1_ref, vec, w_out, dr1_ref, dctx1_ref, gvec)
    gvec[2:3, :] = gain2
    gvec[3:4, :] = shift2
    gvec[4:8, :] = jnp.zeros((4, D), F32)


KINDS = ("hid", "dz", "ctx", "dr1", "left", "right", "act", "branch")


def rest_kernel(rows, dec_ref, *refs):
    count = len(KINDS) * rows
    sources, flat, refs = (refs[:count], refs[count : 2 * count]), refs[2 * count], refs[2 * count + 1 :]
    kept, (hid_t, g_big, g_cross, g_out, sems) = dict(zip(KINDS, refs)), refs[len(KINDS) :]

    def fetch(ins, i):
        target = kept[KINDS[i // rows]].at[pl.ds((i % rows) * ROW, ROW)]
        return pltpu.make_async_copy(ins[i], target, sems.at[i])

    for which, ins in enumerate(sources):

        @pl.when(dec_ref[0] == which)
        def _(ins=ins):
            for i in range(count):
                fetch(ins, i).start()

    def ready(*kinds):
        for kind in kinds:
            for r in range(rows):
                fetch(sources[0], KINDS.index(kind) * rows + r).wait()

    base = {name: MATS[name][2] - REST_AT for name in MATS}
    ready("hid", "dz")
    hid_t[...] = kept["hid"][...].T

    def up(c, _):
        cols = pl.ds(pl.multiple_of(c * CHUNK, CHUNK), CHUNK)
        g_big[:, cols] = dot_nn(hid_t[...], kept["dz"][:, cols])
        return 0

    lax.fori_loop(0, FF // CHUNK, up, 0)
    to_flat("up", g_big, flat, base["up"])
    ready("ctx", "dr1")
    g_out[...] = dot_tn(kept["ctx"][...], kept["dr1"][...].astype(BF))
    to_flat("out", g_out, flat, base["out"])
    ready("left", "right")
    for at in (0, D):
        g_cross[:, at : at + D] = dot_tn(kept["left"][:, at : at + D], kept["right"][:, at : at + D])
    to_flat("cross", g_cross, flat, base["cross"])
    ready("act", "branch")
    rows_n, _, _, group = MATS["down"]
    perm = group_perm("down", True)

    for c in range(rows_n // D):
        cols = slice(c * D, (c + 1) * D)
        g_out[...] = dot_tn(kept["act"][:, cols], kept["branch"][...])
        for g in range(D // group):
            block = g_out[g * group : (g + 1) * group, :].astype(BF)
            blocked = jnp.concatenate([block[:, 128 * j : 128 * j + 128] for j in range(4)], axis=0)
            at = base["down"] + (c * (D // group) + g) * 4 * group
            flat[at : at + 4 * group, :] = dot_nn(perm, blocked).astype(BF)


def self_back_kernel(causal_ref, dr1_ref, dctx_ref, qkv_ref, lse_ref, wqkv, fq, fk, dx_ref, dqkv, dqt_s, kt_s, tri_s):
    attend_bwd(
        causal_ref[0], qkv_ref, 0, qkv_ref, D, qkv_ref, 2 * D, fq[...], fk[...], lse_ref, dctx_ref,
        ((dqkv, 0), (dqkv, D), (dqkv, 2 * D)), dqt_s, kt_s, tri_s,
    )
    dx_ref[...] = (dr1_ref[...] + dot_nt(dqkv[...], wqkv[...])).astype(BF)


def qkv_kernel(rows, x_ref, *refs):
    ins, fl_qkv, dqkv, x_t, g_qkv, sems = refs[:rows], *refs[rows:]
    made = copies(ins, [dqkv.at[pl.ds(r * ROW, ROW)] for r in range(rows)], sems)
    x_t[...] = x_ref[...].T
    for one in made:
        one.wait()

    def step(c, _):
        cols = pl.ds(pl.multiple_of(c * D, D), D)
        g_qkv[:, cols] = dot_nn(x_t[...], dqkv[:, cols])
        return 0

    lax.fori_loop(0, 3, step, 0)
    to_flat("qkv", g_qkv, fl_qkv, 0)


def pack_kernel(share, planes, base, place_ref, *refs):
    parts, outs, flat = refs[:-5], refs[-5:-1], refs[-1]
    send_a, keep_a, send_b, keep_b = outs
    at = 0
    for part in parts:
        flat[at : at + part.shape[0], :] = part[...]
        at += part.shape[0]
    y, x = place_ref[0], place_ref[1]
    half = send_a.shape[2]
    for i, z in enumerate(planes):
        for j in range(2):
            for ref, y_to, x_to, skip in (
                (send_a, 1 - y, j, 0), (keep_a, y, j, 0), (send_b, j, 1 - x, half), (keep_b, j, x, half),
            ):
                b = 4 * z + 2 * y_to + x_to
                start = pl.multiple_of(16 * ((share * b) // TILE) - base + skip, 16)
                ref[i, j] = flat[pl.ds(start, half), :]


def kernel_call(body, micros=1, **options):
    cost = pl.CostEstimate(flops=micros * 10**9, bytes_accessed=0, transcendentals=0)
    call = pl.pallas_call(body, cost_estimate=cost, **options)
    return lambda *operands: tuple(call(*operands))


IN_VMEM = pl.BlockSpec(memory_space=pltpu.VMEM)
IN_SMEM = pl.BlockSpec(memory_space=pltpu.SMEM)
ANYWHERE = pl.BlockSpec(memory_space=pl.ANY)


def at_row(row, cols, rows=ROW):
    return pl.BlockSpec((rows, cols), lambda i: (row, 0), pipeline_mode=pl.Buffered(1))


def shifted(shift, params, share, rows):
    return kernel_call(
        functools.partial(shift_kernel, share),
        in_specs=[IN_SMEM, IN_VMEM],
        out_specs=[IN_VMEM],
        out_shape=[shape_of((rows, 128), BF)],
        scratch_shapes=[pltpu.VMEM((rows + 32, 128), F32)],
        compiler_params=params_of(16),
    )(shift, params)[0]


def unshifted(shift, sums, share):
    return kernel_call(
        functools.partial(unshift_kernel, share),
        in_specs=[IN_SMEM, IN_VMEM],
        out_specs=[IN_VMEM] * 2,
        out_shape=[shape_of((1, share), F32), shape_of((8, 128), F32)],
        compiler_params=params_of(16),
    )(shift, sums)


def adam(clip, grad, first, second, share):
    return kernel_call(
        functools.partial(adam_kernel, share),
        in_specs=[IN_SMEM] + [IN_VMEM] * 3,
        out_specs=[IN_VMEM] * 3,
        out_shape=[shape_of((1, share), F32)] * 3,
        compiler_params=params_of(24),
    )(clip, grad, first, second)


def split_weights(pieces, n, share):
    shapes = [(rows, cols) for rows, cols, _, _ in MATS.values()] + [(32, 128)]
    rows = 16 * (-(-share * n // TILE) + 2)
    return kernel_call(
        functools.partial(weights_kernel, n, share),
        in_specs=[IN_VMEM],
        out_specs=[IN_VMEM] * 6,
        out_shape=[shape_of(s, BF) for s in shapes],
        scratch_shapes=[pltpu.VMEM((rows, 128), BF)],
        compiler_params=params_of(48),
    )(pieces)


def row_shapes(*cols):
    return [shape_of((ROW, abs(c)), F32 if c < 0 else BF) for c in cols]


def self_fwd(causal, row, x, w, fq, fk):
    names = ("qkv", "ctx", "lse", "r1")
    vm = pltpu.VMEM
    got = kernel_call(
        self_fwd_kernel,
        micros=5,
        grid=(1,),
        in_specs=[IN_SMEM, at_row(row, D), whole_spec((D, 3 * D)), whole_spec((D, D)), at_row(row, 128), at_row(row, 128)],
        out_specs=[at_row(0, 3 * D), at_row(0, D), at_row(0, ROW, HEADS), at_row(0, D)],
        out_shape=row_shapes(3 * D, D) + [shape_of((HEADS, ROW), F32)] + row_shapes(-D),
        scratch_shapes=[vm((ROW, 128), F32), vm((ROW, ROW), F32)],
        compiler_params=params_of(32),
    )(causal, x, w["qkv"], w["out"], fq, fk)
    return dict(zip(names, got))


def enc_ffn(r1, w, vec):
    names = ("mem", "kv", "act", "slope", "r2")
    got = kernel_call(
        enc_ffn_kernel,
        micros=10,
        grid=(1,),
        in_specs=[
            at_row(0, D), whole_spec((6, D)), whole_spec((D, FF)), whole_spec((FF, D)), whole_spec((D, 2 * D)),
        ],
        out_specs=[at_row(0, 2 * D), at_row(0, 2 * D), at_row(0, FF), at_row(0, FF), at_row(0, D)],
        out_shape=row_shapes(2 * D, 2 * D, FF, FF, -D),
        scratch_shapes=[pltpu.VMEM((ROW, D), BF), pltpu.VMEM((ROW, D), F32)],
        compiler_params=params_of(48),
    )(r1, vec, w["up"], w["down"], w["cross"])
    return dict(zip(names, got))


def dec_call(row, r1, kv, go, w, vec, fq, fk):
    vm = pltpu.VMEM
    names = ("out", "gkv", "dr1", "dctx", "act", "dz", "hid", "branch", "left", "right", "gvec")
    got = kernel_call(
        functools.partial(dec_kernel, row),
        micros=23,
        grid=(1,),
        in_specs=[
            at_row(0, D), at_row(0, 2 * D), ANYWHERE, whole_spec((6, D)), whole_spec((D, 2 * D)),
            ANYWHERE, ANYWHERE, ANYWHERE, at_row(row, 128), at_row(row, 128),
        ],
        out_specs=[ANYWHERE, at_row(0, 2 * D), at_row(0, D), at_row(0, D)] + [ANYWHERE] * 5
        + [at_row(0, 2 * D), whole_spec((8, D))],
        out_shape=row_shapes(D, 2 * D, -D, D, FF, FF, D, D, 2 * D, 2 * D) + [shape_of((8, D), F32)],
        scratch_shapes=[
            vm((ROW, D), BF), vm((HEADS, ROW), F32), vm((ROW, 128), F32), vm((ROW, D), BF), vm((ROW, D), BF),
            vm((D, ROW), F32), vm((D, ROW), BF), vm((ROW, FF), BF), vm((ROW, FF), BF), vm((ROW, FF), BF), vm((ROW, D), BF),
            vm((ROW, D), BF), vm((ROW, 2 * D), BF), vm((ROW, D), BF), vm((ROW, D), BF), vm((D, D), BF), vm((D, FF), BF),
            vm((FF, D), BF), vm((ROW, D), F32), vm((ROW, D), F32), pltpu.SemaphoreType.DMA((4,)), pltpu.SemaphoreType.DMA((6,)),
        ],
        compiler_params=params_of(56),
    )(r1, kv, go, vec, w["cross"], w["out"], w["up"], w["down"], fq, fk)
    return dict(zip(names, got))


def enc_back(gkv, r1, fwd, w, vec):
    names = ("dr1", "dctx", "dz", "hid", "branch", "gvec")
    got = kernel_call(
        enc_back_kernel,
        micros=10,
        grid=(1,),
        in_specs=[
            at_row(0, 2 * D), at_row(0, D), at_row(0, D), at_row(0, FF), whole_spec((6, D)), whole_spec((D, 2 * D)),
            whole_spec((D, D)), whole_spec((D, FF)), whole_spec((FF, D)),
        ],
        out_specs=[at_row(0, c) for c in (D, D, FF, D, D)] + [whole_spec((8, D))],
        out_shape=row_shapes(-D, D, FF, D, D) + [shape_of((8, D), F32)],
        scratch_shapes=[pltpu.VMEM((ROW, D), F32)] * 2,
        compiler_params=params_of(56),
    )(gkv, r1, fwd["r2"], fwd["slope"], vec, w["cross"], w["out"], w["up"], w["down"])
    return dict(zip(names, got))


def rest_grads(is_dec, enc_rows, dec_rows):
    rows = len(dec_rows)
    ins = [row[kind] for some in (enc_rows, dec_rows) for kind in KINDS for row in some]
    vm = pltpu.VMEM
    kept = [vm((rows * ROW, dec_rows[0][kind].shape[1]), dec_rows[0][kind].dtype) for kind in KINDS]
    return kernel_call(
        functools.partial(rest_kernel, rows),
        micros=18,
        in_specs=[IN_SMEM] + [ANYWHERE] * len(ins),
        out_specs=[IN_VMEM],
        out_shape=[shape_of((VEC_AT - REST_AT, 128), BF)],
        scratch_shapes=kept
        + [vm((D, rows * ROW), BF), vm((D, FF), F32), vm((D, 2 * D), F32), vm((D, D), F32)]
        + [pltpu.SemaphoreType.DMA((len(KINDS) * rows,))],
        compiler_params=params_of(60),
    )(is_dec, *ins)[0]


def self_back(causal, row, grads, fwd, w, fq, fk):
    vm = pltpu.VMEM
    shapes = row_shapes(D, 3 * D)
    return kernel_call(
        self_back_kernel,
        micros=8,
        grid=(1,),
        in_specs=[
            IN_SMEM, at_row(0, D), at_row(0, D), at_row(0, 3 * D), at_row(0, ROW, HEADS), whole_spec((D, 3 * D)),
            at_row(row, 128), at_row(row, 128),
        ],
        out_specs=[whole_spec(s.shape) for s in shapes],
        out_shape=shapes,
        scratch_shapes=[vm((D, ROW), F32), vm((D, ROW), BF), vm((ROW, ROW), F32)],
        compiler_params=params_of(40),
    )(causal, grads["dr1"], grads["dctx"], fwd["qkv"], fwd["lse"], w["qkv"], fq, fk)


def qkv_grad(x, dqkvs):
    vm = pltpu.VMEM
    t, rows = x.shape[0], len(dqkvs)
    return kernel_call(
        functools.partial(qkv_kernel, rows),
        micros=5,
        in_specs=[IN_VMEM] + [ANYWHERE] * rows,
        out_specs=[IN_VMEM],
        out_shape=[shape_of((REST_AT, 128), BF)],
        scratch_shapes=[vm((t, 3 * D), BF), vm((D, t), BF), vm((D, 3 * D), F32), pltpu.SemaphoreType.DMA((rows,))],
        compiler_params=params_of(40),
    )(x, *dqkvs)[0]


def pack(place, parts, planes, base, share, rows):
    half = rows // 2
    total = sum(p.shape[0] for p in parts)
    need = piece_row(share, 4 * planes[-1] + 3) - base + rows
    return kernel_call(
        functools.partial(pack_kernel, share, planes, base),
        in_specs=[IN_SMEM] + [IN_VMEM] * len(parts),
        out_specs=[IN_VMEM] * 4,
        out_shape=[shape_of((len(planes), 2, half, 128), BF)] * 4,
        scratch_shapes=[pltpu.VMEM((max(total, need), 128), BF)],
        compiler_params=params_of(40),
    )(place, *parts)


def mask_features(segments, live):
    t = segments.shape[0]
    lane = (jnp.arange(128, dtype=jnp.int32) % HD)[None, :]
    pair = lane // 2
    odd = lane % 2 == 1
    is_seg = pair < SEG_BITS
    is_pos = (pair >= SEG_BITS) & (pair < SEG_BITS + POS_BITS)
    place = (jnp.arange(t, dtype=jnp.int32) % ROW)[:, None]
    bit = jnp.where(
        is_seg,
        (segments[:, None] >> jnp.minimum(pair, SEG_BITS)) & 1,
        (place >> jnp.clip(pair - SEG_BITS, 0, POS_BITS)) & 1,
    )
    query = jnp.where(odd, 1 - bit, bit) * (is_seg | is_pos)
    key = jnp.where(odd, bit, 1 - bit)
    keys = [jnp.where(is_seg | (is_pos & (live[i][:, None] != 1)), key.astype(F32) * -BIG, 0.0).astype(BF) for i in range(2)]
    return query.astype(BF), keys[0], keys[1]


def passed_along(value, axis, steps):
    count = lax.axis_size(axis)
    first, last = (max(0, -steps), min(count, count - steps))
    return lax.ppermute(value, axis, [(source, source + steps) for source in range(first, last)])


def ghosts(shapes):
    if not shapes:
        return ()
    return kernel_call(lambda *refs: None, out_specs=[ANYWHERE] * len(shapes), out_shape=list(shapes))()


def either(is_decoder, dec, enc):
    thunks = (enc, dec)
    made = [jax.eval_shape(t) for t in thunks]
    slots, where = [], []
    for tree in made:
        free = list(range(len(slots)))
        taken = []
        for leaf in jax.tree.leaves(tree):
            key = (leaf.shape, leaf.dtype)
            match = next((i for i in free if slots[i] == key), None)
            if match is None:
                slots.append(key)
                match = len(slots) - 1
            else:
                free.remove(match)
            taken.append(match)
        where.append(taken)

    def branch(which):
        def run():
            leaves = jax.tree.leaves(thunks[which]())
            filled = dict(zip(where[which], leaves))
            missing = [i for i in range(len(slots)) if i not in filled]
            filled.update(zip(missing, ghosts([shape_of(*slots[i]) for i in missing])))
            return tuple(filled[i] for i in range(len(slots)))

        return run

    got = lax.cond(is_decoder, branch(1), branch(0))
    back = [jax.tree.unflatten(jax.tree.structure(made[i]), [got[s] for s in where[i]]) for i in range(2)]
    return back[1], back[0]


def plane_permute(value, step):
    return lax.ppermute(value, "batch", [(i, i ^ step) for i in range(16)])


def line_permute(value, step, sources):
    pairs = [(4 * z + k, 4 * (z + step) + k) for z in sources for k in range(4)]
    return lax.ppermute(value, "batch", pairs)


def added(*values):
    total = values[0].astype(F32)
    for value in values[1:]:
        total = total + value.astype(F32)
    return total


def plane_sums(packed, y, x):
    send_a, keep_a, send_b, keep_b = packed
    got_a, got_b = plane_permute(send_a, 2), plane_permute(send_b, 1)

    def part(keep, got, index):
        return added(lax.dynamic_index_in_dim(keep, index, 1, False), lax.dynamic_index_in_dim(got, index, 1, False))

    far_a, far_b = part(keep_a, got_a, 1 - x).astype(BF), part(keep_b, got_b, 1 - y).astype(BF)
    in_a, in_b = plane_permute(far_a, 1), plane_permute(far_b, 2)
    sum_a, sum_b = added(part(keep_a, got_a, x), in_a), added(part(keep_b, got_b, y), in_b)
    return jnp.stack([sum_a.astype(BF), sum_b.astype(BF)], axis=1)


def line_sums(early, late, z):
    one, two, three = early[0], early[1], early[2]

    def low(value):
        return value.astype(BF)

    up = line_permute(three, 1, (0,))
    down = line_permute(one, -1, (3,))
    up = line_permute(low(jnp.where(z == 0, two.astype(F32), added(three, up))), 1, (0, 1))
    down = line_permute(low(jnp.where(z == 3, two.astype(F32), added(one, down))), -1, (2, 3))
    third = jnp.where(z == 0, one.astype(F32), added(jnp.where(z == 1, two, three), up))
    up = line_permute(low(third), 1, (0, 1, 2))
    zero = late[0]
    near = line_permute(zero, -1, (1, 3))
    pair = added(zero, near)
    far = line_permute(low(pair), -2, (2,))
    own = jnp.where(z == 1, one, jnp.where(z == 2, two, three))
    return jnp.where(z == 0, added(pair, far), added(own, up, down))


def shards(params, first_moment, second_moment, inputs, segments, live_mask, out_grad):
    is_decoder = lax.axis_index("section") == 1
    me = lax.axis_index("batch")
    n = lax.axis_size("batch")
    share = params.shape[1]
    rows = 16 * (share // TILE + 2)
    shift = lax.rem(me * (share % TILE), TILE)[None]
    x = inputs[0]
    t = x.shape[0]
    count = t // ROW

    own = shifted(shift, params, share, rows)
    pieces = lax.all_gather(own, "batch", axis=0, tiled=False)
    fq, fk_src, fk_tgt = mask_features(segments, live_mask)
    fk_self = jnp.where(is_decoder, fk_tgt, fk_src)
    pieces, fq, fk_src, fk_self = lax.optimization_barrier((pieces, fq, fk_src, fk_self))
    *mats, vec_rows = split_weights(pieces, n, share)
    w = dict(zip(MATS, mats))
    vec = vec_rows[:24].astype(F32).reshape(6, D)

    def nothing():
        return {}

    flag = is_decoder.astype(jnp.int32)[None]
    fwd = [self_fwd(flag, 0, x, w, fq, fk_self)]
    _, first = either(is_decoder, nothing, lambda: enc_ffn(fwd[0]["r1"], w, vec))
    kv_in = passed_along(first["kv"], "section", 1)
    fwd += [self_fwd(flag, r, x, w, fq, fk_self) for r in range(1, count)]
    kept = [first]

    def dec_row(row, kv):
        return dec_call(row, fwd[row]["r1"], kv, out_grad, w, vec, fq, fk_src)

    def enc_row(row, grad_kv):
        return enc_back(grad_kv, fwd[row]["r1"], kept[row], w, vec)

    dec_rows, enc_rows = [], []
    kvs, back = [kv_in], []
    for row in range(count):

        def enc_make():
            done = [enc_row(row - 1, back[row - 1])] if row else []
            ahead = [enc_ffn(fwd[row + 1]["r1"], w, vec)] if row + 1 < count else []
            return ahead, done

        got, (ahead, done) = either(is_decoder, lambda: dec_row(row, kvs[row]), enc_make)
        dec_rows.append(got)
        enc_rows += done
        kept += ahead
        kvs += [passed_along(k["kv"], "section", 1) for k in ahead]
        back.append(passed_along(got["gkv"], "section", -1))
    _, done = either(is_decoder, nothing, lambda: enc_row(count - 1, back[count - 1]))
    enc_rows.append(done)

    def grads_of(rows):
        return [{**made, "ctx": fwd[r]["ctx"]} for r, made in enumerate(rows)]

    enc_all = [
        {**made, "act": kept[r]["act"], "left": kept[r]["mem"], "right": back[r]} for r, made in enumerate(enc_rows)
    ]
    rest = rest_grads(flag, grads_of(enc_all), grads_of(dec_rows))
    gvec = jnp.where(is_decoder, sum(r["gvec"] for r in dec_rows), sum(r["gvec"] for r in enc_rows))
    fl_vec = jnp.pad(gvec[:6].reshape(24, 128).astype(BF), ((0, 24), (0, 0)))

    y, x_at, z = lax.rem(me // 2, 2), lax.rem(me, 2), me // 4
    place = jnp.stack([y, x_at])
    custom = n == 16
    if custom:
        early = plane_sums(pack(place, [rest, fl_vec], (1, 2, 3), REST_AT, share, rows), y, x_at)

    dxs, dqkvs = [], []
    for row in range(count):
        mine = {k: jnp.where(is_decoder, dec_rows[row][k], enc_rows[row][k]) for k in ("dr1", "dctx")}
        dx, dqkv = self_back(flag, row, mine, fwd[row], w, fq, fk_self)
        dxs.append(dx)
        dqkvs.append(dqkv)
    fl_qkv = qkv_grad(x, dqkvs)
    dx = jnp.concatenate(dxs, axis=0)
    layer_out = jnp.where(
        is_decoder,
        jnp.concatenate([r["out"] for r in dec_rows], axis=0),
        jnp.concatenate([k["mem"][:, :D] for k in kept], axis=0),
    )

    if custom:
        need = piece_row(share, 3) + rows
        late = plane_sums(pack(place, [fl_qkv, rest[: need - REST_AT]], (0,), 0, share, rows), y, x_at)
        mine = line_sums(early, late, z).reshape(rows, 128)
    else:
        spare = jnp.zeros((piece_row(share, n - 1) + rows - FLAT_ROWS, 128), BF)
        flat = jnp.concatenate([fl_qkv, rest, fl_vec[:24], spare], axis=0)
        stacked = jnp.concatenate([flat[piece_row(share, b) :][:rows] for b in range(n)], axis=0)
        mine = lax.psum_scatter(stacked, "batch", scatter_dimension=0, tiled=True).astype(F32)
    grad_share, squares = unshifted(shift, jnp.pad(mine, ((0, 8), (0, 0))), share)

    square_sum = jnp.sum(squares)
    if custom:
        square_sum = square_sum.reshape(1, 1)
        square_sum = square_sum + lax.ppermute(square_sum, "section", [(0, 1), (1, 0)])
        for step in (1, 2, 4, 8):
            square_sum = square_sum + plane_permute(square_sum, step)
        square_sum = square_sum[0, 0]
    else:
        square_sum = lax.psum(square_sum, ("section", "batch"))
    grad_norm = jnp.sqrt(square_sum)
    clip_factor = MAXNORM / jnp.maximum(grad_norm, MAXNORM)
    param_step, new_first, new_second = adam(clip_factor[None], grad_share, first_moment, second_moment, share)
    return (param_step, new_first, new_second, grad_share, layer_out[None], dx[None], grad_norm)


def solution(mesh):
    in_specs = (
        P("section", "batch"),
        P("section", "batch"),
        P("section", "batch"),
        P("section", "batch", None),
        P("batch"),
        P(None, "batch"),
        P("batch", None),
    )
    out_specs = (
        P("section", "batch"),
        P("section", "batch"),
        P("section", "batch"),
        P("section", "batch"),
        P("section", "batch", None),
        P("section", "batch", None),
        P(),
    )
    return jax.shard_map(shards, mesh=mesh, in_specs=in_specs, out_specs=out_specs, check_vma=False)
```

```python
import functools

import jax
import jax.numpy as jnp
from jax import lax
from jax.experimental import pallas as pl
from jax.experimental.pallas import tpu as pltpu
from jax.sharding import PartitionSpec as P

D = 512
FF = 2048
HEADS = 8
HD = 64
ROW = 512
STEP = 1000
WARMUP = 4000

BIG = 1e30
LN_EPS = 1e-05
BETA_ONE = 0.9
BETA_TWO = 0.98
ADAM_EPS = 1e-09
MAXNORM = 0.1

F32 = jnp.float32
BF = jnp.bfloat16
TILE = 16 * 128
CHUNK = 512
SEG_BITS = 12
POS_BITS = 9
LOOP = False

MATS = {}
_at = 0
for _name, _rows, _cols in (("qkv", D, 3 * D), ("out", D, D), ("cross", D, 2 * D), ("up", D, FF), ("down", FF, D)):
    _width = _cols // 128
    MATS[_name] = (_rows, _cols, _at, {12: 16, 4: 64, 8: 32, 16: 16}[_width])
    _at += _rows * _width
VEC_AT = _at
FLAT_ROWS = _at + 24
REST_AT = MATS["out"][2]


def dot_nn(lhs, rhs):
    return jnp.dot(lhs, rhs, preferred_element_type=F32)


def dot_nt(lhs, rhs):
    return lax.dot_general(lhs, rhs, (((1,), (1,)), ((), ())), preferred_element_type=F32)


def dot_tn(lhs, rhs):
    return lax.dot_general(lhs, rhs, (((0,), (0,)), ((), ())), preferred_element_type=F32)


def params_of(mib):
    return pltpu.CompilerParams(vmem_limit_bytes=mib * 2**20)


def row_spec(rows, cols):
    return pl.BlockSpec((rows, cols), lambda i: (i, 0))


def whole_spec(shape):
    return pl.BlockSpec(shape, lambda i: (0,) * len(shape), pipeline_mode=pl.Buffered(1))


def shape_of(shape, dtype):
    return jax.ShapeDtypeStruct(shape, dtype)


def ln_parts(resid):
    center = resid - jnp.mean(resid, axis=-1, keepdims=True)
    rstd = lax.rsqrt(jnp.mean(center * center, axis=-1, keepdims=True) + LN_EPS)
    return center * rstd, rstd


def ln_back(grad, hat, rstd, gain):
    scaled = grad * gain
    first = jnp.mean(scaled, axis=-1, keepdims=True)
    second = jnp.mean(scaled * hat, axis=-1, keepdims=True)
    grad_resid = rstd * (scaled - first - hat * second)
    return grad_resid, jnp.sum(grad * hat, axis=0, keepdims=True), jnp.sum(grad, axis=0, keepdims=True)


def gelu_both(pre):
    size = jnp.abs(pre)
    near = 1.0 / (1.0 + (0.3275911 * 0.7071067811865476) * size)
    bell = jnp.exp(-0.5 * pre * pre)
    poly = near * (0.127414796 + near * (-0.142248368 + near * (0.7107068705 + near * (-0.7265760135 + near * 0.5307027145))))
    tail = poly * bell
    phi = jnp.where(pre >= 0.0, 1.0 - tail, tail)
    return pre * phi, phi + pre * bell * 0.3989422804014327


def low_lanes(rows):
    return lax.broadcasted_iota(jnp.int32, (rows, 128), 1) < HD


def triangle(size, keys_first, causal):
    row = lax.broadcasted_iota(jnp.int32, (size, size), 0)
    col = lax.broadcasted_iota(jnp.int32, (size, size), 1)
    keep = (row <= col) if keys_first else (col <= row)
    return jnp.where(keep | (causal == 0), 0.0, -BIG).astype(F32)


def over_pairs(body):
    if LOOP:

        def step(pair, _):
            body(pair)
            return 0

        lax.fori_loop(0, HEADS // 2, step, 0)
    else:
        for pair in range(HEADS // 2):
            body(pair)


def lanes(at, pair):
    first = at + 128 * pair
    return pl.ds(first if isinstance(pair, int) else pl.multiple_of(first, 128), 128)


def attend_fwd(causal, q_ref, q_at, k_ref, k_at, v_ref, v_at, fq, fk, ctx_ref, lse_ref, lse_s, tri_s):
    low = low_lanes(ROW)
    lane = lax.broadcasted_iota(jnp.int32, (ROW, 128), 1)
    one = jnp.asarray(1.0, BF)
    if causal is not None:
        tri_s[...] = triangle(ROW, False, causal)

    def body(pair):
        q_pair = q_ref[:, lanes(q_at, pair)] * jnp.asarray(HD**-0.5, BF)
        k_pair = k_ref[:, lanes(k_at, pair)]
        v_pair = v_ref[:, lanes(v_at, pair)]
        halves = []
        for e in range(2):
            sel = low if e == 0 else ~low
            s = dot_nt(jnp.where(sel, q_pair, fq), jnp.where(sel, k_pair, fk))
            if causal is not None:
                s = s + tri_s[...]
            top = jnp.max(s, axis=1, keepdims=True)
            p = jnp.exp(s - top)
            o = dot_nn(p.astype(BF), jnp.where(sel, v_pair, one))
            total = pltpu.roll(o, 64, 1)
            halves.append(o / total)
            lse = top + jnp.log(jnp.where(sel, total, o))
            lse_s[...] = jnp.where(lane == 2 * pair + e, lse, lse_s[...])
        ctx_ref[:, lanes(0, pair)] = jnp.where(low, halves[0], halves[1]).astype(BF)

    over_pairs(body)
    lse_ref[...] = lse_s[...].T[0:HEADS, :]


def attend_bwd(causal, q_ref, q_at, k_ref, k_at, v_ref, v_at, fq, fk, lse_ref, do_ref, outs, dqt_ref, kt_ref, tri_s):
    low = low_lanes(ROW)
    zero = jnp.zeros((ROW, 128), BF)
    scale = jnp.asarray(HD**-0.5, BF)
    kt_ref[...] = k_ref[:, k_at : k_at + D].T
    if causal is not None:
        tri_s[...] = triangle(ROW, True, causal)

    def body(pair):
        q_pair = q_ref[:, lanes(q_at, pair)] * scale
        k_pair = k_ref[:, lanes(k_at, pair)]
        v_pair = v_ref[:, lanes(v_at, pair)]
        do_pair = do_ref[:, lanes(0, pair)]
        dks, dvs = [], []
        for e in range(2):
            head = 2 * pair + e
            sel = low if e == 0 else ~low
            s = dot_nt(jnp.where(sel, k_pair, fk), jnp.where(sel, q_pair, fq))
            if causal is not None:
                s = s + tri_s[...]
            p = jnp.exp(s - lse_ref[pl.ds(head, 1), :])
            prod = p * dot_nt(jnp.where(sel, v_pair, zero), do_pair)
            ds = (prod - p * jnp.sum(prod, axis=0, keepdims=True)).astype(BF)
            dvs.append(dot_nn(p.astype(BF), do_pair))
            dks.append(dot_nn(ds, q_pair))
            rows = pl.ds(HD * head if isinstance(pair, int) else pl.multiple_of(HD * head, HD), HD)
            dqt_ref[rows, :] = dot_nn(kt_ref[rows, :], ds)
        for (ref, at), parts in ((outs[1], dks), (outs[2], dvs)):
            ref[:, lanes(at, pair)] = jnp.where(low, parts[0], parts[1]).astype(BF)

    over_pairs(body)
    ref, at = outs[0]
    ref[:, at : at + D] = (dqt_ref[...] * HD**-0.5).T.astype(BF)


def group_perm(name, to_flat):
    _, cols, _, group = MATS[name]
    width = cols // 128
    size = group * width
    row = lax.broadcasted_iota(jnp.int32, (size, size), 0)
    col = lax.broadcasted_iota(jnp.int32, (size, size), 1)
    blocked, flat = (col, row) if to_flat else (row, col)
    source = width * (blocked & (group - 1)) + lax.shift_right_logical(blocked, group.bit_length() - 1)
    return jnp.where(source == flat, 1.0, 0.0).astype(BF)


def to_matrix(name, flat_ref, at, mat_ref):
    rows, cols, _, group = MATS[name]
    width = cols // 128
    size = group * width
    perm = group_perm(name, False)

    def move(g, _):
        got = dot_nn(perm, flat_ref[at + g * size : at + (g + 1) * size, :]).astype(BF)
        for c in range(width):
            mat_ref[g * group : (g + 1) * group, 128 * c : 128 * c + 128] = got[c * group : (c + 1) * group]
        return 0

    for g in range(rows // group):
        move(g, 0)


def to_flat(name, mat_ref, flat_ref, at):
    rows, cols, _, group = MATS[name]
    width = cols // 128
    size = group * width
    perm = group_perm(name, True)

    def move(g, _):
        block = mat_ref[g * group : (g + 1) * group, :].astype(BF)
        blocked = jnp.concatenate([block[:, 128 * c : 128 * c + 128] for c in range(width)], axis=0)
        flat_ref[at + g * size : at + (g + 1) * size, :] = dot_nn(perm, blocked).astype(BF)
        return 0

    for g in range(rows // group):
        move(g, 0)


def chunks(body, total_s, loop):
    if not loop:
        parts = [body(slice(c * CHUNK, (c + 1) * CHUNK)) for c in range(FF // CHUNK)]
        return sum(parts[1:], parts[0])

    def step(c, _):
        part = body(pl.ds(pl.multiple_of(c * CHUNK, CHUNK), CHUNK))
        total_s[...] = jnp.where(c == 0, 0.0, total_s[...]) + part
        return 0

    lax.fori_loop(0, FF // CHUNK, step, 0)
    return total_s[...]


def ffn_fwd(hidden_ref, w_up, w_down, act_ref, slope_ref, total_s, loop):
    def body(cols):
        act, slope = gelu_both(dot_nn(hidden_ref[...], w_up[:, cols]))
        act_b = act.astype(BF)
        act_ref[:, cols] = act_b
        slope_ref[:, cols] = slope.astype(slope_ref.dtype)
        return dot_nn(act_b, w_down[cols, :])

    return chunks(body, total_s, loop)


def ffn_bwd(branch_ref, w_up, w_down, slope_ref, dz_ref, total_s, loop):
    def body(cols):
        grad_act = dot_nt(branch_ref[...], w_down[cols, :])
        grad_pre = (grad_act * slope_ref[:, cols].astype(F32)).astype(BF)
        dz_ref[:, cols] = grad_pre
        return dot_nt(grad_pre, w_up[:, cols])

    return chunks(body, total_s, loop)


def self_head(dy1, r1_ref, vec, w_out, dr1_ref, dctx_ref, gvec):
    hat1, rstd1 = ln_parts(r1_ref[...])
    dr1, gain1, shift1 = ln_back(dy1, hat1, rstd1, vec[0:1, :])
    dr1_ref[...] = dr1
    dctx_ref[...] = dot_nt(dr1.astype(BF), w_out[...]).astype(BF)
    gvec[0:1, :] = gain1
    gvec[1:2, :] = shift1


def copies(sources, targets, sems):
    made = [pltpu.make_async_copy(s, t, sems.at[i]) for i, (s, t) in enumerate(zip(sources, targets))]
    for one in made:
        one.start()
    return made


def piece_row(share, b):
    return 16 * (share * b // TILE)


def shift_kernel(share, shift_ref, params_ref, out_ref, rows_s):
    rows = out_ref.shape[0]
    full = share // 1024
    rows_s[0:16, :] = jnp.zeros((16, 128), F32)
    rows_s[16 + 8 * full :, :] = jnp.zeros((rows_s.shape[0] - 16 - 8 * full, 128), F32)

    def fill(k, _):
        at = pl.multiple_of(1024 * k, 1024)
        rows_s[pl.ds(pl.multiple_of(8 * k + 16, 8), 8), :] = params_ref[:, pl.ds(at, 1024)].reshape(8, 128)
        return 0

    lax.fori_loop(0, full, fill, 0, unroll=8)
    for r in range(-(-(share - 1024 * full) // 128)):
        at = 1024 * full + 128 * r
        width = min(128, share - at)
        rows_s[16 + 8 * full + r : 17 + 8 * full + r, 0:width] = params_ref[:, at : at + width]
    shift = shift_ref[0]
    down, right = shift // 128, lax.rem(shift, 128)
    lane = lax.broadcasted_iota(jnp.int32, (16, 128), 1)

    def move(k, _):
        same = rows_s[pl.ds(16 * k + 16 - down, 16), :]
        above = rows_s[pl.ds(16 * k + 15 - down, 16), :]
        got = jnp.where(lane >= right, pltpu.roll(same, right, 1), pltpu.roll(above, right, 1))
        out_ref[pl.ds(pl.multiple_of(16 * k, 16), 16), :] = got.astype(BF)
        return 0

    lax.fori_loop(0, rows // 16, move, 0, unroll=6)


def unshift_kernel(share, shift_ref, sums_ref, grad_ref, square_ref):
    shift = shift_ref[0]
    down, left = shift // 128, lax.rem(shift, 128)
    lane = lax.broadcasted_iota(jnp.int32, (8, 128), 1)
    full = share // 1024

    def block(at):
        same = sums_ref[pl.ds(at + down, 8), :]
        below = sums_ref[pl.ds(at + down + 1, 8), :]
        back = lax.rem(128 - left, 128)
        return jnp.where(lane < 128 - left, pltpu.roll(same, back, 1), pltpu.roll(below, back, 1))

    def move(k, total):
        got = block(8 * k)
        grad_ref[:, pl.ds(pl.multiple_of(1024 * k, 1024), 1024)] = got.reshape(1, 1024)
        return total + got * got

    total = lax.fori_loop(0, full, move, jnp.zeros((8, 128), F32), unroll=8)
    rest = share - 1024 * full
    if rest:
        got = block(8 * full)
        place = lax.broadcasted_iota(jnp.int32, (8, 128), 0) * 128 + lane
        got = jnp.where(place < rest, got, 0.0)
        total = total + got * got
        for r in range(-(-rest // 128)):
            width = min(128, rest - 128 * r)
            at = 1024 * full + 128 * r
            grad_ref[:, at : at + width] = got[r : r + 1, 0:width]
    square_ref[...] = total


def adam_kernel(share, clip_ref, grad_ref, first_ref, second_ref, step_ref, new_first_ref, new_second_ref):
    clip = clip_ref[0]
    rate = D ** (-0.5) * min(STEP ** (-0.5), STEP * WARMUP ** (-1.5))

    def update(at, width, fold):
        shape = (8, 128) if fold else (1, width)
        scaled = grad_ref[:, pl.ds(at, width)].reshape(shape) * clip
        first = BETA_ONE * first_ref[:, pl.ds(at, width)].reshape(shape) + (1.0 - BETA_ONE) * scaled
        second = BETA_TWO * second_ref[:, pl.ds(at, width)].reshape(shape) + (1.0 - BETA_TWO) * scaled * scaled
        first_hat = first / (1.0 - BETA_ONE**STEP)
        second_hat = second / (1.0 - BETA_TWO**STEP)
        step = rate * first_hat / (jnp.sqrt(second_hat) + ADAM_EPS)
        step_ref[:, pl.ds(at, width)] = step.reshape(1, width)
        new_first_ref[:, pl.ds(at, width)] = first.reshape(1, width)
        new_second_ref[:, pl.ds(at, width)] = second.reshape(1, width)

    def move(k, _):
        update(pl.multiple_of(1024 * k, 1024), 1024, True)
        return 0

    full = share // 1024
    lax.fori_loop(0, full, move, 0, unroll=4)
    for at in range(1024 * full, share, 128):
        update(at, min(128, share - at), False)


def weights_kernel(n, share, flat_in, *refs):
    outs, flat = refs[:6], refs[6]
    for b in range(n):
        tile = share * b // TILE
        last = -(-share * (b + 1) // TILE)
        start, count = 16 * tile, 16 * (last - tile)
        if (share * b) % TILE:
            flat[start : start + 16, :] += flat_in[b, 0:16, :]
        else:
            flat[start : start + 16, :] = flat_in[b, 0:16, :]
        flat[start + 16 : start + count, :] = flat_in[b, 16:count, :]
    for name, ref in zip(MATS, outs):
        to_matrix(name, flat, MATS[name][2], ref)
    outs[5][...] = flat[VEC_AT : VEC_AT + 32, :]


SLOTS = ((0, 1, 2, 3), (1, 0, 3, 2), (2, 2, 0, 1), (3, 3, 1, 0))


def place_pieces(share, z_of, y, x, halves, flat):
    half = halves[0].shape[0]
    for which in range(2):
        for dy in range(2):
            for dx in range(2):
                piece = halves[4 * which + 2 * dy + dx]
                b = 4 * z_of + 2 * lax.rem(y + dy, 2) + lax.rem(x + dx, 2)
                row = pl.multiple_of(16 * ((share * b) // TILE), 16)
                if which == 0:
                    flat[pl.ds(row, 16), :] += piece[0:16, :]
                    flat[pl.ds(row + 16, half - 16), :] = piece[16:half, :]
                else:
                    kept = 16 * (share // TILE) - half
                    flat[pl.ds(row + half, kept), :] = piece[0:kept, :]
                    flat[pl.ds(row + half + kept, half - kept), :] += piece[kept:half, :]


def clear_edges(share, pieces, flat):
    for b in pieces:
        row = 16 * (share * b // TILE)
        last = row + 16 * (share // TILE)
        flat[row : row + 16, :] = jnp.zeros((16, 128), BF)
        flat[last : last + 32, :] = jnp.zeros((32, 128), BF)


def slot_copies(refs, kept, sems):
    a, ax, ay, b, by, bx = refs
    order = (a, ax, ay.at[0], ay.at[1], b, bx.at[0], by, bx.at[1])
    return [pltpu.make_async_copy(ref, kept.at[i], sems.at[i]) for i, ref in enumerate(order)]


def place_kernel(share, place_ref, *refs):
    slots, outs, refs = [refs[6 * i : 6 * i + 6] for i in range(4)], refs[24:30], refs[30:]
    mats, (vec_s, kept, flat, sems, out_sems) = refs[:5], refs[5:]
    sent, emit = emitter(out_sems)
    y, x = place_ref[1], place_ref[2]
    made = [slot_copies(slot, kept.at[i], sems.at[i]) for i, slot in enumerate(slots)]
    for some in made:
        for one in some:
            one.start()
    clear_edges(share, range(16), flat)
    for i, some in enumerate(made):
        z_of = place_ref[3 + i]
        for one in some:
            one.wait()
        place_pieces(share, z_of, y, x, [kept.at[i, j] for j in range(8)], flat)
    for name, mat, out in zip(MATS, mats, outs):
        to_matrix(name, flat, MATS[name][2], mat)
        emit(mat, out)
    vec_s[...] = flat[VEC_AT : VEC_AT + 32, :]
    emit(vec_s, outs[5])
    for one in sent:
        one.wait()


def self_fwd_kernel(causal_ref, x_ref, wqkv, fq, fk, qkv_ref, ctx_ref, lse_ref, lse_s, tri_s):
    qkv_ref[...] = dot_nn(x_ref[...], wqkv[...]).astype(BF)
    attend_fwd(
        causal_ref[0], qkv_ref, 0, qkv_ref, D, qkv_ref, 2 * D, fq[...], fk[...], ctx_ref, lse_ref, lse_s, tri_s
    )


def emitter(sems):
    sent = []

    def emit(source, target):
        sent.append(pltpu.make_async_copy(source, target, sems.at[len(sent)]))
        sent[-1].start()

    return sent, emit


def enc_ffn_kernel(
    loop, x_ref, ctx_ref, vec, w_out, w_up_any, w_down_any, w_cross_any,
    mem_ref, kv_ref, act_any, slope_any, r1_any, r2_any,
    hid_s, total_s, act_s, slope_s, r1_s, r2_s, w_up, w_down, w_cross, in_sems, out_sems,
):
    made = copies((w_up_any, w_down_any, w_cross_any), (w_up, w_down, w_cross), in_sems)
    sent, emit = emitter(out_sems)
    r1 = x_ref[...].astype(F32) + dot_nn(ctx_ref[...], w_out[...])
    r1_s[...] = r1
    emit(r1_s, r1_any)
    hat, _ = ln_parts(r1)
    y1 = hat * vec[0:1, :] + vec[1:2, :]
    hid_s[...] = y1.astype(BF)
    r2_s[...] = y1
    made[0].wait()
    made[1].wait()
    r2 = r2_s[...] + ffn_fwd(hid_s, w_up, w_down, act_s, slope_s, total_s, loop)
    emit(act_s, act_any)
    emit(slope_s, slope_any)
    r2_s[...] = r2
    emit(r2_s, r2_any)
    hat, _ = ln_parts(r2)
    mem = (hat * vec[2:3, :] + vec[3:4, :]).astype(BF)
    mem_ref[:, :D] = mem
    mem_ref[:, D:] = mem
    made[2].wait()
    kv_ref[...] = dot_nn(mem, w_cross[...]).astype(BF)
    for one in sent:
        one.wait()


def dec_kernel(
    row, x_ref, ctx1_ref, kv_ref, go_any, vec, w_cross, w_out, w_up_any, w_down_any, fq, fk,
    out_any, gkv_ref, dr1_ref, dctx1_ref, act_any, dz_any, hid_any, br_any, left_any, right_ref, gvec,
    cq_s, lse_s, wide_s, dctx_s, dcq_s, dqt_s, kt_s, slope_s, act_s, dz_s, hid_s, br_s, left_s, out_s,
    go_ref, w_up, w_down, keep_s, r1_s, in_sems, out_sems,
):
    up_copy, down_copy, go_copy = copies(
        (w_up_any, w_down_any, go_any.at[pl.ds(row * ROW, ROW)]), (w_up, w_down, go_ref), in_sems
    )
    sent, emit = emitter(out_sems)
    r1 = x_ref[...].astype(F32) + dot_nn(ctx1_ref[...], w_out[...])
    r1_s[...] = r1
    hat1, _ = ln_parts(r1)
    y1 = hat1 * vec[0:1, :] + vec[1:2, :]
    y1_b = y1.astype(BF)
    left_s[:, :D] = y1_b
    cq_s[...] = dot_nn(y1_b, w_cross[:, :D]).astype(BF)
    ctx_s = left_s.at[:, D:]
    attend_fwd(None, cq_s, 0, kv_ref, 0, kv_ref, D, fq[...], fk[...], ctx_s, lse_s, wide_s, None)
    emit(left_s, left_any)
    r2 = y1 + dot_nn(ctx_s[...], w_cross[:, D:])
    hat2, rstd2 = ln_parts(r2)
    y2 = hat2 * vec[2:3, :] + vec[3:4, :]
    hid_s[...] = y2.astype(BF)
    keep_s[...] = y2
    emit(hid_s, hid_any)
    up_copy.wait()
    down_copy.wait()
    r3 = keep_s[...] + ffn_fwd(hid_s, w_up, w_down, act_s, slope_s, None, False)
    emit(act_s, act_any)
    hat3, rstd3 = ln_parts(r3)
    out_s[...] = (hat3 * vec[4:5, :] + vec[5:6, :]).astype(BF)
    emit(out_s, out_any)

    go_copy.wait()
    dr3, gain3, shift3 = ln_back(go_ref[...].astype(F32), hat3, rstd3, vec[4:5, :])
    br_s[...] = dr3.astype(BF)
    emit(br_s, br_any)
    keep_s[...] = dr3
    dy2 = keep_s[...] + ffn_bwd(br_s, w_up, w_down, slope_s, dz_s, None, False)
    emit(dz_s, dz_any)
    dr2, gain2, shift2 = ln_back(dy2, hat2, rstd2, vec[2:3, :])
    dr2_b = dr2.astype(BF)
    right_ref[:, D:] = dr2_b
    dctx_s[...] = dot_nt(dr2_b, w_cross[:, D:]).astype(BF)
    attend_bwd(
        None, cq_s, 0, kv_ref, 0, kv_ref, D, fq[...], fk[...], lse_s, dctx_s,
        ((dcq_s, 0), (gkv_ref, 0), (gkv_ref, D)), dqt_s, kt_s, None,
    )
    dcq = dcq_s[...]
    right_ref[:, :D] = dcq
    self_head(dr2 + dot_nt(dcq, w_cross[:, :D]), r1_s, vec, w_out, dr1_ref, dctx1_ref, gvec)
    gvec[2:3, :] = gain2
    gvec[3:4, :] = shift2
    gvec[4:5, :] = gain3
    gvec[5:6, :] = shift3
    for one in sent:
        one.wait()


def enc_back_kernel(
    gkv_ref, r1_any, r2_ref, slope_any, vec, w_cross, w_out_any, w_up_any, w_down_any,
    dr1_ref, dctx1_ref, dz_any, hid_any, br_any, gvec,
    keep_s, total_s, r1_ref, slope_s, w_out, w_up, w_down, dz_s, hid_s, br_s, in_sems, out_sems,
):
    made = copies(
        (r1_any, slope_any, w_down_any, w_up_any, w_out_any), (r1_ref, slope_s, w_down, w_up, w_out), in_sems
    )
    sent, emit = emitter(out_sems)
    dmem = dot_nt(gkv_ref[...], w_cross[...])
    hat2, rstd2 = ln_parts(r2_ref[...])
    dr2, gain2, shift2 = ln_back(dmem, hat2, rstd2, vec[2:3, :])
    br_s[...] = dr2.astype(BF)
    emit(br_s, br_any)
    keep_s[...] = dr2
    made[0].wait()
    hat1, _ = ln_parts(r1_ref[...])
    hid_s[...] = (hat1 * vec[0:1, :] + vec[1:2, :]).astype(BF)
    emit(hid_s, hid_any)
    for one in made[1:4]:
        one.wait()
    dy1 = keep_s[...] + ffn_bwd(br_s, w_up, w_down, slope_s, dz_s, total_s, True)
    emit(dz_s, dz_any)
    made[4].wait()
    self_head(dy1, r1_ref, vec, w_out, dr1_ref, dctx1_ref, gvec)
    gvec[2:3, :] = gain2
    gvec[3:4, :] = shift2
    gvec[4:8, :] = jnp.zeros((4, D), F32)
    for one in sent:
        one.wait()


def row_fetcher(kinds, rows, dec_ref, refs):
    count = len(kinds) * rows
    buffers, sems = refs[-len(kinds) - 1 : -1], refs[-1]
    ins = refs[: -len(kinds) - 1]
    sources = [ins[i : i + count] for i in range(0, len(ins), count)]
    kept = dict(zip(kinds, buffers))

    def fetch(some, i):
        size = some[i].shape[0]
        target = kept[kinds[i // rows]].at[pl.ds((i % rows) * size, size)]
        return pltpu.make_async_copy(some[i], target, sems.at[i])

    def begin(some):
        for i in range(count):
            fetch(some, i).start()

    if len(sources) == 1:
        begin(sources[0])
    else:
        for which, some in enumerate(sources):
            pl.when(dec_ref[0] == which)(functools.partial(begin, some))

    def ready(*some):
        for kind in some:
            for r in range(rows):
                fetch(sources[0], kinds.index(kind) * rows + r).wait()

    return kept, ready


def fetched(kinds, sources):
    ins = [row[kind] for some in sources for kind in kinds for row in some]
    rows = len(sources[0])
    kept = []
    for kind in kinds:
        size, cols = sources[0][0][kind].shape
        kept.append(pltpu.VMEM((rows * size, cols), sources[0][0][kind].dtype))
    return ins, kept + [pltpu.SemaphoreType.DMA((len(kinds) * rows,))]


FFN_KINDS = ("hid", "dz", "act", "branch")
ATTEND_KINDS = ("ctx", "dr1", "left", "right")


def ffn_grads_kernel(rows, dec_ref, *refs):
    count = 2 * len(FFN_KINDS) * rows
    ins, flat, (hid_t, g_up, g_down), rest = refs[:count], refs[count], refs[count + 1 : count + 4], refs[count + 4 :]
    kept, ready = row_fetcher(FFN_KINDS, rows, dec_ref, (*ins, *rest))
    ready("hid", "dz")
    hid_t[...] = kept["hid"][...].T
    for c in range(FF // CHUNK):
        cols = slice(c * CHUNK, (c + 1) * CHUNK)
        g_up[:, cols] = dot_nn(hid_t[...], kept["dz"][:, cols])
    to_flat("up", g_up, flat, 0)
    ready("act", "branch")
    for c in range(FF // D):
        part = slice(c * D, (c + 1) * D)
        g_down[part, :] = dot_tn(kept["act"][:, part], kept["branch"][...])
    to_flat("down", g_down, flat, MATS["down"][2] - MATS["up"][2])


def attend_grads_kernel(rows, dec_ref, *refs):
    count = 2 * len(ATTEND_KINDS) * rows
    ins, flat, (g_cross, g_out), rest = refs[:count], refs[count], refs[count + 1 : count + 3], refs[count + 3 :]
    kept, ready = row_fetcher(ATTEND_KINDS, rows, dec_ref, (*ins, *rest))
    ready("ctx", "dr1")
    g_out[...] = dot_tn(kept["ctx"][...], kept["dr1"][...].astype(BF))
    to_flat("out", g_out, flat, 0)
    ready("left", "right")
    for at in (0, D):
        g_cross[:, at : at + D] = dot_tn(kept["left"][:, at : at + D], kept["right"][:, at : at + D])
    to_flat("cross", g_cross, flat, MATS["cross"][2] - REST_AT)


BACK_KINDS = ("qkv", "lse", "dctx", "dr1")


def self_back_kernel(ins, causal_ref, wqkv, fq, fk, *refs):
    (dx_ref, dqkv, dqt_s, kt_s, tri_s), rest = refs[ins : ins + 5], refs[ins + 5 :]
    kept, ready = row_fetcher(BACK_KINDS, 1, causal_ref, (*refs[:ins], *rest))
    ready("qkv", "lse", "dctx")
    qkv = kept["qkv"]
    attend_bwd(
        causal_ref[0], qkv, 0, qkv, D, qkv, 2 * D, fq[...], fk[...], kept["lse"], kept["dctx"],
        ((dqkv, 0), (dqkv, D), (dqkv, 2 * D)), dqt_s, kt_s, tri_s,
    )
    ready("dr1")
    dx_ref[...] = (kept["dr1"][...] + dot_nt(dqkv[...], wqkv[...])).astype(BF)


def qkv_kernel(ins, rows, dec_ref, x_ref, *refs):
    (fl_qkv, x_t, g_qkv), rest = refs[ins : ins + 3], refs[ins + 3 :]
    kept, ready = row_fetcher(("dqkv",), rows, dec_ref, (*refs[:ins], *rest))
    x_t[...] = x_ref[...].T
    ready("dqkv")
    for c in range(3):
        cols = slice(c * D, (c + 1) * D)
        g_qkv[:, cols] = dot_nn(x_t[...], kept["dqkv"][:, cols])
    to_flat("qkv", g_qkv, fl_qkv, 0)


def pack_kernel(share, planes, base, place_ref, *refs):
    parts, outs, flat = refs[:-5], refs[-5:-1], refs[-1]
    send_a, keep_a, send_b, keep_b = outs
    at = 0
    for part in parts:
        flat[at : at + part.shape[0], :] = part[...]
        at += part.shape[0]
    y, x = place_ref[0], place_ref[1]
    half = send_a.shape[2]
    for i, z in enumerate(planes):
        for j in range(2):
            for ref, y_to, x_to, skip in (
                (send_a, 1 - y, j, 0), (keep_a, y, j, 0), (send_b, j, 1 - x, half), (keep_b, j, x, half),
            ):
                b = 4 * z + 2 * y_to + x_to
                start = pl.multiple_of(16 * ((share * b) // TILE) - base + skip, 16)
                ref[i, j] = flat[pl.ds(start, half), :]


def kernel_call(body, micros=1, **options):
    cost = pl.CostEstimate(flops=micros * 10**9, bytes_accessed=0, transcendentals=0)
    call = pl.pallas_call(body, cost_estimate=cost, **options)
    return lambda *operands: tuple(call(*operands))


IN_VMEM = pl.BlockSpec(memory_space=pltpu.VMEM)
IN_SMEM = pl.BlockSpec(memory_space=pltpu.SMEM)
ANYWHERE = pl.BlockSpec(memory_space=pl.ANY)


def at_row(row, cols, rows=ROW):
    return pl.BlockSpec((rows, cols), lambda i: (row, 0), pipeline_mode=pl.Buffered(1))


def shifted(shift, params, share, rows):
    return kernel_call(
        functools.partial(shift_kernel, share),
        in_specs=[IN_SMEM, IN_VMEM],
        out_specs=[IN_VMEM],
        out_shape=[shape_of((rows, 128), BF)],
        scratch_shapes=[pltpu.VMEM((rows + 32, 128), F32)],
        compiler_params=params_of(8),
    )(shift, params)[0]


def unshifted(shift, sums, share):
    return kernel_call(
        functools.partial(unshift_kernel, share),
        in_specs=[IN_SMEM, IN_VMEM],
        out_specs=[IN_VMEM] * 2,
        out_shape=[shape_of((1, share), F32), shape_of((8, 128), F32)],
        compiler_params=params_of(8),
    )(shift, sums)


def adam(clip, grad, first, second, share):
    return kernel_call(
        functools.partial(adam_kernel, share),
        in_specs=[IN_SMEM] + [IN_VMEM] * 3,
        out_specs=[IN_VMEM] * 3,
        out_shape=[shape_of((1, share), F32)] * 3,
        compiler_params=params_of(16),
    )(clip, grad, first, second)


def split_weights(pieces, n, share):
    shapes = [(rows, cols) for rows, cols, _, _ in MATS.values()] + [(32, 128)]
    rows = 16 * (-(-share * n // TILE) + 2)
    got = kernel_call(
        functools.partial(weights_kernel, n, share),
        in_specs=[IN_VMEM],
        out_specs=[IN_VMEM] * 6,
        out_shape=[shape_of(s, BF) for s in shapes],
        scratch_shapes=[pltpu.VMEM((rows, 128), BF)],
        compiler_params=params_of(60),
    )(pieces)
    return dict(zip((*MATS, "vec"), got))


def placed_weights(place, slots, share, rows):
    vm = pltpu.VMEM
    shapes = [(rows, cols) for rows, cols, _, _ in MATS.values()] + [(32, 128)]
    got = kernel_call(
        functools.partial(place_kernel, share),
        micros=9,
        in_specs=[IN_SMEM] + [ANYWHERE] * 24,
        out_specs=[ANYWHERE] * 6,
        out_shape=[shape_of(s, BF) for s in shapes],
        scratch_shapes=[vm(s, BF) for s in shapes]
        + [vm((4, 8, rows // 2, 128), BF), vm((piece_row(share, 15) + rows + 16, 128), BF)]
        + [pltpu.SemaphoreType.DMA((4, 8)), pltpu.SemaphoreType.DMA((6,))],
        compiler_params=params_of(60),
    )(place, *(one for slot in slots for one in slot))
    return dict(zip((*MATS, "vec"), got))


def row_shapes(*cols):
    return [shape_of((ROW, abs(c)), F32 if c < 0 else BF) for c in cols]


def self_fwd(causal, row, x, w_qkv, fq, fk):
    names = ("qkv", "ctx", "lse")
    vm = pltpu.VMEM
    got = kernel_call(
        self_fwd_kernel,
        micros=5,
        grid=(1,),
        in_specs=[IN_SMEM, at_row(row, D), whole_spec((D, 3 * D)), at_row(row, 128), at_row(row, 128)],
        out_specs=[at_row(0, 3 * D), at_row(0, D), at_row(0, ROW, HEADS)],
        out_shape=row_shapes(3 * D, D) + [shape_of((HEADS, ROW), F32)],
        scratch_shapes=[vm((ROW, 128), F32), vm((ROW, ROW), F32)],
        compiler_params=params_of(24),
    )(causal, x, w_qkv, fq, fk)
    return dict(zip(names, got))


def enc_ffn(row, x, fwd, w, vec):
    names = ("mem", "kv", "act", "slope", "r1", "r2")
    vm = pltpu.VMEM
    got = kernel_call(
        functools.partial(enc_ffn_kernel, row > 0),
        micros=8,
        grid=(1,),
        in_specs=[at_row(row, D), at_row(0, D), whole_spec((6, D)), whole_spec((D, D))] + [ANYWHERE] * 3,
        out_specs=[at_row(0, 2 * D), at_row(0, 2 * D)] + [ANYWHERE] * 4,
        out_shape=row_shapes(2 * D, 2 * D, FF, FF, -D, -D),
        scratch_shapes=[
            vm((ROW, D), BF), vm((ROW, D), F32), vm((ROW, FF), BF), vm((ROW, FF), BF), vm((ROW, D), F32), vm((ROW, D), F32),
            vm((D, FF), BF), vm((FF, D), BF), vm((D, 2 * D), BF), pltpu.SemaphoreType.DMA((3,)), pltpu.SemaphoreType.DMA((4,)),
        ],
        compiler_params=params_of(32),
    )(x, fwd["ctx"], vec, w["out"], w["up"], w["down"], w["cross"])
    return dict(zip(names, got))


def dec_call(row, x, fwd, kv, go, w, vec, fq, fk):
    vm = pltpu.VMEM
    names = ("out", "gkv", "dr1", "dctx", "act", "dz", "hid", "branch", "left", "right", "gvec")
    got = kernel_call(
        functools.partial(dec_kernel, row),
        micros=23,
        grid=(1,),
        in_specs=[
            at_row(row, D), at_row(0, D), at_row(0, 2 * D), ANYWHERE, whole_spec((6, D)), whole_spec((D, 2 * D)),
            whole_spec((D, D)), ANYWHERE, ANYWHERE, at_row(row, 128), at_row(row, 128),
        ],
        out_specs=[ANYWHERE, at_row(0, 2 * D), at_row(0, D), at_row(0, D)] + [ANYWHERE] * 5
        + [at_row(0, 2 * D), whole_spec((8, D))],
        out_shape=row_shapes(D, 2 * D, -D, D, FF, FF, D, D, 2 * D, 2 * D) + [shape_of((8, D), F32)],
        scratch_shapes=[
            vm((ROW, D), BF), vm((HEADS, ROW), F32), vm((ROW, 128), F32), vm((ROW, D), BF), vm((ROW, D), BF),
            vm((D, ROW), F32), vm((D, ROW), BF), vm((ROW, FF), BF), vm((ROW, FF), BF), vm((ROW, FF), BF), vm((ROW, D), BF),
            vm((ROW, D), BF), vm((ROW, 2 * D), BF), vm((ROW, D), BF), vm((ROW, D), BF), vm((D, FF), BF),
            vm((FF, D), BF), vm((ROW, D), F32), vm((ROW, D), F32), pltpu.SemaphoreType.DMA((3,)),
            pltpu.SemaphoreType.DMA((6,)),
        ],
        compiler_params=params_of(60),
    )(x, fwd["ctx"], kv, go, vec, w["cross"], w["out"], w["up"], w["down"], fq, fk)
    return dict(zip(names, got))


def enc_back(gkv, fwd, w, vec):
    names = ("dr1", "dctx", "dz", "hid", "branch", "gvec")
    vm = pltpu.VMEM
    got = kernel_call(
        enc_back_kernel,
        micros=8,
        grid=(1,),
        in_specs=[
            at_row(0, 2 * D), ANYWHERE, at_row(0, D), ANYWHERE, whole_spec((6, D)), whole_spec((D, 2 * D)),
            ANYWHERE, ANYWHERE, ANYWHERE,
        ],
        out_specs=[at_row(0, D), at_row(0, D)] + [ANYWHERE] * 3 + [whole_spec((8, D))],
        out_shape=row_shapes(-D, D, FF, D, D) + [shape_of((8, D), F32)],
        scratch_shapes=[
            vm((ROW, D), F32), vm((ROW, D), F32), vm((ROW, D), F32), vm((ROW, FF), BF), vm((D, D), BF), vm((D, FF), BF),
            vm((FF, D), BF), vm((ROW, FF), BF), vm((ROW, D), BF), vm((ROW, D), BF), pltpu.SemaphoreType.DMA((5,)),
            pltpu.SemaphoreType.DMA((3,)),
        ],
        compiler_params=params_of(32),
    )(gkv, fwd["r1"], fwd["r2"], fwd["slope"], vec, w["cross"], w["out"], w["up"], w["down"])
    return dict(zip(names, got))


def row_grads(body, kinds, flat_rows, scratch, is_dec, sources):
    ins, kept = fetched(kinds, sources)
    return kernel_call(
        functools.partial(body, len(sources[0])),
        micros=1,
        in_specs=[IN_SMEM] + [ANYWHERE] * len(ins),
        out_specs=[IN_VMEM],
        out_shape=[shape_of((flat_rows, 128), BF)],
        scratch_shapes=scratch + kept,
        compiler_params=params_of(48),
    )(is_dec, *ins)[0]


def self_back(causal, row, sources, w, fq, fk):
    vm = pltpu.VMEM
    shapes = row_shapes(D, 3 * D)
    ins, kept = fetched(BACK_KINDS, [[one] for one in sources])
    got = kernel_call(
        functools.partial(self_back_kernel, len(ins)),
        micros=1,
        grid=(1,),
        in_specs=[IN_SMEM, whole_spec((D, 3 * D)), at_row(row, 128), at_row(row, 128)] + [ANYWHERE] * len(ins),
        out_specs=[whole_spec(s.shape) for s in shapes],
        out_shape=shapes,
        scratch_shapes=[vm((D, ROW), F32), vm((D, ROW), BF), vm((ROW, ROW), F32)] + kept,
        compiler_params=params_of(28),
    )(causal, w["qkv"], fq, fk, *ins)
    return dict(zip(("dx", "dqkv"), got))


def qkv_grad(is_dec, x, sources):
    vm = pltpu.VMEM
    t, rows = x.shape[0], len(sources[0])
    ins, kept = fetched(("dqkv",), sources)
    return kernel_call(
        functools.partial(qkv_kernel, len(ins), rows),
        micros=1,
        in_specs=[IN_SMEM, IN_VMEM] + [ANYWHERE] * len(ins),
        out_specs=[IN_VMEM],
        out_shape=[shape_of((REST_AT, 128), BF)],
        scratch_shapes=[vm((D, t), BF), vm((D, 3 * D), F32)] + kept,
        compiler_params=params_of(28),
    )(is_dec, x, *ins)[0]


def pack(place, parts, planes, base, share, rows):
    half = rows // 2
    parts = [p if isinstance(p, tuple) else (p, p.shape[0]) for p in parts]
    total = sum(count for _, count in parts)
    need = piece_row(share, 4 * planes[-1] + 3) - base + rows
    return kernel_call(
        functools.partial(pack_kernel, share, planes, base),
        micros=1,
        grid=(1,),
        in_specs=[IN_SMEM] + [pl.BlockSpec((count, 128), lambda i: (0, 0), pipeline_mode=pl.Buffered(1)) for _, count in parts],
        out_specs=[whole_spec((len(planes), 2, half, 128))] * 4,
        out_shape=[shape_of((len(planes), 2, half, 128), BF)] * 4,
        scratch_shapes=[pltpu.VMEM((max(total, need), 128), BF)],
        compiler_params=params_of(32),
    )(place, *(p for p, _ in parts))


def mask_features(segments, live):
    t = segments.shape[0]
    lane = (jnp.arange(128, dtype=jnp.int32) % HD)[None, :]
    pair = lane // 2
    odd = lane % 2 == 1
    is_seg = pair < SEG_BITS
    is_pos = (pair >= SEG_BITS) & (pair < SEG_BITS + POS_BITS)
    place = (jnp.arange(t, dtype=jnp.int32) % ROW)[:, None]
    bit = jnp.where(
        is_seg,
        (segments[:, None] >> jnp.minimum(pair, SEG_BITS)) & 1,
        (place >> jnp.clip(pair - SEG_BITS, 0, POS_BITS)) & 1,
    )
    query = jnp.where(odd, 1 - bit, bit) * (is_seg | is_pos)
    key = jnp.where(odd, bit, 1 - bit)
    keys = [jnp.where(is_seg | (is_pos & (live[i][:, None] != 1)), key.astype(F32) * -BIG, 0.0).astype(BF) for i in range(2)]
    return query.astype(BF), keys[0], keys[1]


def ghosts(shapes):
    if not shapes:
        return ()
    return kernel_call(lambda *refs: None, out_specs=[ANYWHERE] * len(shapes), out_shape=list(shapes))()


def either(is_decoder, dec, enc):
    thunks = (enc, dec)
    made = [jax.eval_shape(t) for t in thunks]
    slots, where = [], []
    for tree in made:
        free = list(range(len(slots)))
        taken = []
        for leaf in jax.tree.leaves(tree):
            key = (leaf.shape, leaf.dtype)
            match = next((i for i in free if slots[i] == key), None)
            if match is None:
                slots.append(key)
                match = len(slots) - 1
            else:
                free.remove(match)
            taken.append(match)
        where.append(taken)

    def branch(which):
        def run():
            leaves = jax.tree.leaves(thunks[which]())
            filled = dict(zip(where[which], leaves))
            missing = [i for i in range(len(slots)) if i not in filled]
            filled.update(zip(missing, ghosts([shape_of(*slots[i]) for i in missing])))
            return tuple(filled[i] for i in range(len(slots)))

        return run

    got = lax.cond(is_decoder, branch(1), branch(0))
    back = [jax.tree.unflatten(jax.tree.structure(made[i]), [got[s] for s in where[i]]) for i in range(2)]
    return back[1], back[0]


def plane_permute(value, step):
    return lax.ppermute(value, "batch", [(i, i ^ step) for i in range(16)])


def line_permute(value, step, sources):
    pairs = [(4 * z + k, 4 * (z + step) + k) for z in sources for k in range(4)]
    return lax.ppermute(value, "batch", pairs)


def over_all(value):
    axes = ("section", "batch")
    places = [(core, i) for core in range(2) for i in range(16)]

    def flat(core, i):
        return core * 16 + i

    total = value
    for core_step in range(2):
        for step in range(4):
            if core_step or step:
                pairs = [(flat(c, i), flat(c ^ core_step, i ^ step)) for c, i in places]
                total = total + lax.ppermute(value, axes, pairs)
    value = total
    for step in (4, 8, 12):
        total = total + plane_permute(value, step)
    return total


def tied(*values):
    return lax.optimization_barrier(values)


def gathered(own, z):
    half = own.shape[0] // 2

    def first(block):
        a, b = block[:half], block[half:]
        return a, b, plane_permute(a, 1), plane_permute(b, 2)

    def second(parts):
        a, b, ax, by = parts
        return (a, ax, plane_permute(jnp.stack([a, ax]), 2), b, by, plane_permute(jnp.stack([b, by]), 1))

    up, down = line_permute(own, 1, (0, 1, 2)), line_permute(own, -1, (1, 2, 3))
    begun = first(own)
    zero = second(begun)
    up, down, _ = tied(up, down, begun)
    up_two, down_two = line_permute(up, 1, (1, 2)), line_permute(down, -1, (1, 2))
    begun = first(jnp.where((z == 0) | (z == 2), down, up))
    zero, begun = tied(zero, begun)
    one = second(begun)
    up_two, down_two, _ = tied(up_two, down_two, zero)
    up_three, down_three = line_permute(up_two, 1, (2,)), line_permute(down_two, -1, (1,))
    begun = first(jnp.where(z == 0, down_two, jnp.where(z == 1, down, up_two)))
    one, begun = tied(one, begun)
    two = second(begun)
    up_three, down_three, _ = tied(up_three, down_three, one)
    begun = first(jnp.where(z == 0, down_three, jnp.where(z == 1, down_two, jnp.where(z == 2, up, up_three))))
    two, begun = tied(two, begun)
    three = second(begun)
    return zero, one, two, three


def added(*values):
    total = values[0].astype(F32)
    for value in values[1:]:
        total = total + value.astype(F32)
    return total


def plane_start(packed):
    send_a, keep_a, send_b, keep_b = packed
    return keep_a, plane_permute(send_a, 2), keep_b, plane_permute(send_b, 1)


def plane_end(begun, y, x):
    keep_a, got_a, keep_b, got_b = begun

    def part(keep, got, index):
        return added(lax.dynamic_index_in_dim(keep, index, 1, False), lax.dynamic_index_in_dim(got, index, 1, False))

    far_a, far_b = part(keep_a, got_a, 1 - x).astype(BF), part(keep_b, got_b, 1 - y).astype(BF)
    in_a, in_b = plane_permute(far_a, 1), plane_permute(far_b, 2)
    sum_a, sum_b = added(part(keep_a, got_a, x), in_a), added(part(keep_b, got_b, y), in_b)
    return jnp.stack([sum_a.astype(BF), sum_b.astype(BF)], axis=1)


def line_sums(early, mid, late, z):
    one, two, three = mid[0], early[0], early[1]

    def low(value):
        return value.astype(BF)

    up = line_permute(three, 1, (0,))
    down = line_permute(one, -1, (3,))
    up = line_permute(low(jnp.where(z == 0, two.astype(F32), added(three, up))), 1, (0, 1))
    down = line_permute(low(jnp.where(z == 3, two.astype(F32), added(one, down))), -1, (2, 3))
    third = jnp.where(z == 0, one.astype(F32), added(jnp.where(z == 1, two, three), up))
    up = line_permute(low(third), 1, (0, 1, 2))
    zero = late[0]
    near = line_permute(zero, -1, (1, 3))
    pair = added(zero, near)
    far = line_permute(low(pair), -2, (2,))
    own = jnp.where(z == 1, one, jnp.where(z == 2, two, three))
    return jnp.where(z == 0, added(pair, far), added(own, up, down))


def shards(params, first_moment, second_moment, inputs, segments, live_mask, out_grad):
    is_decoder = lax.axis_index("section") == 1
    me = lax.axis_index("batch")
    n = lax.axis_size("batch")
    share = params.shape[1]
    rows = 16 * (share // TILE + 2)
    shift = lax.rem(me * (share % TILE), TILE)[None]
    x = inputs[0]
    t = x.shape[0]
    count = t // ROW

    y, x_at, z = lax.rem(me // 2, 2), lax.rem(me, 2), me // 4
    custom = n == 16
    flag = is_decoder.astype(jnp.int32)[None]
    own = shifted(shift, params, share, rows)
    fq, fk_src, fk_tgt = mask_features(segments, live_mask)
    fk_self = jnp.where(is_decoder, fk_tgt, fk_src)
    if custom:
        spot = jnp.concatenate([jnp.stack([z, y, x_at]), jnp.asarray(SLOTS, jnp.int32)[:, z]])
        slots, fq, fk_src, fk_self = tied(gathered(own, z), fq, fk_src, fk_self)
        w = placed_weights(spot, slots, share, rows)
    else:
        pieces = lax.all_gather(own, "batch", axis=0, tiled=False)
        pieces, fq, fk_src, fk_self = tied(pieces, fq, fk_src, fk_self)
        w = split_weights(pieces, n, share)
    def forward(row):
        return self_fwd(flag, row, x, w["qkv"], fq, fk_self)

    first_fwd = forward(0)
    vec = w["vec"][:24].astype(F32).reshape(6, D)

    def nothing():
        return {}

    def swapped(value):
        return lax.ppermute(value, "section", [(0, 1), (1, 0)])

    fwd, first = either(
        is_decoder, lambda: [forward(r) for r in range(1, count)], lambda: enc_ffn(0, x, first_fwd, w, vec)
    )
    dec_fwd, enc_fwd = [first_fwd, *fwd], [first_fwd]
    kept, dec_rows, enc_rows, back, enc_self = [first], [], [], [], []
    kv_in = swapped(first["kv"])
    for row in range(count):

        def dec_make():
            got = dec_call(row, x, dec_fwd[row], kv_in, out_grad, w, vec, fq, fk_src)
            return got.pop("gkv"), got

        def enc_make():
            fwd, ahead, done, far = [], [], [], []
            if row + 1 < count:
                fwd = [forward(r) for r in range(1, count)] if row == 0 else []
                ahead = [enc_ffn(row + 1, x, fwd[0] if row == 0 else enc_fwd[row + 1], w, vec)]
            if row:
                done = [enc_back(back[row - 1], kept[row - 1], w, vec)]
            if row and row == count - 1:
                far = [self_back(flag, 0, [{**enc_rows[0], **enc_fwd[0]} if enc_rows else {**done[0], **enc_fwd[0]}], w, fq, fk_self)]
            return [k.pop("kv") for k in ahead], (fwd, ahead, done, far)

        (sent, got), (_, (fwd, ahead, done, far)) = either(is_decoder, dec_make, enc_make)
        dec_rows.append(got)
        enc_fwd += fwd
        enc_rows += done
        kept += ahead
        enc_self += far
        kv_in = swapped(sent)
        back.append(kv_in)

    last = count - 1
    dec_self, done = either(
        is_decoder,
        lambda: [self_back(flag, 0, [{**dec_rows[0], **dec_fwd[0]}], w, fq, fk_self)] if last else [],
        lambda: enc_back(back[last], kept[last], w, vec),
    )
    enc_rows.append(done)
    dec_all = [{**made, **fwd} for made, fwd in zip(dec_rows, dec_fwd)]
    enc_all = [
        {**made, **fwd, "act": k["act"], "left": k["mem"], "right": g}
        for made, fwd, k, g in zip(enc_rows, enc_fwd, kept, back)
    ]
    both = [enc_all, dec_all]

    gvec = jnp.where(is_decoder, sum(r["gvec"] for r in dec_rows), sum(r["gvec"] for r in enc_rows))
    fl_vec = jnp.pad(gvec[:6].reshape(24, 128).astype(BF), ((0, 24), (0, 0)))

    vm = pltpu.VMEM
    flat_ffn = row_grads(
        ffn_grads_kernel, FFN_KINDS, VEC_AT - MATS["up"][2],
        [vm((D, t), BF), vm((D, FF), F32), vm((FF, D), F32)], flag, both,
    )
    place = jnp.stack([y, x_at])
    if custom:
        packed = pack(place, [flat_ffn, fl_vec], (2, 3), MATS["up"][2], share, rows)
        early = plane_start(packed)
        flag, _ = tied(flag, packed[0])
    flat_attend = row_grads(
        attend_grads_kernel, ATTEND_KINDS, MATS["up"][2] - REST_AT,
        [vm((D, 2 * D), F32), vm((D, D), F32)], flag, both,
    )
    if custom:
        need = piece_row(share, 7) + rows - MATS["up"][2]
        packed = pack(place, [flat_attend, (flat_ffn, need)], (1,), REST_AT, share, rows)
        mid = plane_start(packed)
        flag, _ = tied(flag, packed[0])

    common = []
    for row in range(len(dec_self), count):
        common.append(self_back(flag, row, [enc_all[row], dec_all[row]], w, fq, fk_self))
    if custom:
        early, common[-1] = tied(early, common[-1])
        early = plane_end(early, y, x_at)
    fl_qkv = qkv_grad(flag, x, [[*enc_self, *common], [*dec_self, *common]])
    dx = jnp.concatenate(
        [jnp.where(is_decoder, d["dx"], e["dx"]) for d, e in zip(dec_self, enc_self)] + [r["dx"] for r in common], axis=0
    )
    layer_out = jnp.where(
        is_decoder,
        jnp.concatenate([r["out"] for r in dec_rows], axis=0),
        jnp.concatenate([k["mem"][:, :D] for k in kept], axis=0),
    )

    if custom:
        mid, fl_qkv = tied(mid, fl_qkv)
        mid = plane_end(mid, y, x_at)
        need = piece_row(share, 3) + rows
        late = plane_start(pack(place, [fl_qkv, (flat_attend, need - REST_AT)], (0,), 0, share, rows))
        late = plane_end(late, y, x_at)
        mine = line_sums(early, mid, late, z).reshape(rows, 128)
    else:
        spare = jnp.zeros((piece_row(share, n - 1) + rows - FLAT_ROWS, 128), BF)
        flat = jnp.concatenate([fl_qkv, flat_attend, flat_ffn, fl_vec[:24], spare], axis=0)
        stacked = jnp.concatenate([flat[piece_row(share, b) :][:rows] for b in range(n)], axis=0)
        mine = lax.psum_scatter(stacked, "batch", scatter_dimension=0, tiled=True).astype(F32)
    grad_share, squares = unshifted(shift, jnp.pad(mine, ((0, 8), (0, 0))), share)

    square_sum = jnp.sum(squares)
    if custom:
        square_sum = over_all(square_sum.reshape(1, 1))[0, 0]
    else:
        square_sum = lax.psum(square_sum, ("section", "batch"))
    grad_norm = jnp.sqrt(square_sum)
    clip_factor = MAXNORM / jnp.maximum(grad_norm, MAXNORM)
    param_step, new_first, new_second = adam(clip_factor[None], grad_share, first_moment, second_moment, share)
    return (param_step, new_first, new_second, grad_share, layer_out[None], dx[None], grad_norm)


def solution(mesh):
    in_specs = (
        P("section", "batch"),
        P("section", "batch"),
        P("section", "batch"),
        P("section", "batch", None),
        P("batch"),
        P(None, "batch"),
        P("batch", None),
    )
    out_specs = (
        P("section", "batch"),
        P("section", "batch"),
        P("section", "batch"),
        P("section", "batch"),
        P("section", "batch", None),
        P("section", "batch", None),
        P(),
    )
    return jax.shard_map(shards, mesh=mesh, in_specs=in_specs, out_specs=out_specs, check_vma=False)
```

```python
import functools

import jax
import jax.numpy as jnp
from jax import lax
from jax.experimental import pallas as pl
from jax.experimental.pallas import tpu as pltpu
from jax.sharding import PartitionSpec as P

D = 512
FF = 2048
HEADS = 8
HD = 64
ROW = 512
STEP = 1000
WARMUP = 4000

BIG = 1e30
LN_EPS = 1e-05
BETA_ONE = 0.9
BETA_TWO = 0.98
ADAM_EPS = 1e-09
MAXNORM = 0.1

F32 = jnp.float32
BF = jnp.bfloat16
TILE = 16 * 128
CHUNK = 512
PART = 64
SEG_BITS = 12
POS_BITS = 9
DEC_FIRST = True
LOOP = False

MATS = {}
_at = 0
for _name, _rows, _cols in (("qkv", D, 3 * D), ("out", D, D), ("cross", D, 2 * D), ("up", D, FF), ("down", FF, D)):
    _width = _cols // 128
    MATS[_name] = (_rows, _cols, _at, {12: 16, 4: 64, 8: 32, 16: 16}[_width])
    _at += _rows * _width
VEC_AT = _at
FLAT_ROWS = _at + 24
REST_AT = MATS["out"][2]


def dot_nn(lhs, rhs):
    return jnp.dot(lhs, rhs, preferred_element_type=F32)


def dot_nt(lhs, rhs):
    return lax.dot_general(lhs, rhs, (((1,), (1,)), ((), ())), preferred_element_type=F32)


def dot_tn(lhs, rhs):
    return lax.dot_general(lhs, rhs, (((0,), (0,)), ((), ())), preferred_element_type=F32)


def params_of(mib):
    return pltpu.CompilerParams(vmem_limit_bytes=mib * 2**20)


def row_spec(rows, cols):
    return pl.BlockSpec((rows, cols), lambda i: (i, 0))


def whole_spec(shape):
    return pl.BlockSpec(shape, lambda i: (0,) * len(shape), pipeline_mode=pl.Buffered(1))


def shape_of(shape, dtype):
    return jax.ShapeDtypeStruct(shape, dtype)


def ln_parts(resid):
    center = resid - jnp.mean(resid, axis=-1, keepdims=True)
    rstd = lax.rsqrt(jnp.mean(center * center, axis=-1, keepdims=True) + LN_EPS)
    return center * rstd, rstd


def ln_back(grad, resid, gain):
    hat, rstd = ln_parts(resid)
    scaled = grad * gain
    first = jnp.mean(scaled, axis=-1, keepdims=True)
    second = jnp.mean(scaled * hat, axis=-1, keepdims=True)
    grad_resid = rstd * (scaled - first - hat * second)
    return grad_resid, jnp.sum(grad * hat, axis=0, keepdims=True), jnp.sum(grad, axis=0, keepdims=True)


def by_rows(body):
    total = None
    for c in range(ROW // PART):
        got = body(slice(c * PART, (c + 1) * PART))
        if got is not None:
            total = got if total is None else tuple(a + b for a, b in zip(total, got))
    return total


def gelu_both(pre):
    size = jnp.abs(pre)
    near = 1.0 / (1.0 + (0.3275911 * 0.7071067811865476) * size)
    bell = jnp.exp(-0.5 * pre * pre)
    poly = near * (0.127414796 + near * (-0.142248368 + near * (0.7107068705 + near * (-0.7265760135 + near * 0.5307027145))))
    tail = poly * bell
    phi = jnp.where(pre >= 0.0, 1.0 - tail, tail)
    return pre * phi, phi + pre * bell * 0.3989422804014327


def low_lanes(rows):
    return lax.broadcasted_iota(jnp.int32, (rows, 128), 1) < HD


def triangle(size, keys_first, causal):
    row = lax.broadcasted_iota(jnp.int32, (size, size), 0)
    col = lax.broadcasted_iota(jnp.int32, (size, size), 1)
    keep = (row <= col) if keys_first else (col <= row)
    return jnp.where(keep | (causal == 0), 0.0, -BIG).astype(F32)


def over_pairs(body):
    if LOOP:

        def step(pair, _):
            body(pair)
            return 0

        lax.fori_loop(0, HEADS // 2, step, 0)
    else:
        for pair in range(HEADS // 2):
            body(pair)


def lanes(at, pair):
    first = at + 128 * pair
    return pl.ds(first if isinstance(pair, int) else pl.multiple_of(first, 128), 128)


def attend_fwd(causal, q_ref, q_at, k_ref, k_at, v_ref, v_at, fq, fk, ctx_ref, lse_ref, lse_s, tri_s):
    low = low_lanes(ROW)
    lane = lax.broadcasted_iota(jnp.int32, (ROW, 128), 1)
    one = jnp.asarray(1.0, BF)
    if causal is not None:
        tri_s[...] = triangle(ROW, False, causal)

    def body(pair):
        q_pair = q_ref[:, lanes(q_at, pair)] * jnp.asarray(HD**-0.5, BF)
        k_pair = k_ref[:, lanes(k_at, pair)]
        v_pair = v_ref[:, lanes(v_at, pair)]
        halves = []
        for e in range(2):
            sel = low if e == 0 else ~low
            s = dot_nt(jnp.where(sel, q_pair, fq), jnp.where(sel, k_pair, fk))
            if causal is not None:
                s = s + tri_s[...]
            top = jnp.max(s, axis=1, keepdims=True)
            p = jnp.exp(s - top)
            o = dot_nn(p.astype(BF), jnp.where(sel, v_pair, one))
            total = pltpu.roll(o, 64, 1)
            halves.append(o / total)
            lse = top + jnp.log(jnp.where(sel, total, o))
            lse_s[...] = jnp.where(lane == 2 * pair + e, lse, lse_s[...])
        ctx_ref[:, lanes(0, pair)] = jnp.where(low, halves[0], halves[1]).astype(BF)

    over_pairs(body)
    lse_ref[...] = lse_s[...].T[0:HEADS, :]


def attend_bwd(causal, q_ref, q_at, k_ref, k_at, v_ref, v_at, fq, fk, lse_ref, do_ref, outs, dqt_ref, kt_ref, tri_s):
    low = low_lanes(ROW)
    zero = jnp.zeros((ROW, 128), BF)
    scale = jnp.asarray(HD**-0.5, BF)
    kt_ref[...] = k_ref[:, k_at : k_at + D].T
    if causal is not None:
        tri_s[...] = triangle(ROW, True, causal)

    def body(pair):
        q_pair = q_ref[:, lanes(q_at, pair)] * scale
        k_pair = k_ref[:, lanes(k_at, pair)]
        v_pair = v_ref[:, lanes(v_at, pair)]
        do_pair = do_ref[:, lanes(0, pair)]
        dks, dvs = [], []
        for e in range(2):
            head = 2 * pair + e
            sel = low if e == 0 else ~low
            s = dot_nt(jnp.where(sel, k_pair, fk), jnp.where(sel, q_pair, fq))
            if causal is not None:
                s = s + tri_s[...]
            p = jnp.exp(s - lse_ref[pl.ds(head, 1), :])
            prod = p * dot_nt(jnp.where(sel, v_pair, zero), do_pair)
            ds = (prod - p * jnp.sum(prod, axis=0, keepdims=True)).astype(BF)
            dvs.append(dot_nn(p.astype(BF), do_pair))
            dks.append(dot_nn(ds, q_pair))
            rows = pl.ds(HD * head if isinstance(pair, int) else pl.multiple_of(HD * head, HD), HD)
            dqt_ref[rows, :] = dot_nn(kt_ref[rows, :], ds)
        for (ref, at), parts in ((outs[1], dks), (outs[2], dvs)):
            ref[:, lanes(at, pair)] = jnp.where(low, parts[0], parts[1]).astype(BF)

    over_pairs(body)
    ref, at = outs[0]
    ref[:, at : at + D] = (dqt_ref[...] * HD**-0.5).T.astype(BF)


def group_perm(name, to_flat):
    _, cols, _, group = MATS[name]
    width = cols // 128
    size = group * width
    row = lax.broadcasted_iota(jnp.int32, (size, size), 0)
    col = lax.broadcasted_iota(jnp.int32, (size, size), 1)
    blocked, flat = (col, row) if to_flat else (row, col)
    source = width * (blocked & (group - 1)) + lax.shift_right_logical(blocked, group.bit_length() - 1)
    return jnp.where(source == flat, 1.0, 0.0).astype(BF)


def to_matrix(name, flat_ref, at, mat_ref):
    rows, cols, _, group = MATS[name]
    width = cols // 128
    size = group * width
    perm = group_perm(name, False)

    def move(g, _):
        got = dot_nn(perm, flat_ref[at + g * size : at + (g + 1) * size, :]).astype(BF)
        for c in range(width):
            mat_ref[g * group : (g + 1) * group, 128 * c : 128 * c + 128] = got[c * group : (c + 1) * group]
        return 0

    for g in range(rows // group):
        move(g, 0)


def to_flat(name, mat_ref, flat_ref, at):
    rows, cols, _, group = MATS[name]
    width = cols // 128
    size = group * width
    perm = group_perm(name, True)

    def move(g, _):
        block = mat_ref[g * group : (g + 1) * group, :].astype(BF)
        blocked = jnp.concatenate([block[:, 128 * c : 128 * c + 128] for c in range(width)], axis=0)
        flat_ref[at + g * size : at + (g + 1) * size, :] = dot_nn(perm, blocked).astype(BF)
        return 0

    for g in range(rows // group):
        move(g, 0)


def ffn_fwd(hidden_ref, w_up, w_down, act_ref, slope_ref, total_s):
    for c in range(FF // CHUNK):
        cols = slice(c * CHUNK, (c + 1) * CHUNK)
        act, slope = gelu_both(dot_nn(hidden_ref[...], w_up[:, cols]))
        act_ref[:, cols] = act.astype(BF)
        slope_ref[:, cols] = slope.astype(slope_ref.dtype)
    total_s[...] = dot_nn(act_ref[...], w_down[...])


def ffn_bwd(branch_ref, w_up, w_down, slope_ref, dz_ref, total_s):
    for c in range(FF // CHUNK):
        cols = slice(c * CHUNK, (c + 1) * CHUNK)
        grad_act = dot_nt(branch_ref[...], w_down[cols, :])
        dz_ref[:, cols] = (grad_act * slope_ref[:, cols].astype(F32)).astype(BF)
    total_s[...] = dot_nt(dz_ref[...], w_up[...])


def self_head(grad_s, more_s, r1_ref, vec, w_out, dr1_ref, half_s, dctx_ref, gvec):
    def body(rows):
        dr1, gain, shift = ln_back(grad_s[rows, :] + more_s[rows, :], r1_ref[rows, :], vec[0:1, :])
        dr1_ref[rows, :] = dr1
        half_s[rows, :] = dr1.astype(BF)
        return gain, shift

    gvec[0:1, :], gvec[1:2, :] = by_rows(body)
    dctx_ref[...] = dot_nt(half_s[...], w_out[...]).astype(BF)


def copies(sources, targets, sems):
    made = [pltpu.make_async_copy(s, t, sems.at[i]) for i, (s, t) in enumerate(zip(sources, targets))]
    for one in made:
        one.start()
    return made


def piece_row(share, b):
    return 16 * (share * b // TILE)


def shift_kernel(share, shift_ref, params_ref, out_ref, rows_s):
    rows = out_ref.shape[0]
    full = share // 1024
    rows_s[0:16, :] = jnp.zeros((16, 128), F32)
    rows_s[16 + 8 * full :, :] = jnp.zeros((rows_s.shape[0] - 16 - 8 * full, 128), F32)

    def fill(k, _):
        at = pl.multiple_of(1024 * k, 1024)
        rows_s[pl.ds(pl.multiple_of(8 * k + 16, 8), 8), :] = params_ref[:, pl.ds(at, 1024)].reshape(8, 128)
        return 0

    lax.fori_loop(0, full, fill, 0, unroll=8)
    for r in range(-(-(share - 1024 * full) // 128)):
        at = 1024 * full + 128 * r
        width = min(128, share - at)
        rows_s[16 + 8 * full + r : 17 + 8 * full + r, 0:width] = params_ref[:, at : at + width]
    shift = shift_ref[0]
    down, right = shift // 128, lax.rem(shift, 128)
    lane = lax.broadcasted_iota(jnp.int32, (16, 128), 1)

    def move(k, _):
        same = rows_s[pl.ds(16 * k + 16 - down, 16), :]
        above = rows_s[pl.ds(16 * k + 15 - down, 16), :]
        got = jnp.where(lane >= right, pltpu.roll(same, right, 1), pltpu.roll(above, right, 1))
        out_ref[pl.ds(pl.multiple_of(16 * k, 16), 16), :] = got.astype(BF)
        return 0

    lax.fori_loop(0, rows // 16, move, 0, unroll=6)


def unshift_kernel(share, shift_ref, sums_ref, grad_ref, square_ref):
    shift = shift_ref[0]
    down, left = shift // 128, lax.rem(shift, 128)
    lane = lax.broadcasted_iota(jnp.int32, (8, 128), 1)
    full = share // 1024

    def block(at):
        same = sums_ref[pl.ds(at + down, 8), :]
        below = sums_ref[pl.ds(at + down + 1, 8), :]
        back = lax.rem(128 - left, 128)
        return jnp.where(lane < 128 - left, pltpu.roll(same, back, 1), pltpu.roll(below, back, 1))

    def move(k, total):
        got = block(8 * k)
        grad_ref[:, pl.ds(pl.multiple_of(1024 * k, 1024), 1024)] = got.reshape(1, 1024)
        return total + got * got

    total = lax.fori_loop(0, full, move, jnp.zeros((8, 128), F32), unroll=8)
    rest = share - 1024 * full
    if rest:
        got = block(8 * full)
        place = lax.broadcasted_iota(jnp.int32, (8, 128), 0) * 128 + lane
        got = jnp.where(place < rest, got, 0.0)
        total = total + got * got
        for r in range(-(-rest // 128)):
            width = min(128, rest - 128 * r)
            at = 1024 * full + 128 * r
            grad_ref[:, at : at + width] = got[r : r + 1, 0:width]
    square_ref[...] = total


def adam_kernel(share, clip_ref, grad_ref, first_ref, second_ref, step_ref, new_first_ref, new_second_ref):
    clip = clip_ref[0]
    rate = D ** (-0.5) * min(STEP ** (-0.5), STEP * WARMUP ** (-1.5))

    def update(at, width, fold):
        shape = (8, 128) if fold else (1, width)
        scaled = grad_ref[:, pl.ds(at, width)].reshape(shape) * clip
        first = BETA_ONE * first_ref[:, pl.ds(at, width)].reshape(shape) + (1.0 - BETA_ONE) * scaled
        second = BETA_TWO * second_ref[:, pl.ds(at, width)].reshape(shape) + (1.0 - BETA_TWO) * scaled * scaled
        first_hat = first / (1.0 - BETA_ONE**STEP)
        second_hat = second / (1.0 - BETA_TWO**STEP)
        step = rate * first_hat / (jnp.sqrt(second_hat) + ADAM_EPS)
        step_ref[:, pl.ds(at, width)] = step.reshape(1, width)
        new_first_ref[:, pl.ds(at, width)] = first.reshape(1, width)
        new_second_ref[:, pl.ds(at, width)] = second.reshape(1, width)

    def move(k, _):
        update(pl.multiple_of(1024 * k, 1024), 1024, True)
        return 0

    full = share // 1024
    lax.fori_loop(0, full, move, 0, unroll=4)
    for at in range(1024 * full, share, 128):
        update(at, min(128, share - at), False)


def weights_kernel(n, share, flat_in, *refs):
    outs, flat = refs[:6], refs[6]
    for b in range(n):
        tile = share * b // TILE
        last = -(-share * (b + 1) // TILE)
        start, count = 16 * tile, 16 * (last - tile)
        if (share * b) % TILE:
            flat[start : start + 16, :] += flat_in[b, 0:16, :]
        else:
            flat[start : start + 16, :] = flat_in[b, 0:16, :]
        flat[start + 16 : start + count, :] = flat_in[b, 16:count, :]
    for name, ref in zip(MATS, outs):
        to_matrix(name, flat, MATS[name][2], ref)
    outs[5][...] = flat[VEC_AT : VEC_AT + 32, :]


SLOTS = ((0, 1, 2, 3), (1, 0, 3, 2), (2, 2, 0, 1), (3, 3, 1, 0))


def place_pieces(share, z_of, y, x, halves, flat):
    half = halves[0].shape[0]
    for which in range(2):
        for dy in range(2):
            for dx in range(2):
                piece = halves[4 * which + 2 * dy + dx]
                b = 4 * z_of + 2 * lax.rem(y + dy, 2) + lax.rem(x + dx, 2)
                row = pl.multiple_of(16 * ((share * b) // TILE), 16)
                if which == 0:
                    flat[pl.ds(row, 16), :] += piece[0:16, :]
                    flat[pl.ds(row + 16, half - 16), :] = piece[16:half, :]
                else:
                    kept = 16 * (share // TILE) - half
                    flat[pl.ds(row + half, kept), :] = piece[0:kept, :]
                    flat[pl.ds(row + half + kept, half - kept), :] += piece[kept:half, :]


def clear_edges(share, pieces, flat):
    for b in pieces:
        row = 16 * (share * b // TILE)
        last = row + 16 * (share // TILE)
        flat[row : row + 16, :] = jnp.zeros((16, 128), BF)
        flat[last : last + 32, :] = jnp.zeros((32, 128), BF)


def slot_copies(refs, kept, sems):
    a, ax, ay, b, by, bx = refs
    order = (a, ax, ay.at[0], ay.at[1], b, bx.at[0], by, bx.at[1])
    return [pltpu.make_async_copy(ref, kept.at[i], sems.at[i]) for i, ref in enumerate(order)]


def place_kernel(share, place_ref, *refs):
    slots, outs, refs = [refs[6 * i : 6 * i + 6] for i in range(4)], refs[24:30], refs[30:]
    mats, (vec_s, kept, flat, sems, out_sems) = refs[:5], refs[5:]
    sent, emit = emitter(out_sems)
    y, x = place_ref[1], place_ref[2]
    made = [slot_copies(slot, kept.at[i], sems.at[i]) for i, slot in enumerate(slots)]
    for some in made:
        for one in some:
            one.start()
    clear_edges(share, range(16), flat)
    for i, some in enumerate(made):
        z_of = place_ref[3 + i]
        for one in some:
            one.wait()
        place_pieces(share, z_of, y, x, [kept.at[i, j] for j in range(8)], flat)
    for name, mat, out in zip(MATS, mats, outs):
        to_matrix(name, flat, MATS[name][2], mat)
        emit(mat, out)
    vec_s[...] = flat[VEC_AT : VEC_AT + 32, :]
    emit(vec_s, outs[5])
    for one in sent:
        one.wait()


def self_fwd_kernel(causal_ref, x_ref, wqkv, fq, fk, qkv_ref, ctx_ref, lse_ref, lse_s, tri_s):
    qkv_ref[...] = dot_nn(x_ref[...], wqkv[...]).astype(BF)
    attend_fwd(
        causal_ref[0], qkv_ref, 0, qkv_ref, D, qkv_ref, 2 * D, fq[...], fk[...], ctx_ref, lse_ref, lse_s, tri_s
    )


def emitter(sems):
    sent = []

    def emit(source, target):
        sent.append(pltpu.make_async_copy(source, target, sems.at[len(sent)]))
        sent[-1].start()

    return sent, emit


def enc_ffn_kernel(
    x_ref, ctx_ref, vec, w_out, w_up_any, w_down_any, w_cross_any,
    mem_ref, kv_ref, act_any, slope_any, r1_any, r2_any,
    hid_s, total_s, act_s, slope_s, r1_s, r2_s, w_up, w_down, w_cross, in_sems, out_sems,
):
    made = copies((w_up_any, w_down_any, w_cross_any), (w_up, w_down, w_cross), in_sems)
    sent, emit = emitter(out_sems)
    total_s[...] = dot_nn(ctx_ref[...], w_out[...])

    def first(rows):
        r1 = x_ref[rows, :].astype(F32) + total_s[rows, :]
        r1_s[rows, :] = r1
        y1 = ln_parts(r1)[0] * vec[0:1, :] + vec[1:2, :]
        r2_s[rows, :] = y1
        hid_s[rows, :] = y1.astype(BF)

    by_rows(first)
    emit(r1_s, r1_any)
    made[0].wait()
    made[1].wait()
    ffn_fwd(hid_s, w_up, w_down, act_s, slope_s, total_s)
    emit(act_s, act_any)
    emit(slope_s, slope_any)

    def second(rows):
        r2 = r2_s[rows, :] + total_s[rows, :]
        r2_s[rows, :] = r2
        mem = (ln_parts(r2)[0] * vec[2:3, :] + vec[3:4, :]).astype(BF)
        mem_ref[rows, :D] = mem
        mem_ref[rows, D:] = mem

    by_rows(second)
    emit(r2_s, r2_any)
    made[2].wait()
    kv_ref[...] = dot_nn(mem_ref[:, :D], w_cross[...]).astype(BF)
    for one in sent:
        one.wait()


def dec_kernel(
    row, x_ref, ctx1_ref, kv_ref, go_any, vec, w_cross, w_out, w_up_any, w_down_any, fq, fk,
    out_any, gkv_ref, dr1_ref, dctx1_ref, act_any, dz_any, hid_any, br_any, left_any, right_ref, gvec,
    cq_s, lse_s, wide_s, dctx_s, dcq_s, dqt_s, kt_s, slope_s, act_s, dz_s, hid_s, br_s, left_s, out_s,
    go_ref, w_up, w_down, keep_s, r1_s, r2_s, total_s, in_sems, out_sems,
):
    up_copy, down_copy, go_copy = copies(
        (w_up_any, w_down_any, go_any.at[pl.ds(row * ROW, ROW)]), (w_up, w_down, go_ref), in_sems
    )
    sent, emit = emitter(out_sems)
    total_s[...] = dot_nn(ctx1_ref[...], w_out[...])

    def first(rows):
        r1 = x_ref[rows, :].astype(F32) + total_s[rows, :]
        r1_s[rows, :] = r1
        y1 = ln_parts(r1)[0] * vec[0:1, :] + vec[1:2, :]
        keep_s[rows, :] = y1
        left_s[rows, :D] = y1.astype(BF)

    by_rows(first)
    cq_s[...] = dot_nn(left_s[:, :D], w_cross[:, :D]).astype(BF)
    ctx_s = left_s.at[:, D:]
    attend_fwd(None, cq_s, 0, kv_ref, 0, kv_ref, D, fq[...], fk[...], ctx_s, lse_s, wide_s, None)
    emit(left_s, left_any)
    total_s[...] = dot_nn(ctx_s[...], w_cross[:, D:])

    def second(rows):
        r2 = keep_s[rows, :] + total_s[rows, :]
        r2_s[rows, :] = r2
        y2 = ln_parts(r2)[0] * vec[2:3, :] + vec[3:4, :]
        keep_s[rows, :] = y2
        hid_s[rows, :] = y2.astype(BF)

    by_rows(second)
    emit(hid_s, hid_any)
    up_copy.wait()
    down_copy.wait()
    ffn_fwd(hid_s, w_up, w_down, act_s, slope_s, total_s)
    emit(act_s, act_any)
    go_copy.wait()

    def third(rows):
        r3 = keep_s[rows, :] + total_s[rows, :]
        out_s[rows, :] = (ln_parts(r3)[0] * vec[4:5, :] + vec[5:6, :]).astype(BF)
        dr3, gain, shift = ln_back(go_ref[rows, :].astype(F32), r3, vec[4:5, :])
        keep_s[rows, :] = dr3
        br_s[rows, :] = dr3.astype(BF)
        return gain, shift

    gvec[4:5, :], gvec[5:6, :] = by_rows(third)
    emit(out_s, out_any)
    emit(br_s, br_any)
    ffn_bwd(br_s, w_up, w_down, slope_s, dz_s, total_s)
    emit(dz_s, dz_any)

    def fourth(rows):
        dr2, gain, shift = ln_back(keep_s[rows, :] + total_s[rows, :], r2_s[rows, :], vec[2:3, :])
        keep_s[rows, :] = dr2
        right_ref[rows, D:] = dr2.astype(BF)
        return gain, shift

    gvec[2:3, :], gvec[3:4, :] = by_rows(fourth)
    dctx_s[...] = dot_nt(right_ref[:, D:], w_cross[:, D:]).astype(BF)
    attend_bwd(
        None, cq_s, 0, kv_ref, 0, kv_ref, D, fq[...], fk[...], lse_s, dctx_s,
        ((dcq_s, 0), (gkv_ref, 0), (gkv_ref, D)), dqt_s, kt_s, None,
    )
    right_ref[:, :D] = dcq_s[...]
    total_s[...] = dot_nt(dcq_s[...], w_cross[:, :D])
    self_head(keep_s, total_s, r1_s, vec, w_out, dr1_ref, dctx_s, dctx1_ref, gvec)
    for one in sent:
        one.wait()


def enc_back_kernel(
    gkv_ref, r1_any, r2_ref, slope_any, vec, w_cross, w_out_any, w_up_any, w_down_any,
    dr1_ref, dctx1_ref, dz_any, hid_any, br_any, gvec,
    keep_s, total_s, r1_ref, slope_s, w_out, w_up, w_down, dz_s, hid_s, br_s, half_s, in_sems, out_sems,
):
    made = copies(
        (r1_any, slope_any, w_down_any, w_up_any, w_out_any), (r1_ref, slope_s, w_down, w_up, w_out), in_sems
    )
    sent, emit = emitter(out_sems)
    total_s[...] = dot_nt(gkv_ref[...], w_cross[...])
    made[0].wait()

    def first(rows):
        dr2, gain, shift = ln_back(total_s[rows, :], r2_ref[rows, :], vec[2:3, :])
        keep_s[rows, :] = dr2
        br_s[rows, :] = dr2.astype(BF)
        hid_s[rows, :] = (ln_parts(r1_ref[rows, :])[0] * vec[0:1, :] + vec[1:2, :]).astype(BF)
        return gain, shift

    gvec[2:3, :], gvec[3:4, :] = by_rows(first)
    gvec[4:8, :] = jnp.zeros((4, D), F32)
    emit(br_s, br_any)
    emit(hid_s, hid_any)
    for one in made[1:4]:
        one.wait()
    ffn_bwd(br_s, w_up, w_down, slope_s, dz_s, total_s)
    emit(dz_s, dz_any)
    made[4].wait()
    self_head(keep_s, total_s, r1_ref, vec, w_out, dr1_ref, half_s, dctx1_ref, gvec)
    for one in sent:
        one.wait()


def row_fetcher(kinds, rows, dec_ref, refs):
    count = len(kinds) * rows
    buffers, sems = refs[-len(kinds) - 1 : -1], refs[-1]
    ins = refs[: -len(kinds) - 1]
    sources = [ins[i : i + count] for i in range(0, len(ins), count)]
    kept = dict(zip(kinds, buffers))

    def fetch(some, i):
        size = some[i].shape[0]
        target = kept[kinds[i // rows]].at[pl.ds((i % rows) * size, size)]
        return pltpu.make_async_copy(some[i], target, sems.at[i])

    def begin(some):
        for i in range(count):
            fetch(some, i).start()

    if len(sources) == 1:
        begin(sources[0])
    else:
        for which, some in enumerate(sources):
            pl.when(dec_ref[0] == which)(functools.partial(begin, some))

    def ready(*some):
        for kind in some:
            for r in range(rows):
                fetch(sources[0], kinds.index(kind) * rows + r).wait()

    return kept, ready


def fetched(kinds, sources):
    ins = [row[kind] for some in sources for kind in kinds for row in some]
    rows = len(sources[0])
    kept = []
    for kind in kinds:
        size, cols = sources[0][0][kind].shape
        kept.append(pltpu.VMEM((rows * size, cols), sources[0][0][kind].dtype))
    return ins, kept + [pltpu.SemaphoreType.DMA((len(kinds) * rows,))]


FFN_KINDS = ("hid", "dz", "act", "branch")
ATTEND_KINDS = ("ctx", "dr1", "left", "right")


def ffn_grads_kernel(rows, dec_ref, *refs):
    count = 2 * len(FFN_KINDS) * rows
    ins, flat, (hid_t, g_up, g_down), rest = refs[:count], refs[count], refs[count + 1 : count + 4], refs[count + 4 :]
    kept, ready = row_fetcher(FFN_KINDS, rows, dec_ref, (*ins, *rest))
    ready("hid", "dz")
    hid_t[...] = kept["hid"][...].T
    for c in range(FF // CHUNK):
        cols = slice(c * CHUNK, (c + 1) * CHUNK)
        g_up[:, cols] = dot_nn(hid_t[...], kept["dz"][:, cols])
    to_flat("up", g_up, flat, 0)
    ready("act", "branch")
    for c in range(FF // D):
        part = slice(c * D, (c + 1) * D)
        g_down[part, :] = dot_tn(kept["act"][:, part], kept["branch"][...])
    to_flat("down", g_down, flat, MATS["down"][2] - MATS["up"][2])


def attend_grads_kernel(rows, dec_ref, *refs):
    count = 2 * len(ATTEND_KINDS) * rows
    ins, flat, (g_cross, g_out), rest = refs[:count], refs[count], refs[count + 1 : count + 3], refs[count + 3 :]
    kept, ready = row_fetcher(ATTEND_KINDS, rows, dec_ref, (*ins, *rest))
    ready("ctx", "dr1")
    g_out[...] = dot_tn(kept["ctx"][...], kept["dr1"][...].astype(BF))
    to_flat("out", g_out, flat, 0)
    ready("left", "right")
    for at in (0, D):
        g_cross[:, at : at + D] = dot_tn(kept["left"][:, at : at + D], kept["right"][:, at : at + D])
    to_flat("cross", g_cross, flat, MATS["cross"][2] - REST_AT)


BACK_KINDS = ("qkv", "lse", "dctx", "dr1")


def self_back_kernel(ins, causal_ref, wqkv, fq, fk, *refs):
    (dx_ref, dqkv, dqt_s, kt_s, tri_s), rest = refs[ins : ins + 5], refs[ins + 5 :]
    kept, ready = row_fetcher(BACK_KINDS, 1, causal_ref, (*refs[:ins], *rest))
    ready("qkv", "lse", "dctx")
    qkv = kept["qkv"]
    attend_bwd(
        causal_ref[0], qkv, 0, qkv, D, qkv, 2 * D, fq[...], fk[...], kept["lse"], kept["dctx"],
        ((dqkv, 0), (dqkv, D), (dqkv, 2 * D)), dqt_s, kt_s, tri_s,
    )
    ready("dr1")
    dx_ref[...] = (kept["dr1"][...] + dot_nt(dqkv[...], wqkv[...])).astype(BF)


def qkv_kernel(ins, rows, dec_ref, x_ref, *refs):
    (fl_qkv, x_t, g_qkv), rest = refs[ins : ins + 3], refs[ins + 3 :]
    kept, ready = row_fetcher(("dqkv",), rows, dec_ref, (*refs[:ins], *rest))
    x_t[...] = x_ref[...].T
    ready("dqkv")
    for c in range(3):
        cols = slice(c * D, (c + 1) * D)
        g_qkv[:, cols] = dot_nn(x_t[...], kept["dqkv"][:, cols])
    to_flat("qkv", g_qkv, fl_qkv, 0)


def pack_kernel(share, planes, base, place_ref, *refs):
    parts, outs, flat = refs[:-5], refs[-5:-1], refs[-1]
    send_a, keep_a, send_b, keep_b = outs
    at = 0
    for part in parts:
        flat[at : at + part.shape[0], :] = part[...]
        at += part.shape[0]
    y, x = place_ref[0], place_ref[1]
    half = send_a.shape[2]
    for i, z in enumerate(planes):
        for j in range(2):
            for ref, y_to, x_to, skip in (
                (send_a, 1 - y, j, 0), (keep_a, y, j, 0), (send_b, j, 1 - x, half), (keep_b, j, x, half),
            ):
                b = 4 * z + 2 * y_to + x_to
                start = pl.multiple_of(16 * ((share * b) // TILE) - base + skip, 16)
                ref[i, j] = flat[pl.ds(start, half), :]


def kernel_call(body, micros=1, **options):
    cost = pl.CostEstimate(flops=micros * 10**9, bytes_accessed=0, transcendentals=0)
    call = pl.pallas_call(body, cost_estimate=cost, **options)
    return lambda *operands: tuple(call(*operands))


IN_VMEM = pl.BlockSpec(memory_space=pltpu.VMEM)
IN_SMEM = pl.BlockSpec(memory_space=pltpu.SMEM)
ANYWHERE = pl.BlockSpec(memory_space=pl.ANY)


def at_row(row, cols, rows=ROW):
    return pl.BlockSpec((rows, cols), lambda i: (row, 0), pipeline_mode=pl.Buffered(1))


def shifted(shift, params, share, rows):
    return kernel_call(
        functools.partial(shift_kernel, share),
        in_specs=[IN_SMEM, IN_VMEM],
        out_specs=[IN_VMEM],
        out_shape=[shape_of((rows, 128), BF)],
        scratch_shapes=[pltpu.VMEM((rows + 32, 128), F32)],
        compiler_params=params_of(8),
    )(shift, params)[0]


def unshifted(shift, sums, share):
    return kernel_call(
        functools.partial(unshift_kernel, share),
        in_specs=[IN_SMEM, IN_VMEM],
        out_specs=[IN_VMEM] * 2,
        out_shape=[shape_of((1, share), F32), shape_of((8, 128), F32)],
        compiler_params=params_of(8),
    )(shift, sums)


def adam(clip, grad, first, second, share):
    return kernel_call(
        functools.partial(adam_kernel, share),
        in_specs=[IN_SMEM] + [IN_VMEM] * 3,
        out_specs=[IN_VMEM] * 3,
        out_shape=[shape_of((1, share), F32)] * 3,
        compiler_params=params_of(16),
    )(clip, grad, first, second)


def split_weights(pieces, n, share):
    shapes = [(rows, cols) for rows, cols, _, _ in MATS.values()] + [(32, 128)]
    rows = 16 * (-(-share * n // TILE) + 2)
    got = kernel_call(
        functools.partial(weights_kernel, n, share),
        in_specs=[IN_VMEM],
        out_specs=[IN_VMEM] * 6,
        out_shape=[shape_of(s, BF) for s in shapes],
        scratch_shapes=[pltpu.VMEM((rows, 128), BF)],
        compiler_params=params_of(60),
    )(pieces)
    return dict(zip((*MATS, "vec"), got))


def placed_weights(place, slots, share, rows):
    vm = pltpu.VMEM
    shapes = [(rows, cols) for rows, cols, _, _ in MATS.values()] + [(32, 128)]
    got = kernel_call(
        functools.partial(place_kernel, share),
        micros=9,
        in_specs=[IN_SMEM] + [ANYWHERE] * 24,
        out_specs=[ANYWHERE] * 6,
        out_shape=[shape_of(s, BF) for s in shapes],
        scratch_shapes=[vm(s, BF) for s in shapes]
        + [vm((4, 8, rows // 2, 128), BF), vm((piece_row(share, 15) + rows + 16, 128), BF)]
        + [pltpu.SemaphoreType.DMA((4, 8)), pltpu.SemaphoreType.DMA((6,))],
        compiler_params=params_of(60),
    )(place, *(one for slot in slots for one in slot))
    return dict(zip((*MATS, "vec"), got))


def row_shapes(*cols):
    return [shape_of((ROW, abs(c)), F32 if c < 0 else BF) for c in cols]


def self_fwd(causal, row, x, w_qkv, fq, fk):
    names = ("qkv", "ctx", "lse")
    vm = pltpu.VMEM
    got = kernel_call(
        self_fwd_kernel,
        micros=5,
        grid=(1,),
        in_specs=[IN_SMEM, at_row(row, D), whole_spec((D, 3 * D)), at_row(row, 128), at_row(row, 128)],
        out_specs=[at_row(0, 3 * D), at_row(0, D), at_row(0, ROW, HEADS)],
        out_shape=row_shapes(3 * D, D) + [shape_of((HEADS, ROW), F32)],
        scratch_shapes=[vm((ROW, 128), F32), vm((ROW, ROW), F32)],
        compiler_params=params_of(24),
    )(causal, x, w_qkv, fq, fk)
    return dict(zip(names, got))


def enc_ffn(row, x, fwd, w, vec):
    names = ("mem", "kv", "act", "slope", "r1", "r2")
    vm = pltpu.VMEM
    got = kernel_call(
        enc_ffn_kernel,
        micros=8,
        grid=(1,),
        in_specs=[at_row(row, D), at_row(0, D), whole_spec((6, D)), whole_spec((D, D))] + [ANYWHERE] * 3,
        out_specs=[at_row(0, 2 * D), at_row(0, 2 * D)] + [ANYWHERE] * 4,
        out_shape=row_shapes(2 * D, 2 * D, FF, FF, -D, -D),
        scratch_shapes=[
            vm((ROW, D), BF), vm((ROW, D), F32), vm((ROW, FF), BF), vm((ROW, FF), BF), vm((ROW, D), F32), vm((ROW, D), F32),
            vm((D, FF), BF), vm((FF, D), BF), vm((D, 2 * D), BF), pltpu.SemaphoreType.DMA((3,)), pltpu.SemaphoreType.DMA((4,)),
        ],
        compiler_params=params_of(32),
    )(x, fwd["ctx"], vec, w["out"], w["up"], w["down"], w["cross"])
    return dict(zip(names, got))


def dec_call(row, x, fwd, kv, go, w, vec, fq, fk):
    vm = pltpu.VMEM
    names = ("out", "gkv", "dr1", "dctx", "act", "dz", "hid", "branch", "left", "right", "gvec")
    got = kernel_call(
        functools.partial(dec_kernel, row),
        micros=23,
        grid=(1,),
        in_specs=[
            at_row(row, D), at_row(0, D), at_row(0, 2 * D), ANYWHERE, whole_spec((6, D)), whole_spec((D, 2 * D)),
            whole_spec((D, D)), ANYWHERE, ANYWHERE, at_row(row, 128), at_row(row, 128),
        ],
        out_specs=[ANYWHERE, at_row(0, 2 * D), at_row(0, D), at_row(0, D)] + [ANYWHERE] * 5
        + [at_row(0, 2 * D), whole_spec((8, D))],
        out_shape=row_shapes(D, 2 * D, -D, D, FF, FF, D, D, 2 * D, 2 * D) + [shape_of((8, D), F32)],
        scratch_shapes=[
            vm((ROW, D), BF), vm((HEADS, ROW), F32), vm((ROW, 128), F32), vm((ROW, D), BF), vm((ROW, D), BF),
            vm((D, ROW), F32), vm((D, ROW), BF), vm((ROW, FF), BF), vm((ROW, FF), BF), vm((ROW, FF), BF), vm((ROW, D), BF),
            vm((ROW, D), BF), vm((ROW, 2 * D), BF), vm((ROW, D), BF), vm((ROW, D), BF), vm((D, FF), BF),
            vm((FF, D), BF), vm((ROW, D), F32), vm((ROW, D), F32), vm((ROW, D), F32), vm((ROW, D), F32),
            pltpu.SemaphoreType.DMA((3,)), pltpu.SemaphoreType.DMA((6,)),
        ],
        compiler_params=params_of(60),
    )(x, fwd["ctx"], kv, go, vec, w["cross"], w["out"], w["up"], w["down"], fq, fk)
    return dict(zip(names, got))


def enc_back(gkv, fwd, w, vec):
    names = ("dr1", "dctx", "dz", "hid", "branch", "gvec")
    vm = pltpu.VMEM
    got = kernel_call(
        enc_back_kernel,
        micros=8,
        grid=(1,),
        in_specs=[
            at_row(0, 2 * D), ANYWHERE, at_row(0, D), ANYWHERE, whole_spec((6, D)), whole_spec((D, 2 * D)),
            ANYWHERE, ANYWHERE, ANYWHERE,
        ],
        out_specs=[at_row(0, D), at_row(0, D)] + [ANYWHERE] * 3 + [whole_spec((8, D))],
        out_shape=row_shapes(-D, D, FF, D, D) + [shape_of((8, D), F32)],
        scratch_shapes=[
            vm((ROW, D), F32), vm((ROW, D), F32), vm((ROW, D), F32), vm((ROW, FF), BF), vm((D, D), BF), vm((D, FF), BF),
            vm((FF, D), BF), vm((ROW, FF), BF), vm((ROW, D), BF), vm((ROW, D), BF), vm((ROW, D), BF), pltpu.SemaphoreType.DMA((5,)),
            pltpu.SemaphoreType.DMA((3,)),
        ],
        compiler_params=params_of(32),
    )(gkv, fwd["r1"], fwd["r2"], fwd["slope"], vec, w["cross"], w["out"], w["up"], w["down"])
    return dict(zip(names, got))


def row_grads(body, kinds, flat_rows, scratch, is_dec, sources):
    ins, kept = fetched(kinds, sources)
    return kernel_call(
        functools.partial(body, len(sources[0])),
        micros=1,
        in_specs=[IN_SMEM] + [ANYWHERE] * len(ins),
        out_specs=[IN_VMEM],
        out_shape=[shape_of((flat_rows, 128), BF)],
        scratch_shapes=scratch + kept,
        compiler_params=params_of(48),
    )(is_dec, *ins)[0]


def self_back(causal, row, sources, w, fq, fk):
    vm = pltpu.VMEM
    shapes = row_shapes(D, 3 * D)
    ins, kept = fetched(BACK_KINDS, [[one] for one in sources])
    got = kernel_call(
        functools.partial(self_back_kernel, len(ins)),
        micros=1,
        grid=(1,),
        in_specs=[IN_SMEM, whole_spec((D, 3 * D)), at_row(row, 128), at_row(row, 128)] + [ANYWHERE] * len(ins),
        out_specs=[whole_spec(s.shape) for s in shapes],
        out_shape=shapes,
        scratch_shapes=[vm((D, ROW), F32), vm((D, ROW), BF), vm((ROW, ROW), F32)] + kept,
        compiler_params=params_of(28),
    )(causal, w["qkv"], fq, fk, *ins)
    return dict(zip(("dx", "dqkv"), got))


def qkv_grad(is_dec, x, sources):
    vm = pltpu.VMEM
    t, rows = x.shape[0], len(sources[0])
    ins, kept = fetched(("dqkv",), sources)
    return kernel_call(
        functools.partial(qkv_kernel, len(ins), rows),
        micros=1,
        in_specs=[IN_SMEM, IN_VMEM] + [ANYWHERE] * len(ins),
        out_specs=[IN_VMEM],
        out_shape=[shape_of((REST_AT, 128), BF)],
        scratch_shapes=[vm((D, t), BF), vm((D, 3 * D), F32)] + kept,
        compiler_params=params_of(28),
    )(is_dec, x, *ins)[0]


def pack(place, parts, planes, base, share, rows):
    half = rows // 2
    parts = [p if isinstance(p, tuple) else (p, p.shape[0]) for p in parts]
    total = sum(count for _, count in parts)
    need = piece_row(share, 4 * planes[-1] + 3) - base + rows
    return kernel_call(
        functools.partial(pack_kernel, share, planes, base),
        micros=1,
        grid=(1,),
        in_specs=[IN_SMEM] + [pl.BlockSpec((count, 128), lambda i: (0, 0), pipeline_mode=pl.Buffered(1)) for _, count in parts],
        out_specs=[whole_spec((len(planes), 2, half, 128))] * 4,
        out_shape=[shape_of((len(planes), 2, half, 128), BF)] * 4,
        scratch_shapes=[pltpu.VMEM((max(total, need), 128), BF)],
        compiler_params=params_of(32),
    )(place, *(p for p, _ in parts))


def mask_features(segments, live):
    t = segments.shape[0]
    lane = (jnp.arange(128, dtype=jnp.int32) % HD)[None, :]
    pair = lane // 2
    odd = lane % 2 == 1
    is_seg = pair < SEG_BITS
    is_pos = (pair >= SEG_BITS) & (pair < SEG_BITS + POS_BITS)
    place = (jnp.arange(t, dtype=jnp.int32) % ROW)[:, None]
    bit = jnp.where(
        is_seg,
        (segments[:, None] >> jnp.minimum(pair, SEG_BITS)) & 1,
        (place >> jnp.clip(pair - SEG_BITS, 0, POS_BITS)) & 1,
    )
    query = jnp.where(odd, 1 - bit, bit) * (is_seg | is_pos)
    key = jnp.where(odd, bit, 1 - bit)
    keys = [jnp.where(is_seg | (is_pos & (live[i][:, None] != 1)), key.astype(F32) * -BIG, 0.0).astype(BF) for i in range(2)]
    return query.astype(BF), keys[0], keys[1]


def ghosts(shapes):
    if not shapes:
        return ()
    return kernel_call(lambda *refs: None, out_specs=[ANYWHERE] * len(shapes), out_shape=list(shapes))()


def either(is_decoder, dec, enc, dec_first=False):
    thunks = (enc, dec)
    made = [jax.eval_shape(t) for t in thunks]
    slots, where = [], []
    for tree in made:
        free = list(range(len(slots)))
        taken = []
        for leaf in jax.tree.leaves(tree):
            key = (leaf.shape, leaf.dtype)
            match = next((i for i in free if slots[i] == key), None)
            if match is None:
                slots.append(key)
                match = len(slots) - 1
            else:
                free.remove(match)
            taken.append(match)
        where.append(taken)

    def branch(which):
        def run():
            leaves = jax.tree.leaves(thunks[which]())
            filled = dict(zip(where[which], leaves))
            missing = [i for i in range(len(slots)) if i not in filled]
            filled.update(zip(missing, ghosts([shape_of(*slots[i]) for i in missing])))
            return tuple(filled[i] for i in range(len(slots)))

        return run

    if dec_first:
        got = lax.cond(jnp.logical_not(is_decoder), branch(0), branch(1))
    else:
        got = lax.cond(is_decoder, branch(1), branch(0))
    back = [jax.tree.unflatten(jax.tree.structure(made[i]), [got[s] for s in where[i]]) for i in range(2)]
    return back[1], back[0]


def plane_permute(value, step):
    return lax.ppermute(value, "batch", [(i, i ^ step) for i in range(16)])


def line_permute(value, step, sources):
    pairs = [(4 * z + k, 4 * (z + step) + k) for z in sources for k in range(4)]
    return lax.ppermute(value, "batch", pairs)


def over_all(value):
    axes = ("section", "batch")
    places = [(core, i) for core in range(2) for i in range(16)]

    def flat(core, i):
        return core * 16 + i

    total = value
    for core_step in range(2):
        for step in range(4):
            if core_step or step:
                pairs = [(flat(c, i), flat(c ^ core_step, i ^ step)) for c, i in places]
                total = total + lax.ppermute(value, axes, pairs)
    value = total
    for step in (4, 8, 12):
        total = total + plane_permute(value, step)
    return total


def tied(*values):
    return lax.optimization_barrier(values)


def gathered(own, z):
    half = own.shape[0] // 2

    def first(block):
        a, b = block[:half], block[half:]
        return a, b, plane_permute(a, 1), plane_permute(b, 2)

    def second(parts):
        a, b, ax, by = parts
        return (a, ax, plane_permute(jnp.stack([a, ax]), 2), b, by, plane_permute(jnp.stack([b, by]), 1))

    up, down = line_permute(own, 1, (0, 1, 2)), line_permute(own, -1, (1, 2, 3))
    begun = first(own)
    zero = second(begun)
    up, down, _ = tied(up, down, begun)
    up_two, down_two = line_permute(up, 1, (1, 2)), line_permute(down, -1, (1, 2))
    begun = first(jnp.where((z == 0) | (z == 2), down, up))
    zero, begun = tied(zero, begun)
    one = second(begun)
    up_two, down_two, _ = tied(up_two, down_two, zero)
    up_three, down_three = line_permute(up_two, 1, (2,)), line_permute(down_two, -1, (1,))
    begun = first(jnp.where(z == 0, down_two, jnp.where(z == 1, down, up_two)))
    one, begun = tied(one, begun)
    two = second(begun)
    up_three, down_three, _ = tied(up_three, down_three, one)
    begun = first(jnp.where(z == 0, down_three, jnp.where(z == 1, down_two, jnp.where(z == 2, up, up_three))))
    two, begun = tied(two, begun)
    three = second(begun)
    return zero, one, two, three


def added(*values):
    total = values[0].astype(F32)
    for value in values[1:]:
        total = total + value.astype(F32)
    return total


def plane_start(packed):
    send_a, keep_a, send_b, keep_b = packed
    return keep_a, plane_permute(send_a, 2), keep_b, plane_permute(send_b, 1)


def plane_end(begun, y, x):
    keep_a, got_a, keep_b, got_b = begun

    def part(keep, got, index):
        return added(lax.dynamic_index_in_dim(keep, index, 1, False), lax.dynamic_index_in_dim(got, index, 1, False))

    far_a, far_b = part(keep_a, got_a, 1 - x).astype(BF), part(keep_b, got_b, 1 - y).astype(BF)
    in_a, in_b = plane_permute(far_a, 1), plane_permute(far_b, 2)
    sum_a, sum_b = added(part(keep_a, got_a, x), in_a), added(part(keep_b, got_b, y), in_b)
    return jnp.stack([sum_a.astype(BF), sum_b.astype(BF)], axis=1)


def line_sums(early, mid, late, z):
    one, two, three = mid[0], early[0], early[1]

    def low(value):
        return value.astype(BF)

    up = line_permute(three, 1, (0,))
    down = line_permute(one, -1, (3,))
    up = line_permute(low(jnp.where(z == 0, two.astype(F32), added(three, up))), 1, (0, 1))
    down = line_permute(low(jnp.where(z == 3, two.astype(F32), added(one, down))), -1, (2, 3))
    third = jnp.where(z == 0, one.astype(F32), added(jnp.where(z == 1, two, three), up))
    up = line_permute(low(third), 1, (0, 1, 2))
    zero = late[0]
    near = line_permute(zero, -1, (1, 3))
    pair = added(zero, near)
    far = line_permute(low(pair), -2, (2,))
    own = jnp.where(z == 1, one, jnp.where(z == 2, two, three))
    return jnp.where(z == 0, added(pair, far), added(own, up, down))


def shards(params, first_moment, second_moment, inputs, segments, live_mask, out_grad):
    is_decoder = lax.axis_index("section") == 1
    me = lax.axis_index("batch")
    n = lax.axis_size("batch")
    share = params.shape[1]
    rows = 16 * (share // TILE + 2)
    shift = lax.rem(me * (share % TILE), TILE)[None]
    x = inputs[0]
    t = x.shape[0]
    count = t // ROW

    y, x_at, z = lax.rem(me // 2, 2), lax.rem(me, 2), me // 4
    custom = n == 16
    flag = is_decoder.astype(jnp.int32)[None]
    own = shifted(shift, params, share, rows)
    fq, fk_src, fk_tgt = mask_features(segments, live_mask)
    fk_self = jnp.where(is_decoder, fk_tgt, fk_src)
    if custom:
        spot = jnp.concatenate([jnp.stack([z, y, x_at]), jnp.asarray(SLOTS, jnp.int32)[:, z]])
        slots, fq, fk_src, fk_self = tied(gathered(own, z), fq, fk_src, fk_self)
        w = placed_weights(spot, slots, share, rows)
    else:
        pieces = lax.all_gather(own, "batch", axis=0, tiled=False)
        pieces, fq, fk_src, fk_self = tied(pieces, fq, fk_src, fk_self)
        w = split_weights(pieces, n, share)
    def forward(row):
        return self_fwd(flag, row, x, w["qkv"], fq, fk_self)

    first_fwd = forward(0)
    vec = w["vec"][:24].astype(F32).reshape(6, D)

    def nothing():
        return {}

    def swapped(value):
        return lax.ppermute(value, "section", [(0, 1), (1, 0)])

    fwd = [first_fwd]
    first = enc_ffn(0, x, first_fwd, w, vec)
    kept, dec_rows, enc_rows, back, enc_self = [first], [], [], [], []
    kv_in = swapped(first["kv"])
    if count > 1:
        fwd.append(forward(1))
        kv_in, fwd[1] = tied(kv_in, fwd[1])
    for row in range(count):

        def dec_make():
            got = dec_call(row, x, fwd[row], kv_in, out_grad, w, vec, fq, fk_src)
            return got.pop("gkv"), got

        def enc_make():
            ahead = [enc_ffn(row + 1, x, fwd[row + 1], w, vec)] if row + 1 < count else []
            done = [enc_back(back[row - 1], kept[row - 1], w, vec)] if row else []
            far = []
            if row and row == count - 1:
                far = [self_back(flag, 0, [{**(enc_rows or done)[0], **fwd[0]}], w, fq, fk_self)]
            return [k.pop("kv") for k in ahead], (ahead, done, far)

        (sent, got), (_, (ahead, done, far)) = either(is_decoder, dec_make, enc_make, DEC_FIRST)
        dec_rows.append(got)
        enc_rows += done
        kept += ahead
        enc_self += far
        kv_in = swapped(sent)
        if row + 2 < count:
            fwd.append(forward(row + 2))
            kv_in, fwd[-1] = tied(kv_in, fwd[-1])
        back.append(kv_in)
    dec_fwd = enc_fwd = fwd

    last = count - 1
    dec_self, done = either(
        is_decoder,
        lambda: [self_back(flag, 0, [{**dec_rows[0], **dec_fwd[0]}], w, fq, fk_self)] if last else [],
        lambda: enc_back(back[last], kept[last], w, vec),
    )
    enc_rows.append(done)
    dec_all = [{**made, **fwd} for made, fwd in zip(dec_rows, dec_fwd)]
    enc_all = [
        {**made, **fwd, "act": k["act"], "left": k["mem"], "right": g}
        for made, fwd, k, g in zip(enc_rows, enc_fwd, kept, back)
    ]
    both = [enc_all, dec_all]

    gvec = jnp.where(is_decoder, sum(r["gvec"] for r in dec_rows), sum(r["gvec"] for r in enc_rows))
    fl_vec = jnp.pad(gvec[:6].reshape(24, 128).astype(BF), ((0, 24), (0, 0)))

    vm = pltpu.VMEM
    flat_ffn = row_grads(
        ffn_grads_kernel, FFN_KINDS, VEC_AT - MATS["up"][2],
        [vm((D, t), BF), vm((D, FF), F32), vm((FF, D), F32)], flag, both,
    )
    place = jnp.stack([y, x_at])
    if custom:
        packed = pack(place, [flat_ffn, fl_vec], (2, 3), MATS["up"][2], share, rows)
        early = plane_start(packed)
        flag, _ = tied(flag, packed[0])
    flat_attend = row_grads(
        attend_grads_kernel, ATTEND_KINDS, MATS["up"][2] - REST_AT,
        [vm((D, 2 * D), F32), vm((D, D), F32)], flag, both,
    )
    if custom:
        need = piece_row(share, 7) + rows - MATS["up"][2]
        packed = pack(place, [flat_attend, (flat_ffn, need)], (1,), REST_AT, share, rows)
        mid = plane_start(packed)
        flag, _ = tied(flag, packed[0])

    common = []
    for row in range(len(dec_self), count):
        common.append(self_back(flag, row, [enc_all[row], dec_all[row]], w, fq, fk_self))
    if custom:
        early, common[-1] = tied(early, common[-1])
        early = plane_end(early, y, x_at)
    fl_qkv = qkv_grad(flag, x, [[*enc_self, *common], [*dec_self, *common]])
    dx = jnp.concatenate(
        [jnp.where(is_decoder, d["dx"], e["dx"]) for d, e in zip(dec_self, enc_self)] + [r["dx"] for r in common], axis=0
    )
    layer_out = jnp.where(
        is_decoder,
        jnp.concatenate([r["out"] for r in dec_rows], axis=0),
        jnp.concatenate([k["mem"][:, :D] for k in kept], axis=0),
    )

    if custom:
        mid, fl_qkv = tied(mid, fl_qkv)
        mid = plane_end(mid, y, x_at)
        need = piece_row(share, 3) + rows
        late = plane_start(pack(place, [fl_qkv, (flat_attend, need - REST_AT)], (0,), 0, share, rows))
        late = plane_end(late, y, x_at)
        mine = line_sums(early, mid, late, z).reshape(rows, 128)
    else:
        spare = jnp.zeros((piece_row(share, n - 1) + rows - FLAT_ROWS, 128), BF)
        flat = jnp.concatenate([fl_qkv, flat_attend, flat_ffn, fl_vec[:24], spare], axis=0)
        stacked = jnp.concatenate([flat[piece_row(share, b) :][:rows] for b in range(n)], axis=0)
        mine = lax.psum_scatter(stacked, "batch", scatter_dimension=0, tiled=True).astype(F32)
    grad_share, squares = unshifted(shift, jnp.pad(mine, ((0, 8), (0, 0))), share)

    if custom:
        square_sum = jnp.sum(over_all(squares))
    else:
        square_sum = lax.psum(jnp.sum(squares), ("section", "batch"))
    grad_norm = jnp.sqrt(square_sum)
    clip_factor = MAXNORM / jnp.maximum(grad_norm, MAXNORM)
    param_step, new_first, new_second = adam(clip_factor[None], grad_share, first_moment, second_moment, share)
    return (param_step, new_first, new_second, grad_share, layer_out[None], dx[None], grad_norm)


def solution(mesh):
    in_specs = (
        P("section", "batch"),
        P("section", "batch"),
        P("section", "batch"),
        P("section", "batch", None),
        P("batch"),
        P(None, "batch"),
        P("batch", None),
    )
    out_specs = (
        P("section", "batch"),
        P("section", "batch"),
        P("section", "batch"),
        P("section", "batch"),
        P("section", "batch", None),
        P("section", "batch", None),
        P(),
    )
    return jax.shard_map(shards, mesh=mesh, in_specs=in_specs, out_specs=out_specs, check_vma=False)
```

```python
import functools

import jax
import jax.numpy as jnp
from jax import lax
from jax.experimental import pallas as pl
from jax.experimental.pallas import tpu as pltpu
from jax.sharding import PartitionSpec as P

D = 512
FF = 2048
HEADS = 8
HD = 64
ROW = 512
STEP = 1000
WARMUP = 4000

BIG = 1e30
LN_EPS = 1e-05
BETA_ONE = 0.9
BETA_TWO = 0.98
ADAM_EPS = 1e-09
MAXNORM = 0.1

F32 = jnp.float32
BF = jnp.bfloat16
TILE = 16 * 128
CHUNK = 512
PART = 64
SEG_BITS = 12
POS_BITS = 9
DEC_FIRST = True
LOOP = False

MATS = {}
_at = 0
for _name, _rows, _cols in (("qkv", D, 3 * D), ("out", D, D), ("cross", D, 2 * D), ("up", D, FF), ("down", FF, D)):
    _width = _cols // 128
    MATS[_name] = (_rows, _cols, _at, {12: 16, 4: 64, 8: 32, 16: 16}[_width])
    _at += _rows * _width
VEC_AT = _at
FLAT_ROWS = _at + 24
REST_AT = MATS["out"][2]


def dot_nn(lhs, rhs):
    return jnp.dot(lhs, rhs, preferred_element_type=F32)


def dot_nt(lhs, rhs):
    return lax.dot_general(lhs, rhs, (((1,), (1,)), ((), ())), preferred_element_type=F32)


def dot_tn(lhs, rhs):
    return lax.dot_general(lhs, rhs, (((0,), (0,)), ((), ())), preferred_element_type=F32)


def params_of(mib):
    return pltpu.CompilerParams(vmem_limit_bytes=mib * 2**20)


def row_spec(rows, cols):
    return pl.BlockSpec((rows, cols), lambda i: (i, 0))


def whole_spec(shape):
    return pl.BlockSpec(shape, lambda i: (0,) * len(shape), pipeline_mode=pl.Buffered(1))


def shape_of(shape, dtype):
    return jax.ShapeDtypeStruct(shape, dtype)


def ln_parts(resid):
    center = resid - jnp.mean(resid, axis=-1, keepdims=True)
    rstd = lax.rsqrt(jnp.mean(center * center, axis=-1, keepdims=True) + LN_EPS)
    return center * rstd, rstd


def ln_back(grad, resid, gain):
    hat, rstd = ln_parts(resid)
    scaled = grad * gain
    first = jnp.mean(scaled, axis=-1, keepdims=True)
    second = jnp.mean(scaled * hat, axis=-1, keepdims=True)
    grad_resid = rstd * (scaled - first - hat * second)
    return grad_resid, jnp.sum(grad * hat, axis=0, keepdims=True), jnp.sum(grad, axis=0, keepdims=True)


def by_rows(body):
    total = None
    for c in range(ROW // PART):
        got = body(slice(c * PART, (c + 1) * PART))
        if got is not None:
            total = got if total is None else tuple(a + b for a, b in zip(total, got))
    return total


def gelu_both(pre):
    size = jnp.abs(pre)
    near = 1.0 / (1.0 + (0.3275911 * 0.7071067811865476) * size)
    bell = jnp.exp(-0.5 * pre * pre)
    poly = near * (0.127414796 + near * (-0.142248368 + near * (0.7107068705 + near * (-0.7265760135 + near * 0.5307027145))))
    tail = poly * bell
    phi = jnp.where(pre >= 0.0, 1.0 - tail, tail)
    return pre * phi, phi + pre * bell * 0.3989422804014327


def low_lanes(rows):
    return lax.broadcasted_iota(jnp.int32, (rows, 128), 1) < HD


def triangle(size, keys_first, causal):
    row = lax.broadcasted_iota(jnp.int32, (size, size), 0)
    col = lax.broadcasted_iota(jnp.int32, (size, size), 1)
    keep = (row <= col) if keys_first else (col <= row)
    return jnp.where(keep | (causal == 0), 0.0, -BIG).astype(F32)


def over_pairs(body):
    if LOOP:

        def step(pair, _):
            body(pair)
            return 0

        lax.fori_loop(0, HEADS // 2, step, 0)
    else:
        for pair in range(HEADS // 2):
            body(pair)


def lanes(at, pair):
    first = at + 128 * pair
    return pl.ds(first if isinstance(pair, int) else pl.multiple_of(first, 128), 128)


def attend_fwd(causal, q_ref, q_at, k_ref, k_at, v_ref, v_at, fq, fk, ctx_ref, lse_ref, lse_s, tri_s):
    low = low_lanes(ROW)
    lane = lax.broadcasted_iota(jnp.int32, (ROW, 128), 1)
    one = jnp.asarray(1.0, BF)
    if causal is not None:
        tri_s[...] = triangle(ROW, False, causal)

    def body(pair):
        q_pair = q_ref[:, lanes(q_at, pair)] * jnp.asarray(HD**-0.5, BF)
        k_pair = k_ref[:, lanes(k_at, pair)]
        v_pair = v_ref[:, lanes(v_at, pair)]
        halves = []
        for e in range(2):
            sel = low if e == 0 else ~low
            s = dot_nt(jnp.where(sel, q_pair, fq), jnp.where(sel, k_pair, fk))
            if causal is not None:
                s = s + tri_s[...]
            top = jnp.max(s, axis=1, keepdims=True)
            p = jnp.exp(s - top)
            o = dot_nn(p.astype(BF), jnp.where(sel, v_pair, one))
            total = pltpu.roll(o, 64, 1)
            halves.append(o / total)
            lse = top + jnp.log(jnp.where(sel, total, o))
            lse_s[...] = jnp.where(lane == 2 * pair + e, lse, lse_s[...])
        ctx_ref[:, lanes(0, pair)] = jnp.where(low, halves[0], halves[1]).astype(BF)

    over_pairs(body)
    lse_ref[...] = lse_s[...].T[0:HEADS, :]


def attend_bwd(causal, q_ref, q_at, k_ref, k_at, v_ref, v_at, fq, fk, lse_ref, do_ref, outs, dqt_ref, kt_ref, tri_s):
    low = low_lanes(ROW)
    zero = jnp.zeros((ROW, 128), BF)
    scale = jnp.asarray(HD**-0.5, BF)
    kt_ref[...] = k_ref[:, k_at : k_at + D].T
    if causal is not None:
        tri_s[...] = triangle(ROW, True, causal)

    def body(pair):
        q_pair = q_ref[:, lanes(q_at, pair)] * scale
        k_pair = k_ref[:, lanes(k_at, pair)]
        v_pair = v_ref[:, lanes(v_at, pair)]
        do_pair = do_ref[:, lanes(0, pair)]
        dks, dvs = [], []
        for e in range(2):
            head = 2 * pair + e
            sel = low if e == 0 else ~low
            s = dot_nt(jnp.where(sel, k_pair, fk), jnp.where(sel, q_pair, fq))
            if causal is not None:
                s = s + tri_s[...]
            p = jnp.exp(s - lse_ref[pl.ds(head, 1), :])
            prod = p * dot_nt(jnp.where(sel, v_pair, zero), do_pair)
            ds = (prod - p * jnp.sum(prod, axis=0, keepdims=True)).astype(BF)
            dvs.append(dot_nn(p.astype(BF), do_pair))
            dks.append(dot_nn(ds, q_pair))
            rows = pl.ds(HD * head if isinstance(pair, int) else pl.multiple_of(HD * head, HD), HD)
            dqt_ref[rows, :] = dot_nn(kt_ref[rows, :], ds)
        for (ref, at), parts in ((outs[1], dks), (outs[2], dvs)):
            ref[:, lanes(at, pair)] = jnp.where(low, parts[0], parts[1]).astype(BF)

    over_pairs(body)
    ref, at = outs[0]
    ref[:, at : at + D] = (dqt_ref[...] * HD**-0.5).T.astype(BF)


def group_perm(name, to_flat):
    _, cols, _, group = MATS[name]
    width = cols // 128
    size = group * width
    row = lax.broadcasted_iota(jnp.int32, (size, size), 0)
    col = lax.broadcasted_iota(jnp.int32, (size, size), 1)
    blocked, flat = (col, row) if to_flat else (row, col)
    source = width * (blocked & (group - 1)) + lax.shift_right_logical(blocked, group.bit_length() - 1)
    return jnp.where(source == flat, 1.0, 0.0).astype(BF)


def to_matrix(name, flat_ref, at, mat_ref):
    rows, cols, _, group = MATS[name]
    width = cols // 128
    size = group * width
    perm = group_perm(name, False)

    def move(g, _):
        got = dot_nn(perm, flat_ref[at + g * size : at + (g + 1) * size, :]).astype(BF)
        for c in range(width):
            mat_ref[g * group : (g + 1) * group, 128 * c : 128 * c + 128] = got[c * group : (c + 1) * group]
        return 0

    for g in range(rows // group):
        move(g, 0)


def to_flat(name, mat_ref, flat_ref, at):
    rows, cols, _, group = MATS[name]
    width = cols // 128
    size = group * width
    perm = group_perm(name, True)

    def move(g, _):
        block = mat_ref[g * group : (g + 1) * group, :].astype(BF)
        blocked = jnp.concatenate([block[:, 128 * c : 128 * c + 128] for c in range(width)], axis=0)
        flat_ref[at + g * size : at + (g + 1) * size, :] = dot_nn(perm, blocked).astype(BF)
        return 0

    for g in range(rows // group):
        move(g, 0)


def ffn_fwd(hidden_ref, w_up, w_down, act_ref, slope_ref, total_s):
    for c in range(FF // CHUNK):
        cols = slice(c * CHUNK, (c + 1) * CHUNK)
        act, slope = gelu_both(dot_nn(hidden_ref[...], w_up[:, cols]))
        act_ref[:, cols] = act.astype(BF)
        slope_ref[:, cols] = slope.astype(slope_ref.dtype)
    total_s[...] = dot_nn(act_ref[...], w_down[...])


def ffn_bwd(branch_ref, w_up, w_down, slope_ref, dz_ref, total_s):
    for c in range(FF // CHUNK):
        cols = slice(c * CHUNK, (c + 1) * CHUNK)
        grad_act = dot_nt(branch_ref[...], w_down[cols, :])
        dz_ref[:, cols] = (grad_act * slope_ref[:, cols].astype(F32)).astype(BF)
    total_s[...] = dot_nt(dz_ref[...], w_up[...])


def self_head(grad_s, more_s, r1_ref, vec, w_out, dr1_ref, half_s, dctx_ref, gvec):
    def body(rows):
        dr1, gain, shift = ln_back(grad_s[rows, :] + more_s[rows, :], r1_ref[rows, :], vec[0:1, :])
        dr1_ref[rows, :] = dr1
        half_s[rows, :] = dr1.astype(BF)
        return gain, shift

    gvec[0:1, :], gvec[1:2, :] = by_rows(body)
    dctx_ref[...] = dot_nt(half_s[...], w_out[...]).astype(BF)


def copies(sources, targets, sems):
    made = [pltpu.make_async_copy(s, t, sems.at[i]) for i, (s, t) in enumerate(zip(sources, targets))]
    for one in made:
        one.start()
    return made


def piece_row(share, b):
    return 16 * (share * b // TILE)


def shift_kernel(share, shift_ref, params_ref, out_ref, rows_s):
    rows = out_ref.shape[0]
    full = share // 1024
    rows_s[0:16, :] = jnp.zeros((16, 128), F32)
    rows_s[16 + 8 * full :, :] = jnp.zeros((rows_s.shape[0] - 16 - 8 * full, 128), F32)

    def fill(k, _):
        at = pl.multiple_of(1024 * k, 1024)
        rows_s[pl.ds(pl.multiple_of(8 * k + 16, 8), 8), :] = params_ref[:, pl.ds(at, 1024)].reshape(8, 128)
        return 0

    lax.fori_loop(0, full, fill, 0, unroll=8)
    for r in range(-(-(share - 1024 * full) // 128)):
        at = 1024 * full + 128 * r
        width = min(128, share - at)
        rows_s[16 + 8 * full + r : 17 + 8 * full + r, 0:width] = params_ref[:, at : at + width]
    shift = shift_ref[0]
    down, right = shift // 128, lax.rem(shift, 128)
    lane = lax.broadcasted_iota(jnp.int32, (16, 128), 1)

    def move(k, _):
        same = rows_s[pl.ds(16 * k + 16 - down, 16), :]
        above = rows_s[pl.ds(16 * k + 15 - down, 16), :]
        got = jnp.where(lane >= right, pltpu.roll(same, right, 1), pltpu.roll(above, right, 1))
        out_ref[pl.ds(pl.multiple_of(16 * k, 16), 16), :] = got.astype(BF)
        return 0

    lax.fori_loop(0, rows // 16, move, 0, unroll=6)


def unshift_kernel(share, shift_ref, sums_ref, grad_ref, square_ref):
    shift = shift_ref[0]
    down, left = shift // 128, lax.rem(shift, 128)
    lane = lax.broadcasted_iota(jnp.int32, (8, 128), 1)
    full = share // 1024

    def block(at):
        same = sums_ref[pl.ds(at + down, 8), :]
        below = sums_ref[pl.ds(at + down + 1, 8), :]
        back = lax.rem(128 - left, 128)
        return jnp.where(lane < 128 - left, pltpu.roll(same, back, 1), pltpu.roll(below, back, 1))

    def move(k, total):
        got = block(8 * k)
        grad_ref[:, pl.ds(pl.multiple_of(1024 * k, 1024), 1024)] = got.reshape(1, 1024)
        return total + got * got

    total = lax.fori_loop(0, full, move, jnp.zeros((8, 128), F32), unroll=8)
    rest = share - 1024 * full
    if rest:
        got = block(8 * full)
        place = lax.broadcasted_iota(jnp.int32, (8, 128), 0) * 128 + lane
        got = jnp.where(place < rest, got, 0.0)
        total = total + got * got
        for r in range(-(-rest // 128)):
            width = min(128, rest - 128 * r)
            at = 1024 * full + 128 * r
            grad_ref[:, at : at + width] = got[r : r + 1, 0:width]
    square_ref[...] = total


def adam_kernel(share, clip_ref, grad_ref, first_ref, second_ref, step_ref, new_first_ref, new_second_ref):
    clip = clip_ref[0]
    rate = D ** (-0.5) * min(STEP ** (-0.5), STEP * WARMUP ** (-1.5))

    def update(at, width, fold):
        shape = (8, 128) if fold else (1, width)
        scaled = grad_ref[:, pl.ds(at, width)].reshape(shape) * clip
        first = BETA_ONE * first_ref[:, pl.ds(at, width)].reshape(shape) + (1.0 - BETA_ONE) * scaled
        second = BETA_TWO * second_ref[:, pl.ds(at, width)].reshape(shape) + (1.0 - BETA_TWO) * scaled * scaled
        first_hat = first / (1.0 - BETA_ONE**STEP)
        second_hat = second / (1.0 - BETA_TWO**STEP)
        step = rate * first_hat / (jnp.sqrt(second_hat) + ADAM_EPS)
        step_ref[:, pl.ds(at, width)] = step.reshape(1, width)
        new_first_ref[:, pl.ds(at, width)] = first.reshape(1, width)
        new_second_ref[:, pl.ds(at, width)] = second.reshape(1, width)

    def move(k, _):
        update(pl.multiple_of(1024 * k, 1024), 1024, True)
        return 0

    full = share // 1024
    lax.fori_loop(0, full, move, 0, unroll=4)
    for at in range(1024 * full, share, 128):
        update(at, min(128, share - at), False)


def weights_kernel(n, share, flat_in, *refs):
    outs, flat = refs[:6], refs[6]
    for b in range(n):
        tile = share * b // TILE
        last = -(-share * (b + 1) // TILE)
        start, count = 16 * tile, 16 * (last - tile)
        if (share * b) % TILE:
            flat[start : start + 16, :] += flat_in[b, 0:16, :]
        else:
            flat[start : start + 16, :] = flat_in[b, 0:16, :]
        flat[start + 16 : start + count, :] = flat_in[b, 16:count, :]
    for name, ref in zip(MATS, outs):
        to_matrix(name, flat, MATS[name][2], ref)
    outs[5][...] = flat[VEC_AT : VEC_AT + 32, :]


SLOTS = ((0, 1, 2, 3), (1, 0, 3, 2), (2, 2, 0, 1), (3, 3, 1, 0))


def place_pieces(share, z_of, y, x, halves, flat):
    half = halves[0].shape[0]
    for which in range(2):
        for dy in range(2):
            for dx in range(2):
                piece = halves[4 * which + 2 * dy + dx]
                b = 4 * z_of + 2 * lax.rem(y + dy, 2) + lax.rem(x + dx, 2)
                row = pl.multiple_of(16 * ((share * b) // TILE), 16)
                if which == 0:
                    flat[pl.ds(row, 16), :] += piece[0:16, :]
                    flat[pl.ds(row + 16, half - 16), :] = piece[16:half, :]
                else:
                    kept = 16 * (share // TILE) - half
                    flat[pl.ds(row + half, kept), :] = piece[0:kept, :]
                    flat[pl.ds(row + half + kept, half - kept), :] += piece[kept:half, :]


def clear_edges(share, pieces, flat):
    for b in pieces:
        row = 16 * (share * b // TILE)
        last = row + 16 * (share // TILE)
        flat[row : row + 16, :] = jnp.zeros((16, 128), BF)
        flat[last : last + 32, :] = jnp.zeros((32, 128), BF)


def slot_copies(refs, kept, sems):
    a, ax, ay, b, by, bx = refs
    order = (a, ax, ay.at[0], ay.at[1], b, bx.at[0], by, bx.at[1])
    return [pltpu.make_async_copy(ref, kept.at[i], sems.at[i]) for i, ref in enumerate(order)]


def place_kernel(share, place_ref, *refs):
    slots, outs, refs = [refs[6 * i : 6 * i + 6] for i in range(4)], refs[24:30], refs[30:]
    mats, (vec_s, kept, flat, sems, out_sems) = refs[:5], refs[5:]
    sent, emit = emitter(out_sems)
    y, x = place_ref[1], place_ref[2]
    made = [slot_copies(slot, kept.at[i], sems.at[i]) for i, slot in enumerate(slots)]
    for some in made:
        for one in some:
            one.start()
    clear_edges(share, range(16), flat)
    for i, some in enumerate(made):
        z_of = place_ref[3 + i]
        for one in some:
            one.wait()
        place_pieces(share, z_of, y, x, [kept.at[i, j] for j in range(8)], flat)
    for name, mat, out in zip(MATS, mats, outs):
        to_matrix(name, flat, MATS[name][2], mat)
        emit(mat, out)
    vec_s[...] = flat[VEC_AT : VEC_AT + 32, :]
    emit(vec_s, outs[5])
    for one in sent:
        one.wait()


def self_fwd_kernel(causal_ref, x_ref, wqkv, fq, fk, qkv_ref, ctx_ref, lse_ref, lse_s, tri_s):
    qkv_ref[...] = dot_nn(x_ref[...], wqkv[...]).astype(BF)
    attend_fwd(
        causal_ref[0], qkv_ref, 0, qkv_ref, D, qkv_ref, 2 * D, fq[...], fk[...], ctx_ref, lse_ref, lse_s, tri_s
    )


def emitter(sems):
    sent = []

    def emit(source, target):
        sent.append(pltpu.make_async_copy(source, target, sems.at[len(sent)]))
        sent[-1].start()

    return sent, emit


def enc_ffn_kernel(
    x_ref, ctx_ref, vec, w_out, w_up_any, w_down_any, w_cross_any,
    mem_ref, kv_ref, act_any, slope_any, r1_any, r2_any,
    hid_s, total_s, act_s, slope_s, r1_s, r2_s, w_up, w_down, w_cross, in_sems, out_sems,
):
    made = copies((w_up_any, w_down_any, w_cross_any), (w_up, w_down, w_cross), in_sems)
    sent, emit = emitter(out_sems)
    total_s[...] = dot_nn(ctx_ref[...], w_out[...])

    def first(rows):
        r1 = x_ref[rows, :].astype(F32) + total_s[rows, :]
        r1_s[rows, :] = r1
        y1 = ln_parts(r1)[0] * vec[0:1, :] + vec[1:2, :]
        r2_s[rows, :] = y1
        hid_s[rows, :] = y1.astype(BF)

    by_rows(first)
    emit(r1_s, r1_any)
    made[0].wait()
    made[1].wait()
    ffn_fwd(hid_s, w_up, w_down, act_s, slope_s, total_s)
    emit(act_s, act_any)
    emit(slope_s, slope_any)

    def second(rows):
        r2 = r2_s[rows, :] + total_s[rows, :]
        r2_s[rows, :] = r2
        mem = (ln_parts(r2)[0] * vec[2:3, :] + vec[3:4, :]).astype(BF)
        mem_ref[rows, :D] = mem
        mem_ref[rows, D:] = mem

    by_rows(second)
    emit(r2_s, r2_any)
    made[2].wait()
    kv_ref[...] = dot_nn(mem_ref[:, :D], w_cross[...]).astype(BF)
    for one in sent:
        one.wait()


def dec_kernel(
    row, x_ref, ctx1_ref, kv_ref, go_any, vec, w_cross, w_out, w_up_any, w_down_any, fq, fk,
    out_any, gkv_ref, dr1_ref, dctx1_ref, act_any, dz_any, hid_any, br_any, left_any, right_ref, gvec,
    cq_s, lse_s, wide_s, dctx_s, dcq_s, dqt_s, kt_s, slope_s, act_s, dz_s, hid_s, br_s, left_s, out_s,
    go_ref, w_up, w_down, keep_s, r1_s, r2_s, total_s, in_sems, out_sems,
):
    up_copy, down_copy, go_copy = copies(
        (w_up_any, w_down_any, go_any.at[pl.ds(row * ROW, ROW)]), (w_up, w_down, go_ref), in_sems
    )
    sent, emit = emitter(out_sems)
    total_s[...] = dot_nn(ctx1_ref[...], w_out[...])

    def first(rows):
        r1 = x_ref[rows, :].astype(F32) + total_s[rows, :]
        r1_s[rows, :] = r1
        y1 = ln_parts(r1)[0] * vec[0:1, :] + vec[1:2, :]
        keep_s[rows, :] = y1
        left_s[rows, :D] = y1.astype(BF)

    by_rows(first)
    cq_s[...] = dot_nn(left_s[:, :D], w_cross[:, :D]).astype(BF)
    ctx_s = left_s.at[:, D:]
    attend_fwd(None, cq_s, 0, kv_ref, 0, kv_ref, D, fq[...], fk[...], ctx_s, lse_s, wide_s, None)
    emit(left_s, left_any)
    total_s[...] = dot_nn(ctx_s[...], w_cross[:, D:])

    def second(rows):
        r2 = keep_s[rows, :] + total_s[rows, :]
        r2_s[rows, :] = r2
        y2 = ln_parts(r2)[0] * vec[2:3, :] + vec[3:4, :]
        keep_s[rows, :] = y2
        hid_s[rows, :] = y2.astype(BF)

    by_rows(second)
    emit(hid_s, hid_any)
    up_copy.wait()
    down_copy.wait()
    ffn_fwd(hid_s, w_up, w_down, act_s, slope_s, total_s)
    emit(act_s, act_any)
    go_copy.wait()

    def third(rows):
        r3 = keep_s[rows, :] + total_s[rows, :]
        out_s[rows, :] = (ln_parts(r3)[0] * vec[4:5, :] + vec[5:6, :]).astype(BF)
        dr3, gain, shift = ln_back(go_ref[rows, :].astype(F32), r3, vec[4:5, :])
        keep_s[rows, :] = dr3
        br_s[rows, :] = dr3.astype(BF)
        return gain, shift

    gvec[4:5, :], gvec[5:6, :] = by_rows(third)
    emit(out_s, out_any)
    emit(br_s, br_any)
    ffn_bwd(br_s, w_up, w_down, slope_s, dz_s, total_s)
    emit(dz_s, dz_any)

    def fourth(rows):
        dr2, gain, shift = ln_back(keep_s[rows, :] + total_s[rows, :], r2_s[rows, :], vec[2:3, :])
        keep_s[rows, :] = dr2
        right_ref[rows, D:] = dr2.astype(BF)
        return gain, shift

    gvec[2:3, :], gvec[3:4, :] = by_rows(fourth)
    dctx_s[...] = dot_nt(right_ref[:, D:], w_cross[:, D:]).astype(BF)
    attend_bwd(
        None, cq_s, 0, kv_ref, 0, kv_ref, D, fq[...], fk[...], lse_s, dctx_s,
        ((dcq_s, 0), (gkv_ref, 0), (gkv_ref, D)), dqt_s, kt_s, None,
    )
    right_ref[:, :D] = dcq_s[...]
    total_s[...] = dot_nt(dcq_s[...], w_cross[:, :D])
    self_head(keep_s, total_s, r1_s, vec, w_out, dr1_ref, dctx_s, dctx1_ref, gvec)
    for one in sent:
        one.wait()


def enc_back_kernel(
    gkv_ref, r1_any, r2_ref, slope_any, vec, w_cross, w_out_any, w_up_any, w_down_any,
    dr1_ref, dctx1_ref, dz_any, hid_any, br_any, gvec,
    keep_s, total_s, r1_ref, slope_s, w_out, w_up, w_down, dz_s, hid_s, br_s, half_s, in_sems, out_sems,
):
    made = copies(
        (r1_any, slope_any, w_down_any, w_up_any, w_out_any), (r1_ref, slope_s, w_down, w_up, w_out), in_sems
    )
    sent, emit = emitter(out_sems)
    total_s[...] = dot_nt(gkv_ref[...], w_cross[...])
    made[0].wait()

    def first(rows):
        dr2, gain, shift = ln_back(total_s[rows, :], r2_ref[rows, :], vec[2:3, :])
        keep_s[rows, :] = dr2
        br_s[rows, :] = dr2.astype(BF)
        hid_s[rows, :] = (ln_parts(r1_ref[rows, :])[0] * vec[0:1, :] + vec[1:2, :]).astype(BF)
        return gain, shift

    gvec[2:3, :], gvec[3:4, :] = by_rows(first)
    gvec[4:8, :] = jnp.zeros((4, D), F32)
    emit(br_s, br_any)
    emit(hid_s, hid_any)
    for one in made[1:4]:
        one.wait()
    ffn_bwd(br_s, w_up, w_down, slope_s, dz_s, total_s)
    emit(dz_s, dz_any)
    made[4].wait()
    self_head(keep_s, total_s, r1_ref, vec, w_out, dr1_ref, half_s, dctx1_ref, gvec)
    for one in sent:
        one.wait()


def row_fetcher(kinds, rows, dec_ref, refs):
    count = len(kinds) * rows
    buffers, sems = refs[-len(kinds) - 1 : -1], refs[-1]
    ins = refs[: -len(kinds) - 1]
    sources = [ins[i : i + count] for i in range(0, len(ins), count)]
    kept = dict(zip(kinds, buffers))

    def fetch(some, i):
        size = some[i].shape[0]
        target = kept[kinds[i // rows]].at[pl.ds((i % rows) * size, size)]
        return pltpu.make_async_copy(some[i], target, sems.at[i])

    def begin(some):
        for i in range(count):
            fetch(some, i).start()

    if len(sources) == 1:
        begin(sources[0])
    else:
        for which, some in enumerate(sources):
            pl.when(dec_ref[0] == which)(functools.partial(begin, some))

    def ready(*some):
        for kind in some:
            for r in range(rows):
                fetch(sources[0], kinds.index(kind) * rows + r).wait()

    return kept, ready


def fetched(kinds, sources):
    ins = [row[kind] for some in sources for kind in kinds for row in some]
    rows = len(sources[0])
    kept = []
    for kind in kinds:
        size, cols = sources[0][0][kind].shape
        kept.append(pltpu.VMEM((rows * size, cols), sources[0][0][kind].dtype))
    return ins, kept + [pltpu.SemaphoreType.DMA((len(kinds) * rows,))]


FFN_KINDS = ("hid", "dz", "act", "branch")
ATTEND_KINDS = ("ctx", "dr1", "left", "right")


def ffn_grads_kernel(rows, dec_ref, *refs):
    count = 2 * len(FFN_KINDS) * rows
    ins, flat, (hid_t, g_up, g_down), rest = refs[:count], refs[count], refs[count + 1 : count + 4], refs[count + 4 :]
    kept, ready = row_fetcher(FFN_KINDS, rows, dec_ref, (*ins, *rest))
    ready("hid", "dz")
    hid_t[...] = kept["hid"][...].T
    for c in range(FF // CHUNK):
        cols = slice(c * CHUNK, (c + 1) * CHUNK)
        g_up[:, cols] = dot_nn(hid_t[...], kept["dz"][:, cols])
    to_flat("up", g_up, flat, 0)
    ready("act", "branch")
    for c in range(FF // D):
        part = slice(c * D, (c + 1) * D)
        g_down[part, :] = dot_tn(kept["act"][:, part], kept["branch"][...])
    to_flat("down", g_down, flat, MATS["down"][2] - MATS["up"][2])


def attend_grads_kernel(rows, dec_ref, *refs):
    count = 2 * len(ATTEND_KINDS) * rows
    ins, flat, (g_cross, g_out), rest = refs[:count], refs[count], refs[count + 1 : count + 3], refs[count + 3 :]
    kept, ready = row_fetcher(ATTEND_KINDS, rows, dec_ref, (*ins, *rest))
    ready("ctx", "dr1")
    g_out[...] = dot_tn(kept["ctx"][...], kept["dr1"][...].astype(BF))
    to_flat("out", g_out, flat, 0)
    ready("left", "right")
    for at in (0, D):
        g_cross[:, at : at + D] = dot_tn(kept["left"][:, at : at + D], kept["right"][:, at : at + D])
    to_flat("cross", g_cross, flat, MATS["cross"][2] - REST_AT)


BACK_KINDS = ("qkv", "lse", "dctx", "dr1")


def self_back_kernel(ins, causal_ref, wqkv, fq, fk, *refs):
    (dx_ref, dqkv, dqt_s, kt_s, tri_s), rest = refs[ins : ins + 5], refs[ins + 5 :]
    kept, ready = row_fetcher(BACK_KINDS, 1, causal_ref, (*refs[:ins], *rest))
    ready("qkv", "lse", "dctx")
    qkv = kept["qkv"]
    attend_bwd(
        causal_ref[0], qkv, 0, qkv, D, qkv, 2 * D, fq[...], fk[...], kept["lse"], kept["dctx"],
        ((dqkv, 0), (dqkv, D), (dqkv, 2 * D)), dqt_s, kt_s, tri_s,
    )
    ready("dr1")
    dx_ref[...] = (kept["dr1"][...] + dot_nt(dqkv[...], wqkv[...])).astype(BF)


def qkv_kernel(ins, rows, dec_ref, x_ref, *refs):
    (fl_qkv, x_t, g_qkv), rest = refs[ins : ins + 3], refs[ins + 3 :]
    kept, ready = row_fetcher(("dqkv",), rows, dec_ref, (*refs[:ins], *rest))
    x_t[...] = x_ref[...].T
    ready("dqkv")
    for c in range(3):
        cols = slice(c * D, (c + 1) * D)
        g_qkv[:, cols] = dot_nn(x_t[...], kept["dqkv"][:, cols])
    to_flat("qkv", g_qkv, fl_qkv, 0)


def pack_kernel(share, planes, base, place_ref, *refs):
    parts, outs, flat = refs[:-5], refs[-5:-1], refs[-1]
    send_a, keep_a, send_b, keep_b = outs
    at = 0
    for part in parts:
        flat[at : at + part.shape[0], :] = part[...]
        at += part.shape[0]
    y, x = place_ref[0], place_ref[1]
    half = send_a.shape[2]
    for i, z in enumerate(planes):
        for j in range(2):
            for ref, y_to, x_to, skip in (
                (send_a, 1 - y, j, 0), (keep_a, y, j, 0), (send_b, j, 1 - x, half), (keep_b, j, x, half),
            ):
                b = 4 * z + 2 * y_to + x_to
                start = pl.multiple_of(16 * ((share * b) // TILE) - base + skip, 16)
                ref[i, j] = flat[pl.ds(start, half), :]


def kernel_call(body, micros=1, **options):
    cost = pl.CostEstimate(flops=micros * 10**9, bytes_accessed=0, transcendentals=0)
    call = pl.pallas_call(body, cost_estimate=cost, **options)
    return lambda *operands: tuple(call(*operands))


IN_VMEM = pl.BlockSpec(memory_space=pltpu.VMEM)
IN_SMEM = pl.BlockSpec(memory_space=pltpu.SMEM)
ANYWHERE = pl.BlockSpec(memory_space=pl.ANY)


def at_row(row, cols, rows=ROW):
    return pl.BlockSpec((rows, cols), lambda i: (row, 0), pipeline_mode=pl.Buffered(1))


def shifted(shift, params, share, rows):
    return kernel_call(
        functools.partial(shift_kernel, share),
        in_specs=[IN_SMEM, IN_VMEM],
        out_specs=[IN_VMEM],
        out_shape=[shape_of((rows, 128), BF)],
        scratch_shapes=[pltpu.VMEM((rows + 32, 128), F32)],
        compiler_params=params_of(8),
    )(shift, params)[0]


def unshifted(shift, sums, share):
    return kernel_call(
        functools.partial(unshift_kernel, share),
        in_specs=[IN_SMEM, IN_VMEM],
        out_specs=[IN_VMEM] * 2,
        out_shape=[shape_of((1, share), F32), shape_of((8, 128), F32)],
        compiler_params=params_of(8),
    )(shift, sums)


def adam(clip, grad, first, second, share):
    return kernel_call(
        functools.partial(adam_kernel, share),
        in_specs=[IN_SMEM] + [IN_VMEM] * 3,
        out_specs=[IN_VMEM] * 3,
        out_shape=[shape_of((1, share), F32)] * 3,
        compiler_params=params_of(16),
    )(clip, grad, first, second)


def split_weights(pieces, n, share):
    shapes = [(rows, cols) for rows, cols, _, _ in MATS.values()] + [(32, 128)]
    rows = 16 * (-(-share * n // TILE) + 2)
    got = kernel_call(
        functools.partial(weights_kernel, n, share),
        in_specs=[IN_VMEM],
        out_specs=[IN_VMEM] * 6,
        out_shape=[shape_of(s, BF) for s in shapes],
        scratch_shapes=[pltpu.VMEM((rows, 128), BF)],
        compiler_params=params_of(60),
    )(pieces)
    return dict(zip((*MATS, "vec"), got))


def placed_weights(place, slots, share, rows):
    vm = pltpu.VMEM
    shapes = [(rows, cols) for rows, cols, _, _ in MATS.values()] + [(32, 128)]
    got = kernel_call(
        functools.partial(place_kernel, share),
        micros=9,
        in_specs=[IN_SMEM] + [ANYWHERE] * 24,
        out_specs=[ANYWHERE] * 6,
        out_shape=[shape_of(s, BF) for s in shapes],
        scratch_shapes=[vm(s, BF) for s in shapes]
        + [vm((4, 8, rows // 2, 128), BF), vm((piece_row(share, 15) + rows + 16, 128), BF)]
        + [pltpu.SemaphoreType.DMA((4, 8)), pltpu.SemaphoreType.DMA((6,))],
        compiler_params=params_of(60),
    )(place, *(one for slot in slots for one in slot))
    return dict(zip((*MATS, "vec"), got))


def row_shapes(*cols):
    return [shape_of((ROW, abs(c)), F32 if c < 0 else BF) for c in cols]


def self_fwd(causal, row, x, w_qkv, fq, fk):
    names = ("qkv", "ctx", "lse")
    vm = pltpu.VMEM
    got = kernel_call(
        self_fwd_kernel,
        micros=5,
        grid=(1,),
        in_specs=[IN_SMEM, at_row(row, D), whole_spec((D, 3 * D)), at_row(row, 128), at_row(row, 128)],
        out_specs=[at_row(0, 3 * D), at_row(0, D), at_row(0, ROW, HEADS)],
        out_shape=row_shapes(3 * D, D) + [shape_of((HEADS, ROW), F32)],
        scratch_shapes=[vm((ROW, 128), F32), vm((ROW, ROW), F32)],
        compiler_params=params_of(24),
    )(causal, x, w_qkv, fq, fk)
    return dict(zip(names, got))


def enc_ffn(row, x, fwd, w, vec):
    names = ("mem", "kv", "act", "slope", "r1", "r2")
    vm = pltpu.VMEM
    got = kernel_call(
        enc_ffn_kernel,
        micros=8,
        grid=(1,),
        in_specs=[at_row(row, D), at_row(0, D), whole_spec((6, D)), whole_spec((D, D))] + [ANYWHERE] * 3,
        out_specs=[at_row(0, 2 * D), at_row(0, 2 * D)] + [ANYWHERE] * 4,
        out_shape=row_shapes(2 * D, 2 * D, FF, FF, -D, -D),
        scratch_shapes=[
            vm((ROW, D), BF), vm((ROW, D), F32), vm((ROW, FF), BF), vm((ROW, FF), BF), vm((ROW, D), F32), vm((ROW, D), F32),
            vm((D, FF), BF), vm((FF, D), BF), vm((D, 2 * D), BF), pltpu.SemaphoreType.DMA((3,)), pltpu.SemaphoreType.DMA((4,)),
        ],
        compiler_params=params_of(32),
    )(x, fwd["ctx"], vec, w["out"], w["up"], w["down"], w["cross"])
    return dict(zip(names, got))


def dec_call(row, x, fwd, kv, go, w, vec, fq, fk):
    vm = pltpu.VMEM
    names = ("out", "gkv", "dr1", "dctx", "act", "dz", "hid", "branch", "left", "right", "gvec")
    got = kernel_call(
        functools.partial(dec_kernel, row),
        micros=23,
        grid=(1,),
        in_specs=[
            at_row(row, D), at_row(0, D), at_row(0, 2 * D), ANYWHERE, whole_spec((6, D)), whole_spec((D, 2 * D)),
            whole_spec((D, D)), ANYWHERE, ANYWHERE, at_row(row, 128), at_row(row, 128),
        ],
        out_specs=[ANYWHERE, at_row(0, 2 * D), at_row(0, D), at_row(0, D)] + [ANYWHERE] * 5
        + [at_row(0, 2 * D), whole_spec((8, D))],
        out_shape=row_shapes(D, 2 * D, -D, D, FF, FF, D, D, 2 * D, 2 * D) + [shape_of((8, D), F32)],
        scratch_shapes=[
            vm((ROW, D), BF), vm((HEADS, ROW), F32), vm((ROW, 128), F32), vm((ROW, D), BF), vm((ROW, D), BF),
            vm((D, ROW), F32), vm((D, ROW), BF), vm((ROW, FF), BF), vm((ROW, FF), BF), vm((ROW, FF), BF), vm((ROW, D), BF),
            vm((ROW, D), BF), vm((ROW, 2 * D), BF), vm((ROW, D), BF), vm((ROW, D), BF), vm((D, FF), BF),
            vm((FF, D), BF), vm((ROW, D), F32), vm((ROW, D), F32), vm((ROW, D), F32), vm((ROW, D), F32),
            pltpu.SemaphoreType.DMA((3,)), pltpu.SemaphoreType.DMA((6,)),
        ],
        compiler_params=params_of(60),
    )(x, fwd["ctx"], kv, go, vec, w["cross"], w["out"], w["up"], w["down"], fq, fk)
    return dict(zip(names, got))


def enc_back(gkv, fwd, w, vec):
    names = ("dr1", "dctx", "dz", "hid", "branch", "gvec")
    vm = pltpu.VMEM
    got = kernel_call(
        enc_back_kernel,
        micros=8,
        grid=(1,),
        in_specs=[
            at_row(0, 2 * D), ANYWHERE, at_row(0, D), ANYWHERE, whole_spec((6, D)), whole_spec((D, 2 * D)),
            ANYWHERE, ANYWHERE, ANYWHERE,
        ],
        out_specs=[at_row(0, D), at_row(0, D)] + [ANYWHERE] * 3 + [whole_spec((8, D))],
        out_shape=row_shapes(-D, D, FF, D, D) + [shape_of((8, D), F32)],
        scratch_shapes=[
            vm((ROW, D), F32), vm((ROW, D), F32), vm((ROW, D), F32), vm((ROW, FF), BF), vm((D, D), BF), vm((D, FF), BF),
            vm((FF, D), BF), vm((ROW, FF), BF), vm((ROW, D), BF), vm((ROW, D), BF), vm((ROW, D), BF), pltpu.SemaphoreType.DMA((5,)),
            pltpu.SemaphoreType.DMA((3,)),
        ],
        compiler_params=params_of(32),
    )(gkv, fwd["r1"], fwd["r2"], fwd["slope"], vec, w["cross"], w["out"], w["up"], w["down"])
    return dict(zip(names, got))


def row_grads(body, kinds, flat_rows, scratch, is_dec, sources):
    ins, kept = fetched(kinds, sources)
    return kernel_call(
        functools.partial(body, len(sources[0])),
        micros=1,
        in_specs=[IN_SMEM] + [ANYWHERE] * len(ins),
        out_specs=[IN_VMEM],
        out_shape=[shape_of((flat_rows, 128), BF)],
        scratch_shapes=scratch + kept,
        compiler_params=params_of(48),
    )(is_dec, *ins)[0]


def self_back(causal, row, sources, w, fq, fk):
    vm = pltpu.VMEM
    shapes = row_shapes(D, 3 * D)
    ins, kept = fetched(BACK_KINDS, [[one] for one in sources])
    got = kernel_call(
        functools.partial(self_back_kernel, len(ins)),
        micros=1,
        grid=(1,),
        in_specs=[IN_SMEM, whole_spec((D, 3 * D)), at_row(row, 128), at_row(row, 128)] + [ANYWHERE] * len(ins),
        out_specs=[whole_spec(s.shape) for s in shapes],
        out_shape=shapes,
        scratch_shapes=[vm((D, ROW), F32), vm((D, ROW), BF), vm((ROW, ROW), F32)] + kept,
        compiler_params=params_of(28),
    )(causal, w["qkv"], fq, fk, *ins)
    return dict(zip(("dx", "dqkv"), got))


def qkv_grad(is_dec, x, sources):
    vm = pltpu.VMEM
    t, rows = x.shape[0], len(sources[0])
    ins, kept = fetched(("dqkv",), sources)
    return kernel_call(
        functools.partial(qkv_kernel, len(ins), rows),
        micros=1,
        in_specs=[IN_SMEM, IN_VMEM] + [ANYWHERE] * len(ins),
        out_specs=[IN_VMEM],
        out_shape=[shape_of((REST_AT, 128), BF)],
        scratch_shapes=[vm((D, t), BF), vm((D, 3 * D), F32)] + kept,
        compiler_params=params_of(28),
    )(is_dec, x, *ins)[0]


def pack(place, parts, planes, base, share, rows):
    half = rows // 2
    parts = [p if isinstance(p, tuple) else (p, p.shape[0]) for p in parts]
    total = sum(count for _, count in parts)
    need = piece_row(share, 4 * planes[-1] + 3) - base + rows
    return kernel_call(
        functools.partial(pack_kernel, share, planes, base),
        micros=1,
        grid=(1,),
        in_specs=[IN_SMEM] + [pl.BlockSpec((count, 128), lambda i: (0, 0), pipeline_mode=pl.Buffered(1)) for _, count in parts],
        out_specs=[whole_spec((len(planes), 2, half, 128))] * 4,
        out_shape=[shape_of((len(planes), 2, half, 128), BF)] * 4,
        scratch_shapes=[pltpu.VMEM((max(total, need), 128), BF)],
        compiler_params=params_of(32),
    )(place, *(p for p, _ in parts))


def mask_features(segments, live):
    t = segments.shape[0]
    lane = (jnp.arange(128, dtype=jnp.int32) % HD)[None, :]
    pair = lane // 2
    odd = lane % 2 == 1
    is_seg = pair < SEG_BITS
    is_pos = (pair >= SEG_BITS) & (pair < SEG_BITS + POS_BITS)
    place = (jnp.arange(t, dtype=jnp.int32) % ROW)[:, None]
    bit = jnp.where(
        is_seg,
        (segments[:, None] >> jnp.minimum(pair, SEG_BITS)) & 1,
        (place >> jnp.clip(pair - SEG_BITS, 0, POS_BITS)) & 1,
    )
    query = jnp.where(odd, 1 - bit, bit) * (is_seg | is_pos)
    key = jnp.where(odd, bit, 1 - bit)
    keys = [jnp.where(is_seg | (is_pos & (live[i][:, None] != 1)), key.astype(F32) * -BIG, 0.0).astype(BF) for i in range(2)]
    return query.astype(BF), keys[0], keys[1]


def ghosts(shapes):
    if not shapes:
        return ()
    return kernel_call(lambda *refs: None, out_specs=[ANYWHERE] * len(shapes), out_shape=list(shapes))()


def either(is_decoder, dec, enc, dec_first=False):
    thunks = (enc, dec)
    made = [jax.eval_shape(t) for t in thunks]
    slots, where = [], []
    for tree in made:
        free = list(range(len(slots)))
        taken = []
        for leaf in jax.tree.leaves(tree):
            key = (leaf.shape, leaf.dtype)
            match = next((i for i in free if slots[i] == key), None)
            if match is None:
                slots.append(key)
                match = len(slots) - 1
            else:
                free.remove(match)
            taken.append(match)
        where.append(taken)

    def branch(which):
        def run():
            leaves = jax.tree.leaves(thunks[which]())
            filled = dict(zip(where[which], leaves))
            missing = [i for i in range(len(slots)) if i not in filled]
            filled.update(zip(missing, ghosts([shape_of(*slots[i]) for i in missing])))
            return tuple(filled[i] for i in range(len(slots)))

        return run

    if dec_first:
        got = lax.cond(jnp.logical_not(is_decoder), branch(0), branch(1))
    else:
        got = lax.cond(is_decoder, branch(1), branch(0))
    back = [jax.tree.unflatten(jax.tree.structure(made[i]), [got[s] for s in where[i]]) for i in range(2)]
    return back[1], back[0]


def plane_permute(value, step):
    return lax.ppermute(value, "batch", [(i, i ^ step) for i in range(16)])


def line_permute(value, step, sources):
    pairs = [(4 * z + k, 4 * (z + step) + k) for z in sources for k in range(4)]
    return lax.ppermute(value, "batch", pairs)


def over_all(value):
    axes = ("section", "batch")
    places = [(core, i) for core in range(2) for i in range(16)]

    def flat(core, i):
        return core * 16 + i

    total = value
    for core_step in range(2):
        for step in range(4):
            if core_step or step:
                pairs = [(flat(c, i), flat(c ^ core_step, i ^ step)) for c, i in places]
                total = total + lax.ppermute(value, axes, pairs)
    value = total
    for step in (4, 8, 12):
        total = total + plane_permute(value, step)
    return total


def tied(*values):
    return lax.optimization_barrier(values)


def gathered(own, z):
    half = own.shape[0] // 2

    def first(block):
        a, b = block[:half], block[half:]
        return a, b, plane_permute(a, 1), plane_permute(b, 2)

    def second(parts):
        a, b, ax, by = parts
        return (a, ax, plane_permute(jnp.stack([a, ax]), 2), b, by, plane_permute(jnp.stack([b, by]), 1))

    up, down = line_permute(own, 1, (0, 1, 2)), line_permute(own, -1, (1, 2, 3))
    begun = first(own)
    zero = second(begun)
    up, down, _ = tied(up, down, begun)
    up_two, down_two = line_permute(up, 1, (1, 2)), line_permute(down, -1, (1, 2))
    begun = first(jnp.where((z == 0) | (z == 2), down, up))
    zero, begun = tied(zero, begun)
    one = second(begun)
    up_two, down_two, _ = tied(up_two, down_two, zero)
    ends = both_ends(jnp.where(z == 2, up_two, down_two), ((2, 3), (1, 0)))
    begun = first(jnp.where(z == 0, down_two, jnp.where(z == 1, down, up_two)))
    one, begun = tied(one, begun)
    two = second(begun)
    ends, _ = tied(ends, one)
    begun = first(jnp.where((z == 0) | (z == 3), ends, jnp.where(z == 1, down_two, up)))
    two, begun = tied(two, begun)
    three = second(begun)
    return zero, one, two, three


def both_ends(value, steps):
    return lax.ppermute(value, "batch", [(4 * a + k, 4 * b + k) for a, b in steps for k in range(4)])


def added(*values):
    total = values[0].astype(F32)
    for value in values[1:]:
        total = total + value.astype(F32)
    return total


def plane_start(packed):
    send_a, keep_a, send_b, keep_b = packed
    return keep_a, plane_permute(send_a, 2), keep_b, plane_permute(send_b, 1)


def plane_end(begun, y, x):
    keep_a, got_a, keep_b, got_b = begun

    def part(keep, got, index):
        return added(lax.dynamic_index_in_dim(keep, index, 1, False), lax.dynamic_index_in_dim(got, index, 1, False))

    far_a, far_b = part(keep_a, got_a, 1 - x).astype(BF), part(keep_b, got_b, 1 - y).astype(BF)
    in_a, in_b = plane_permute(far_a, 1), plane_permute(far_b, 2)
    sum_a, sum_b = added(part(keep_a, got_a, x), in_a), added(part(keep_b, got_b, y), in_b)
    return jnp.stack([sum_a.astype(BF), sum_b.astype(BF)], axis=1)


def line_sums(early, mid, late, z):
    one, two, three = mid[0], early[0], early[1]

    def low(value):
        return value.astype(BF)

    up = line_permute(three, 1, (0,))
    down = line_permute(one, -1, (3,))
    up = line_permute(low(jnp.where(z == 0, two.astype(F32), added(three, up))), 1, (0, 1))
    down = line_permute(low(jnp.where(z == 3, two.astype(F32), added(one, down))), -1, (2, 3))
    third = jnp.where(z == 0, one.astype(F32), added(jnp.where(z == 1, two, three), up))
    up = line_permute(low(third), 1, (0, 1, 2))
    zero = late[0]
    near = line_permute(zero, -1, (1, 3))
    pair = added(zero, near)
    far = line_permute(low(pair), -2, (2,))
    own = jnp.where(z == 1, one, jnp.where(z == 2, two, three))
    return jnp.where(z == 0, added(pair, far), added(own, up, down))


def shards(params, first_moment, second_moment, inputs, segments, live_mask, out_grad):
    is_decoder = lax.axis_index("section") == 1
    me = lax.axis_index("batch")
    n = lax.axis_size("batch")
    share = params.shape[1]
    rows = 16 * (share // TILE + 2)
    shift = lax.rem(me * (share % TILE), TILE)[None]
    x = inputs[0]
    t = x.shape[0]
    count = t // ROW

    y, x_at, z = lax.rem(me // 2, 2), lax.rem(me, 2), me // 4
    custom = n == 16
    flag = is_decoder.astype(jnp.int32)[None]
    own = shifted(shift, params, share, rows)
    fq, fk_src, fk_tgt = mask_features(segments, live_mask)
    fk_self = jnp.where(is_decoder, fk_tgt, fk_src)
    if custom:
        spot = jnp.concatenate([jnp.stack([z, y, x_at]), jnp.asarray(SLOTS, jnp.int32)[:, z]])
        slots, fq, fk_src, fk_self = tied(gathered(own, z), fq, fk_src, fk_self)
        w = placed_weights(spot, slots, share, rows)
    else:
        pieces = lax.all_gather(own, "batch", axis=0, tiled=False)
        pieces, fq, fk_src, fk_self = tied(pieces, fq, fk_src, fk_self)
        w = split_weights(pieces, n, share)
    def forward(row):
        return self_fwd(flag, row, x, w["qkv"], fq, fk_self)

    first_fwd = forward(0)
    vec = w["vec"][:24].astype(F32).reshape(6, D)

    def nothing():
        return {}

    def swapped(value):
        return lax.ppermute(value, "section", [(0, 1), (1, 0)])

    fwd = [first_fwd]
    first = enc_ffn(0, x, first_fwd, w, vec)
    kept, dec_rows, enc_rows, back, enc_self = [first], [], [], [], []
    kv_in = swapped(first["kv"])
    if count > 1:
        fwd.append(forward(1))
        kv_in, fwd[1] = tied(kv_in, fwd[1])
    for row in range(count):

        def dec_make():
            got = dec_call(row, x, fwd[row], kv_in, out_grad, w, vec, fq, fk_src)
            return got.pop("gkv"), got

        def enc_make():
            ahead = [enc_ffn(row + 1, x, fwd[row + 1], w, vec)] if row + 1 < count else []
            done = [enc_back(back[row - 1], kept[row - 1], w, vec)] if row else []
            far = []
            if row and row == count - 1:
                far = [self_back(flag, 0, [{**(enc_rows or done)[0], **fwd[0]}], w, fq, fk_self)]
            return [k.pop("kv") for k in ahead], (ahead, done, far)

        (sent, got), (_, (ahead, done, far)) = either(is_decoder, dec_make, enc_make, DEC_FIRST)
        dec_rows.append(got)
        enc_rows += done
        kept += ahead
        enc_self += far
        kv_in = swapped(sent)
        if row + 2 < count:
            fwd.append(forward(row + 2))
            kv_in, fwd[-1] = tied(kv_in, fwd[-1])
        back.append(kv_in)
    dec_fwd = enc_fwd = fwd

    last = count - 1
    dec_self, done = either(
        is_decoder,
        lambda: [self_back(flag, 0, [{**dec_rows[0], **dec_fwd[0]}], w, fq, fk_self)] if last else [],
        lambda: enc_back(back[last], kept[last], w, vec),
    )
    enc_rows.append(done)
    dec_all = [{**made, **fwd} for made, fwd in zip(dec_rows, dec_fwd)]
    enc_all = [
        {**made, **fwd, "act": k["act"], "left": k["mem"], "right": g}
        for made, fwd, k, g in zip(enc_rows, enc_fwd, kept, back)
    ]
    both = [enc_all, dec_all]

    gvec = jnp.where(is_decoder, sum(r["gvec"] for r in dec_rows), sum(r["gvec"] for r in enc_rows))
    fl_vec = jnp.pad(gvec[:6].reshape(24, 128).astype(BF), ((0, 24), (0, 0)))

    vm = pltpu.VMEM
    flat_ffn = row_grads(
        ffn_grads_kernel, FFN_KINDS, VEC_AT - MATS["up"][2],
        [vm((D, t), BF), vm((D, FF), F32), vm((FF, D), F32)], flag, both,
    )
    place = jnp.stack([y, x_at])
    if custom:
        packed = pack(place, [flat_ffn, fl_vec], (2, 3), MATS["up"][2], share, rows)
        early = plane_start(packed)
        flag, _ = tied(flag, packed[0])
    flat_attend = row_grads(
        attend_grads_kernel, ATTEND_KINDS, MATS["up"][2] - REST_AT,
        [vm((D, 2 * D), F32), vm((D, D), F32)], flag, both,
    )
    if custom:
        need = piece_row(share, 7) + rows - MATS["up"][2]
        packed = pack(place, [flat_attend, (flat_ffn, need)], (1,), REST_AT, share, rows)
        mid = plane_start(packed)
        flag, _ = tied(flag, packed[0])

    common = []
    for row in range(len(dec_self), count):
        common.append(self_back(flag, row, [enc_all[row], dec_all[row]], w, fq, fk_self))
    if custom:
        early, common[-1] = tied(early, common[-1])
        early = plane_end(early, y, x_at)
    fl_qkv = qkv_grad(flag, x, [[*enc_self, *common], [*dec_self, *common]])
    dx = jnp.concatenate(
        [jnp.where(is_decoder, d["dx"], e["dx"]) for d, e in zip(dec_self, enc_self)] + [r["dx"] for r in common], axis=0
    )
    layer_out = jnp.where(
        is_decoder,
        jnp.concatenate([r["out"] for r in dec_rows], axis=0),
        jnp.concatenate([k["mem"][:, :D] for k in kept], axis=0),
    )

    if custom:
        mid, fl_qkv = tied(mid, fl_qkv)
        mid = plane_end(mid, y, x_at)
        need = piece_row(share, 3) + rows
        late = plane_start(pack(place, [fl_qkv, (flat_attend, need - REST_AT)], (0,), 0, share, rows))
        late = plane_end(late, y, x_at)
        mine = line_sums(early, mid, late, z).reshape(rows, 128)
    else:
        spare = jnp.zeros((piece_row(share, n - 1) + rows - FLAT_ROWS, 128), BF)
        flat = jnp.concatenate([fl_qkv, flat_attend, flat_ffn, fl_vec[:24], spare], axis=0)
        stacked = jnp.concatenate([flat[piece_row(share, b) :][:rows] for b in range(n)], axis=0)
        mine = lax.psum_scatter(stacked, "batch", scatter_dimension=0, tiled=True).astype(F32)
    grad_share, squares = unshifted(shift, jnp.pad(mine, ((0, 8), (0, 0))), share)

    if custom:
        square_sum = jnp.sum(over_all(squares))
    else:
        square_sum = lax.psum(jnp.sum(squares), ("section", "batch"))
    grad_norm = jnp.sqrt(square_sum)
    clip_factor = MAXNORM / jnp.maximum(grad_norm, MAXNORM)
    param_step, new_first, new_second = adam(clip_factor[None], grad_share, first_moment, second_moment, share)
    return (param_step, new_first, new_second, grad_share, layer_out[None], dx[None], grad_norm)


def solution(mesh):
    in_specs = (
        P("section", "batch"),
        P("section", "batch"),
        P("section", "batch"),
        P("section", "batch", None),
        P("batch"),
        P(None, "batch"),
        P("batch", None),
    )
    out_specs = (
        P("section", "batch"),
        P("section", "batch"),
        P("section", "batch"),
        P("section", "batch"),
        P("section", "batch", None),
        P("section", "batch", None),
        P(),
    )
    return jax.shard_map(shards, mesh=mesh, in_specs=in_specs, out_specs=out_specs, check_vma=False)
```
